32 devices in a mesh: seq: 4 (over z), rows: 8 (over y, x, core).
Axes of the slice: x: 2, y: 2, z: 4, core: 2. Of those that a mesh axis runs over, the one named last changes fastest.
Arguments:
- tokens: bfloat16 [16, 1024, 768], P('rows', 'seq'), may hold values from -6 to 6
- segments: int32 [16, 1024], P('rows', 'seq'), may hold values from -1 to 5, as said below
- ln1_gain: float32 [768], replicated, may hold values from 0.5 to 1.5
- ln1_bias: float32 [768], replicated, may hold values from -3 to 3
- w_qkv: bfloat16 [768, 2304], replicated, may hold values from -0.21875 to 0.21875
- q_bias: float32 [768], replicated, may hold values from -3 to 3
- v_bias: float32 [768], replicated, may hold values from -3 to 3
- w_out: bfloat16 [768, 768], replicated, may hold values from -1.75 to 1.75
- out_bias: float32 [768], replicated, may hold values from -3 to 3
- ln2_gain: float32 [768], replicated, may hold values from 0.5 to 1.5
- ln2_bias: float32 [768], replicated, may hold values from -3 to 3
- w_up: bfloat16 [768, 3072], replicated, may hold values from -0.21875 to 0.21875
- up_bias: float32 [3072], replicated, may hold values from -3 to 3
- w_down: bfloat16 [3072, 768], replicated, may hold values from -0.109375 to 0.109375
- down_bias: float32 [768], replicated, may hold values from -3 to 3
- cotangent: bfloat16 [16, 1024, 768], P('rows', 'seq'), may hold values from -6 to 6
Outputs:
- output: bfloat16 [16, 1024, 768], P('rows', 'seq')
- grad_tokens: bfloat16 [16, 1024, 768], P('rows', 'seq')
- grad_ln1_gain: float32 [768], replicated
- grad_ln1_bias: float32 [768], replicated
- grad_w_qkv: float32 [768, 2304], P('rows', 'seq')
- grad_q_bias: float32 [768], replicated
- grad_v_bias: float32 [768], replicated
- grad_w_out: float32 [768, 768], P('rows', 'seq')
- grad_out_bias: float32 [768], replicated
- grad_ln2_gain: float32 [768], replicated
- grad_ln2_bias: float32 [768], replicated
- grad_w_up: float32 [768, 3072], P('rows', 'seq')
- grad_up_bias: float32 [3072], replicated
- grad_w_down: float32 [3072, 768], P('seq', 'rows')
- grad_down_bias: float32 [768], replicated
The draws below stay inside these ranges and needn't reach their ends.
Inputs may be any that keep to these rules, and one draw needn't show every extreme that they name: `segments`: every clip is 157 slots long; clips are numbered from 0 in order from a row's first slot, a row holds five or six of them, and the rest of the row is padding (-1).
All inputs are finite; a program needn't handle non-finite values.
Results may differ from the reference program's by a relative error of at most 0.012.
Values may be sent and summed in bfloat16 or wider, within the bound.
No kernel may reach another device: no remote copies, remote signals or barrier semaphores. Data moves between devices by JAX's collectives and lax.ppermute only.
A program may use at most 192 MiB of HBM per device.

```python
import jax
import jax.numpy as jnp
from jax import lax

D = 768
HEADS = 12
HEAD_DIM = 64
FF = 3072
CLIP = 157
LENGTH = 1024
ROWS = 16


def draw_segments(key, part):
    key = jax.random.fold_in(key, 11)
    count_key, pick_key = jax.random.split(key)
    counts = jax.random.randint(count_key, (ROWS, 1), 5, 7)
    chosen = jax.random.randint(pick_key, (), 0, ROWS)
    row_ids = jnp.arange(ROWS, dtype=jnp.int32)[:, None]
    counts = jnp.where(row_ids == chosen, 6, counts)
    places = jnp.arange(LENGTH, dtype=jnp.int32)[None, :]
    clips = places // CLIP
    clips = jnp.where(clips < counts, clips, -1)
    return clips.astype(jnp.int32)


def levels(key, shape, cuts, least, largest):
    factor_of, own = 1.0, jax.random.fold_in(key, 6)
    for dim, shards_of in cuts:
        heights = jnp.exp(jax.random.uniform(jax.random.fold_in(own, dim), (shards_of,), jnp.float32, least / len(cuts), largest / len(cuts)))
        factor_of = factor_of * jnp.repeat(heights, shape[dim] // shards_of).reshape([-1 if axis == dim else 1 for axis in range(len(shape))])
    return factor_of


def noise(rng, dims, deviation, most, cuts=(), kind=jnp.bfloat16):
    entries = deviation * jax.random.normal(rng, dims, jnp.float32)
    if cuts:
        entries = entries * levels(rng, dims, cuts, -0.22, 0.18)
    return jnp.clip(entries, -most, most).astype(kind)


def setup_inputs(seed: int = 0) -> dict:
    splits = jax.random.split(jax.random.key(seed), 17)
    return {
        "tokens": noise(splits[0], (ROWS, LENGTH, D), 1.0, 6.0, ((0, 8), (1, 4))),
        "segments": draw_segments(jax.random.fold_in(splits[16], 71), 0),
        "ln1_gain": jnp.clip(1.0 + 0.1 * jax.random.normal(splits[2], (D,), jnp.float32), 0.5, 1.5),
        "ln1_bias": noise(splits[3], (D,), 0.5, 3.0, (), jnp.float32),
        "w_qkv": noise(splits[4], (D, 3 * D), D ** -0.5, 0.21875),
        "q_bias": noise(splits[5], (D,), 0.5, 3.0, (), jnp.float32),
        "v_bias": noise(splits[6], (D,), 0.5, 3.0, (), jnp.float32),
        "w_out": noise(splits[7], (D, D), (D // 64) ** -0.5, 1.75),
        "out_bias": noise(splits[8], (D,), 0.5, 3.0, (), jnp.float32),
        "ln2_gain": jnp.clip(1.0 + 0.1 * jax.random.normal(splits[9], (D,), jnp.float32), 0.5, 1.5),
        "ln2_bias": noise(splits[10], (D,), 0.5, 3.0, (), jnp.float32),
        "w_up": noise(splits[11], (D, FF), D ** -0.5, 0.21875),
        "up_bias": noise(splits[12], (FF,), 0.5, 3.0, (), jnp.float32),
        "w_down": noise(splits[13], (FF, D), FF ** -0.5, 0.109375),
        "down_bias": noise(splits[14], (D,), 0.5, 3.0, (), jnp.float32),
        "cotangent": noise(splits[15], (ROWS, LENGTH, D), 1.0, 6.0, ((0, 8), (1, 4))),
    }


@jax.custom_vjp
def low(v):
    return lax.optimization_barrier(v.astype(jnp.bfloat16)).astype(jnp.float32)

@jax.custom_vjp
def low_back(v):
    return v

def low_keep(v):
    return (low(v), None)

def low_pass(kept, grad):
    return (grad,)

def back_keep(v):
    return (v, None)

def back_low(kept, grad):
    return (low(grad),)
low.defvjp(low_keep, low_pass)
low_back.defvjp(back_keep, back_low)

def layer_norm(values, gain, bias):
    center = values - lax.optimization_barrier(jnp.mean(values, -1, keepdims=True))
    spread = lax.optimization_barrier(jnp.mean(center * center, -1, keepdims=True))
    return center * lax.rsqrt(spread + 1e-06) * gain + bias

def project(left, right):
    return jnp.einsum('rsd,de->rse', left, right, precision=lax.Precision.HIGHEST)

def attend_row(block):
    query, key, value, clips = block
    scores = jnp.einsum('qhd,khd->hqk', query, key, precision=lax.Precision.HIGHEST) * HEAD_DIM ** (-0.5)
    scores = low_back(scores)
    allowed = clips[:, None] == clips[None, :]
    scores = jnp.where(allowed[None], scores, -1e+30)
    prob = low(jax.nn.softmax(scores, -1))
    mixed = jnp.einsum('hqk,khd->qhd', prob, value, precision=lax.Precision.HIGHEST)
    return mixed.reshape(LENGTH, D)

def reference(tokens, segments, ln1_gain, ln1_bias, w_qkv, q_bias, v_bias, w_out, out_bias, ln2_gain, ln2_bias, w_up, up_bias, w_down, down_bias, cotangent):

    def forward(inputs, gain_one, bias_one, weight_qkv, bias_q, bias_v, weight_out, bias_out, gain_two, bias_two, weight_up, bias_up, weight_down, bias_down):
        normed = low(layer_norm(inputs, gain_one, bias_one))
        joined = jnp.concatenate([bias_q, jnp.zeros((D,), jnp.float32), bias_v])
        qkv = low(low_back(project(normed, weight_qkv) + joined))
        query = qkv[..., :D].reshape(ROWS, LENGTH, HEADS, HEAD_DIM)
        key = qkv[..., D:2 * D].reshape(ROWS, LENGTH, HEADS, HEAD_DIM)
        value = qkv[..., 2 * D:].reshape(ROWS, LENGTH, HEADS, HEAD_DIM)
        attended = lax.map(jax.checkpoint(attend_row), (query, key, value, segments))
        attended = low(low_back(attended))
        branch = low_back(project(attended, weight_out) + bias_out)
        middle = inputs + branch
        normed_two = low(layer_norm(middle, gain_two, bias_two))
        hidden = low_back(project(normed_two, weight_up) + bias_up)
        active = low(jax.nn.gelu(hidden, approximate=False))
        return middle + project(active, weight_down) + bias_down
    primals = (tokens.astype(jnp.float32), ln1_gain, ln1_bias, w_qkv.astype(jnp.float32), q_bias, v_bias, w_out.astype(jnp.float32), out_bias, ln2_gain, ln2_bias, w_up.astype(jnp.float32), up_bias, w_down.astype(jnp.float32), down_bias)
    result, backward = jax.vjp(forward, *primals)
    grads = backward(cotangent.astype(jnp.float32))
    return (result.astype(jnp.bfloat16), grads[0].astype(jnp.bfloat16), grads[1], grads[2], grads[3], grads[4], grads[5], grads[6], grads[7], grads[8], grads[9], grads[10], grads[11], grads[12], grads[13])
```

```python
import jax
import jax.numpy as jnp
import numpy as np
from jax import lax
from jax.experimental import pallas as pl
from jax.experimental.pallas import tpu as pltpu
from jax.sharding import PartitionSpec as P

HEADS = 12
HEAD_DIM = 64
CLIP = 157
UNIT = 768


def with_halo(block, sides, width):
    for axis, dim in sides:
        count = lax.axis_size(axis)
        forward = [(i, i + 1) for i in range(count - 1)]
        backward = [(target, source) for source, target in forward]
        low = lax.ppermute(
            lax.slice_in_dim(block, block.shape[dim] - width, None, axis=dim), axis, forward
        )
        high = lax.ppermute(lax.slice_in_dim(block, 0, width, axis=dim), axis, backward)
        block = jnp.concatenate([low, block, high], axis=dim)
    return block


def passed_along(block, axis, distance):
    devices = range(lax.axis_size(axis))
    route = [(i - distance, i) for i in devices if i - distance in devices]
    return lax.ppermute(block, axis, route)


def layer_norm(values, gain, bias):
    center = values - jnp.mean(values, -1, keepdims=True)
    spread = jnp.mean(center * center, -1, keepdims=True)
    return center * lax.rsqrt(spread + 1e-06) * gain + bias


def gelu_exact(values):
    return jax.nn.gelu(values, approximate=False)


def bit_orders(count, offset):
    bits = max(count.bit_length() - 1, 0)
    free = list(range(offset, bits))
    return free, free[::-1]


class Route:
    def __init__(self, seq_count, rows_count):
        self.seq_count, self.rows_count = seq_count, rows_count
        plain, turned = bit_orders(rows_count, 1)
        first = [0] if rows_count > 1 else []
        self.row_bits = [first + plain, first + turned]
        self.col_bits = list(bit_orders(seq_count, 0))
        self.row_stages = len(self.row_bits[0])
        self.col_stages = len(self.col_bits[0])
        table = [
            self.one_device(s, r) for s in range(seq_count) for r in range(rows_count)
        ]
        self.table = np.array([row for row, _ in table], np.int32)
        self.places = table[0][1]

    def one_device(self, s, r):
        row, places = [], {}
        core = r & 1
        kept, lists = list(range(self.rows_count)), []
        for t, bit in enumerate(self.row_bits[core]):
            send = [b for b in kept if (b ^ r) >> bit & 1]
            kept = [b for b in kept if not (b ^ r) >> bit & 1]
            for u, origin in enumerate([list(range(self.rows_count))] + lists):
                places["row", t, u] = (len(row), len(send))
                row += [origin.index(b) for b in send]
            lists.append(kept)
        for u, origin in enumerate([list(range(self.rows_count))] + lists):
            places["own", u] = (len(row), 1)
            row += [origin.index(r)]
        kept, lists = list(range(self.seq_count)), []
        for t, bit in enumerate(self.col_bits[core]):
            send = [b for b in kept if (b ^ s) >> bit & 1]
            kept = [b for b in kept if not (b ^ s) >> bit & 1]
            for u, origin in enumerate([list(range(self.seq_count))] + lists):
                places["col", t, u] = (len(row), len(send))
                row += [origin.index(b) for b in send]
            lists.append(kept)
        for u, origin in enumerate([list(range(self.seq_count))] + lists):
            places["end", u] = (len(row), 1)
            row += [origin.index(s)]
        return row, places

    def pairs(self, kind, t):
        out = []
        for s in range(self.seq_count):
            for r in range(self.rows_count):
                if kind == "row":
                    to = s * self.rows_count + (r ^ (1 << self.row_bits[r & 1][t]))
                else:
                    to = (s ^ (1 << self.col_bits[r & 1][t])) * self.rows_count + r
                out.append((s * self.rows_count + r, to))
        return out


def add_up(refs, dtype):
    total = refs[0][...].astype(jnp.float32)
    for ref in refs[1:]:
        total = total + ref[...].astype(jnp.float32)
    return total.astype(dtype)


def sum_kernel(tab_ref, *refs):
    del tab_ref
    refs[-1][...] = add_up(refs[:-1], refs[-1].dtype)


def row_part(route, tab, t, sources):
    _, rows, width = sources[0].shape
    count = route.places["row", t, 0][1]
    chunk = width // 2

    def spec(u):
        base = route.places["row", t, u][0]
        return pl.BlockSpec((1, rows, chunk), lambda j, c, tab: (tab[base + j], 0, c))

    return pl.pallas_call(
        sum_kernel,
        grid_spec=pltpu.PrefetchScalarGridSpec(
            num_scalar_prefetch=1,
            grid=(count, width // chunk),
            in_specs=[spec(u) for u in range(len(sources))],
            out_specs=pl.BlockSpec((1, rows, chunk), lambda j, c, tab: (j, 0, c)),
        ),
        out_shape=jax.ShapeDtypeStruct((count, rows, width), jnp.bfloat16),
        name="row_part",
    )(tab, *sources)


def col_part(route, tab, t, row_sources, col_sources, last=False):
    _, rows, width = row_sources[0].shape
    seq_count = route.seq_count
    groups = width // (seq_count * UNIT)
    key = ("end",) if last else ("col", t)
    count = route.places[key + (0,)][1]

    def row_spec(u):
        at = route.places["own", u][0]
        base = route.places[key + (0,)][0]
        return pl.BlockSpec(
            (1, rows, UNIT),
            lambda i, j, tab: (tab[at], 0, i * seq_count + tab[base + j]),
        )

    def col_spec(u):
        base = route.places[key + (u + 1,)][0]
        held = col_sources[u].shape[2] // (groups * UNIT)
        return pl.BlockSpec((1, rows, UNIT), lambda i, j, tab: (0, 0, i * held + tab[base + j]))

    if last:
        out_spec = pl.BlockSpec((1, rows, UNIT), lambda i, j, tab: (i, 0, 0))
        out_shape = jax.ShapeDtypeStruct((groups, rows, UNIT), jnp.float32)
    else:
        out_spec = pl.BlockSpec((1, rows, UNIT), lambda i, j, tab: (0, 0, i * count + j))
        out_shape = jax.ShapeDtypeStruct((1, rows, groups * count * UNIT), jnp.bfloat16)
    return pl.pallas_call(
        sum_kernel,
        grid_spec=pltpu.PrefetchScalarGridSpec(
            num_scalar_prefetch=1,
            grid=(groups, count),
            in_specs=[row_spec(u) for u in range(len(row_sources))]
            + [col_spec(u) for u in range(len(col_sources))],
            out_specs=out_spec,
        ),
        out_shape=out_shape,
        name="col_part",
    )(tab, *row_sources, *col_sources)


def scatter_sum(route, tab, grad):
    rows = grad.shape[0] // route.rows_count
    row_sources = [grad.reshape(route.rows_count, rows, grad.shape[1])]
    for t in range(route.row_stages):
        send = row_part(route, tab, t, row_sources)
        row_sources.append(lax.ppermute(send, ("seq", "rows"), route.pairs("row", t)))
    col_sources = []
    for t in range(route.col_stages):
        send = col_part(route, tab, t, row_sources, col_sources)
        col_sources.append(lax.ppermute(send, ("seq", "rows"), route.pairs("col", t)))
    return col_part(route, tab, 0, row_sources, col_sources, last=True)


def sum_everywhere(route, values):
    for t in range(route.row_stages):
        values = values + lax.ppermute(values, ("seq", "rows"), route.pairs("row", t))
    for t in range(route.col_stages):
        values = values + lax.ppermute(values, ("seq", "rows"), route.pairs("col", t))
    return values


def on_device(
    tokens,
    segments,
    ln1_gain,
    ln1_bias,
    w_qkv,
    q_bias,
    v_bias,
    w_out,
    out_bias,
    ln2_gain,
    ln2_bias,
    w_up,
    up_bias,
    w_down,
    down_bias,
    cotangent,
):
    row_count, slot_count, width = tokens.shape
    margin = CLIP - 1
    scale = HEAD_DIM ** (-0.5)
    inputs = tokens.astype(jnp.float32)
    normed, norm_one_back = jax.vjp(layer_norm, inputs, ln1_gain, ln1_bias)
    normed_b = normed.astype(jnp.bfloat16)
    joined = jnp.concatenate([q_bias, jnp.zeros_like(q_bias), v_bias])
    qkv = (
        jnp.einsum("rsd,de->rse", normed_b, w_qkv, preferred_element_type=jnp.float32) + joined
    ).astype(jnp.bfloat16)
    query = qkv[..., :width]
    key_value = qkv[..., width:]
    shifted_ids = (segments + 2).astype(jnp.bfloat16)
    kv_ext, clip_ext = (
        with_halo(key_value, (("seq", 1),), margin),
        with_halo(shifted_ids, (("seq", 1),), margin),
    )
    full_len = kv_ext.shape[1]
    query4 = query.reshape(row_count, slot_count, HEADS, HEAD_DIM)
    key4 = kv_ext[..., :width].reshape(row_count, full_len, HEADS, HEAD_DIM)
    value4 = kv_ext[..., width:].reshape(row_count, full_len, HEADS, HEAD_DIM)
    own_ids = (segments + 2).astype(jnp.float32)
    allowed = own_ids[:, None, :, None] == clip_ext.astype(jnp.float32)[:, None, None, :]

    def masked_scores():
        raw = (
            jnp.einsum("rqhd,rkhd->rhqk", query4, key4, preferred_element_type=jnp.float32) * scale
        )
        return jnp.where(allowed, raw, -1e30)

    scores = masked_scores()
    peak = jnp.max(scores, -1, keepdims=True)
    weights = jnp.exp(scores - peak)
    total = jnp.sum(weights, -1, keepdims=True)
    log_total = peak + jnp.log(total)
    prob_b = (weights / total).astype(jnp.bfloat16)
    attended = jnp.einsum("rhqk,rkhd->rqhd", prob_b, value4, preferred_element_type=jnp.float32)
    attended_b = attended.reshape(row_count, slot_count, width).astype(jnp.bfloat16)
    middle = (
        inputs
        + jnp.einsum("rsd,de->rse", attended_b, w_out, preferred_element_type=jnp.float32)
        + out_bias
    )
    normed_two, norm_two_back = jax.vjp(layer_norm, middle, ln2_gain, ln2_bias)
    normed_two_b = normed_two.astype(jnp.bfloat16)
    hidden = (
        jnp.einsum("rsd,df->rsf", normed_two_b, w_up, preferred_element_type=jnp.float32) + up_bias
    )
    active, gelu_back = jax.vjp(gelu_exact, hidden)
    active_b = active.astype(jnp.bfloat16)
    result = (
        middle
        + jnp.einsum("rsf,fd->rsd", active_b, w_down, preferred_element_type=jnp.float32)
        + down_bias
    )
    grad_w_down = jnp.einsum("rsd,rsf->df", cotangent, active_b, preferred_element_type=jnp.float32)
    grad_down_bias = jnp.sum(cotangent.astype(jnp.float32), (0, 1))
    d_active = jnp.einsum("rsd,fd->rsf", cotangent, w_down, preferred_element_type=jnp.float32)
    d_hidden = gelu_back(d_active)[0].astype(jnp.bfloat16)
    grad_w_up = jnp.einsum(
        "rsd,rsf->df", normed_two_b, d_hidden, preferred_element_type=jnp.float32
    )
    grad_up_bias = jnp.sum(d_hidden.astype(jnp.float32), (0, 1))
    d_normed_two = jnp.einsum("rsf,df->rsd", d_hidden, w_up, preferred_element_type=jnp.float32)
    d_middle_norm, grad_ln2_gain, grad_ln2_bias = norm_two_back(d_normed_two)
    d_middle = cotangent.astype(jnp.float32) + d_middle_norm
    d_branch = d_middle.astype(jnp.bfloat16)
    grad_w_out = jnp.einsum("rsd,rse->de", attended_b, d_branch, preferred_element_type=jnp.float32)
    grad_out_bias = jnp.sum(d_branch.astype(jnp.float32), (0, 1))
    d_attended = jnp.einsum("rse,de->rsd", d_branch, w_out, preferred_element_type=jnp.float32)
    d_attended4 = d_attended.astype(jnp.bfloat16).reshape(row_count, slot_count, HEADS, HEAD_DIM)
    again = jnp.exp(masked_scores() - log_total)
    again_b = again.astype(jnp.bfloat16)
    d_value_part = jnp.einsum(
        "rhqk,rqhd->rkhd", again_b, d_attended4, preferred_element_type=jnp.float32
    )
    d_prob = jnp.einsum("rqhd,rkhd->rhqk", d_attended4, value4, preferred_element_type=jnp.float32)
    centre = jnp.sum(d_prob * again, -1, keepdims=True)
    d_scores = (again * (d_prob - centre)).astype(jnp.bfloat16)
    d_query = (
        jnp.einsum("rhqk,rkhd->rqhd", d_scores, key4, preferred_element_type=jnp.float32) * scale
    )
    d_key_part = (
        jnp.einsum("rhqk,rqhd->rkhd", d_scores, query4, preferred_element_type=jnp.float32) * scale
    )
    d_kv_ext = jnp.concatenate(
        [
            d_key_part.reshape(row_count, full_len, width),
            d_value_part.reshape(row_count, full_len, width),
        ],
        -1,
    )
    lower_rim = d_kv_ext[:, :margin]
    upper_rim = d_kv_ext[:, margin + slot_count :]
    d_kv_own = d_kv_ext[:, margin : margin + slot_count]
    from_above = passed_along(lower_rim.astype(jnp.bfloat16), "seq", -1).astype(lower_rim.dtype)
    from_below = passed_along(upper_rim.astype(jnp.bfloat16), "seq", 1).astype(upper_rim.dtype)
    d_kv_own = d_kv_own.at[:, slot_count - margin :].add(from_above)
    d_kv_own = d_kv_own.at[:, :margin].add(from_below)
    d_qkv = jnp.concatenate(
        [
            d_query.reshape(row_count, slot_count, width).astype(jnp.bfloat16),
            d_kv_own.astype(jnp.bfloat16),
        ],
        -1,
    )
    grad_w_qkv = jnp.einsum("rsd,rse->de", normed_b, d_qkv, preferred_element_type=jnp.float32)
    d_qkv_sums = jnp.sum(d_qkv.astype(jnp.float32), (0, 1))
    grad_q_bias = d_qkv_sums[:width]
    grad_v_bias = d_qkv_sums[2 * width :]
    d_normed = jnp.einsum("rse,de->rsd", d_qkv, w_qkv, preferred_element_type=jnp.float32)
    d_input_norm, grad_ln1_gain, grad_ln1_bias = norm_one_back(d_normed)
    grad_input = (d_middle + d_input_norm).astype(jnp.bfloat16)
    vectors = jnp.stack(
        [
            grad_ln1_gain,
            grad_ln1_bias,
            grad_q_bias,
            grad_v_bias,
            grad_out_bias,
            grad_ln2_gain,
            grad_ln2_bias,
            grad_down_bias,
        ],
        0,
    )
    seq_count = lax.axis_size("seq")
    rows_count = lax.axis_size("rows")
    route = Route(seq_count, rows_count)
    tab = jnp.asarray(route.table)[lax.axis_index("seq") * rows_count + lax.axis_index("rows")]
    all_vectors = jnp.concatenate([vectors, grad_up_bias.reshape(4, width)], 0)
    all_vectors = sum_everywhere(route, all_vectors)
    sums_vec, sum_up_bias = all_vectors[:8], all_vectors[8:].reshape(4 * width)
    mlp_grads = jnp.concatenate([grad_w_up, grad_w_down], 1).astype(jnp.bfloat16)
    attention_grads = jnp.concatenate(
        [
            grad_w_qkv.reshape(width, seq_count, -1),
            grad_w_out.reshape(width, seq_count, -1),
        ],
        2,
    ).reshape(width, 4 * width).astype(jnp.bfloat16)
    sums_mlp = scatter_sum(route, tab, mlp_grads)
    sums_attention = scatter_sum(route, tab, attention_grads)
    sum_up, sum_down = sums_mlp[0], sums_mlp[1].T
    cut = 3 * width // seq_count
    sum_qkv, sum_out = sums_attention[0][:, :cut], sums_attention[0][:, cut:]
    return (
        result.astype(jnp.bfloat16),
        grad_input,
        sums_vec[0],
        sums_vec[1],
        sum_qkv,
        sums_vec[2],
        sums_vec[3],
        sum_out,
        sums_vec[4],
        sums_vec[5],
        sums_vec[6],
        sum_up,
        sum_up_bias,
        sum_down,
        sums_vec[7],
    )


def solution(mesh):
    placed = (
        P("rows", "seq", None),
        P("rows", "seq"),
        P(),
        P(),
        P(),
        P(),
        P(),
        P(),
        P(),
        P(),
        P(),
        P(),
        P(),
        P(),
        P(),
        P("rows", "seq", None),
    )
    return jax.shard_map(
        on_device,
        mesh=mesh,
        in_specs=placed,
        out_specs=(
            P("rows", "seq", None),
            P("rows", "seq", None),
            P(),
            P(),
            P("rows", "seq"),
            P(),
            P(),
            P("rows", "seq"),
            P(),
            P(),
            P(),
            P("rows", "seq"),
            P(),
            P("seq", "rows"),
            P(),
        ),
        check_vma=False,
    )
```

```python
import functools

import jax
import jax.numpy as jnp
import numpy as np
from jax import lax
from jax.experimental import pallas as pl
from jax.experimental.pallas import tpu as pltpu
from jax.sharding import PartitionSpec as P

HEAD_DIM = 64
CLIP = 157
UNIT = 768
VMEM_LIMIT = 56 * 1024 * 1024


def bit_orders(count, offset):
    bits = max(count.bit_length() - 1, 0)
    free = list(range(offset, bits))
    return free, free[::-1]


class Route:
    def __init__(self, seq_count, rows_count):
        self.seq_count, self.rows_count = seq_count, rows_count
        plain, turned = bit_orders(rows_count, 1)
        first = [0] if rows_count > 1 else []
        self.row_bits = [first + plain, first + turned]
        self.col_bits = list(bit_orders(seq_count, 0))
        self.row_stages = len(self.row_bits[0])
        self.col_stages = len(self.col_bits[0])
        table = [
            self.one_device(s, r) for s in range(seq_count) for r in range(rows_count)
        ]
        self.table = np.array([row for row, _ in table], np.int32)
        self.places = table[0][1]

    def one_device(self, s, r):
        row, places = [], {}
        core = r & 1
        kept, lists = list(range(self.rows_count)), []
        for t, bit in enumerate(self.row_bits[core]):
            send = [b for b in kept if (b ^ r) >> bit & 1]
            kept = [b for b in kept if not (b ^ r) >> bit & 1]
            for u, origin in enumerate(lists[:1] + lists):
                places["row", t, u] = (len(row), len(send))
                row += [origin.index(b) for b in send]
            lists.append(kept)
        for u, origin in enumerate(lists[:1] + lists):
            places["own", u] = (len(row), 1)
            row += [origin.index(r)]
        kept, lists = list(range(self.seq_count)), []
        for t, bit in enumerate(self.col_bits[core]):
            send = [b for b in kept if (b ^ s) >> bit & 1]
            kept = [b for b in kept if not (b ^ s) >> bit & 1]
            for u, origin in enumerate([list(range(self.seq_count))] + lists):
                places["col", t, u] = (len(row), len(send))
                row += [origin.index(b) for b in send]
            lists.append(kept)
        for u, origin in enumerate([list(range(self.seq_count))] + lists):
            places["end", u] = (len(row), 1)
            row += [origin.index(s)]
        return row, places

    def pairs(self, kind, t):
        out = []
        for s in range(self.seq_count):
            for r in range(self.rows_count):
                if kind == "row":
                    to = s * self.rows_count + (r ^ (1 << self.row_bits[r & 1][t]))
                else:
                    to = (s ^ (1 << self.col_bits[r & 1][t])) * self.rows_count + r
                out.append((s * self.rows_count + r, to))
        return out


def add_up(refs, dtype):
    total = refs[0][...].astype(jnp.float32)
    for ref in refs[1:]:
        total = total + ref[...].astype(jnp.float32)
    return total.astype(dtype)


def sum_kernel(tab_ref, *refs):
    del tab_ref
    refs[-1][...] = add_up(refs[:-1], refs[-1].dtype)


def row_part(route, tab, t, sources):
    _, rows, width = sources[0].shape
    count = route.places["row", t, 0][1]
    chunk = width // 2

    def spec(u):
        base = route.places["row", t, u][0]
        return pl.BlockSpec((1, rows, chunk), lambda j, c, tab: (tab[base + j], 0, c))

    return pl.pallas_call(
        sum_kernel,
        grid_spec=pltpu.PrefetchScalarGridSpec(
            num_scalar_prefetch=1,
            grid=(count, width // chunk),
            in_specs=[spec(u) for u in range(len(sources))],
            out_specs=pl.BlockSpec((1, rows, chunk), lambda j, c, tab: (j, 0, c)),
        ),
        out_shape=jax.ShapeDtypeStruct((count, rows, width), jnp.bfloat16),
        name="row_part",
    )(tab, *sources)


def col_part(route, tab, t, row_sources, col_sources, last=False):
    _, rows, width = row_sources[0].shape
    chunk = width // route.seq_count
    key = ("end",) if last else ("col", t)
    count = route.places[key + (0,)][1]

    def row_spec(u):
        at = route.places["own", u][0]
        base = route.places[key + (0,)][0]
        return pl.BlockSpec((None, rows, chunk), lambda j, tab: (tab[at], 0, tab[base + j]))

    def col_spec(u):
        base = route.places[key + (u + 1,)][0]
        return pl.BlockSpec((rows, chunk), lambda j, tab: (0, tab[base + j]))

    return pl.pallas_call(
        sum_kernel,
        grid_spec=pltpu.PrefetchScalarGridSpec(
            num_scalar_prefetch=1,
            grid=(count,),
            in_specs=[row_spec(u) for u in range(len(row_sources))]
            + [col_spec(u) for u in range(len(col_sources))],
            out_specs=pl.BlockSpec((rows, chunk), lambda j, tab: (0, j)),
        ),
        out_shape=jax.ShapeDtypeStruct((rows, count * chunk), jnp.float32 if last else jnp.bfloat16),
        name="col_part",
    )(tab, *row_sources, *col_sources)


def scatter_sum(route, tab, send, keep):
    row_sources = [keep]
    for t in range(route.row_stages):
        if t > 0:
            send = row_part(route, tab, t, row_sources)
        row_sources.append(lax.ppermute(send, ("seq", "rows"), route.pairs("row", t)))
    col_sources = []
    for t in range(route.col_stages):
        send = col_part(route, tab, t, row_sources, col_sources)
        col_sources.append(lax.ppermute(send, ("seq", "rows"), route.pairs("col", t)))
    return col_part(route, tab, 0, row_sources, col_sources, last=True)


def sum_everywhere(route, values):
    for t in range(route.row_stages):
        values = values + lax.ppermute(values, ("seq", "rows"), route.pairs("row", t))
    for t in range(route.col_stages):
        values = values + lax.ppermute(values, ("seq", "rows"), route.pairs("col", t))
    return values


def dot(left, right):
    return lax.dot_general(left, right, (((1,), (0,)), ((), ())), preferred_element_type=jnp.float32)


def dot_t(left, right):
    return lax.dot_general(left, right, (((1,), (1,)), ((), ())), preferred_element_type=jnp.float32)


def t_dot(left, right):
    return lax.dot_general(left, right, (((0,), (0,)), ((), ())), preferred_element_type=jnp.float32)


def up_to(value, step):
    return -(-value // step) * step


class Clips:
    def __init__(self, slot_count, seq_count):
        self.slots = slot_count
        length = slot_count * seq_count
        sure = length // CLIP - 1
        self.tail = length - sure * CLIP
        self.a_rows = up_to(CLIP, 16)
        self.b_rows = up_to(max(CLIP, self.tail), 16)
        self.rows = self.a_rows + self.b_rows
        self.shards = []
        reach = 0
        for s in range(seq_count):
            low = s * slot_count
            held = [(k * CLIP - low, CLIP) for k in range(sure) if 0 <= k * CLIP - low < slot_count]
            block_a, block_b, has_tail = (0, 0), (0, 0), 0
            if held:
                block_a = held[0]
            if len(held) > 1:
                block_b = held[1]
            if 0 <= sure * CLIP - low < slot_count:
                assert len(held) < 2
                block_b, has_tail = (sure * CLIP - low, self.tail), 1
            assert len(held) < 3
            reach = max([reach] + [at + count - slot_count for at, count in (block_a, block_b)])
            self.shards.append((*block_a, *block_b, has_tail))
        self.tail_at = (sure * CLIP) % slot_count
        self.halo = up_to(reach, 16)
        self.window = slot_count + self.halo


CORE_AT = 4
SPLITS_AT = 5


def chosen(tab_ref, clips, turned):
    a_at, a_len, b_at, b_len = (tab_ref[k] for k in range(4))
    if turned:
        shape, row_dim = (clips.window, clips.rows), 1
    else:
        shape, row_dim = (clips.rows, clips.window), 0
    row = lax.broadcasted_iota(jnp.int32, shape, row_dim)
    slot = lax.broadcasted_iota(jnp.int32, shape, 1 - row_dim)
    in_a = (row < a_len) & (slot == row + a_at)
    second = row - clips.a_rows
    in_b = (second >= 0) & (second < b_len) & (slot == second + b_at)
    return jnp.where(in_a | in_b, 1.0, 0.0).astype(jnp.bfloat16)


def block_masks(tab_ref, clips, row, key_dim):
    shape_a = (1, clips.a_rows) if key_dim == 1 else (clips.a_rows, 1)
    key_a = lax.broadcasted_iota(jnp.int32, shape_a, key_dim)
    mask_a = jnp.where(key_a < CLIP, 0.0, -1e30)
    shape_b = (clips.b_rows, clips.b_rows)
    key_b = lax.broadcasted_iota(jnp.int32, shape_b, key_dim)
    query_b = lax.broadcasted_iota(jnp.int32, shape_b, 1 - key_dim)
    split, b_len = tab_ref[SPLITS_AT + row], jnp.maximum(tab_ref[3], 1)
    fits = (key_b < b_len) & ((key_b < split) == (query_b < split))
    mask_b = jnp.where(fits, 0.0, -1e30)
    return mask_a, mask_b


def norm_parts(values):
    center = values - jnp.mean(values, -1, keepdims=True)
    spread = jnp.mean(center * center, -1, keepdims=True)
    rate = lax.rsqrt(spread + 1e-06)
    return center * rate, rate


def norm_back(d_unit, unit, rate):
    return rate * (
        d_unit
        - jnp.mean(d_unit, -1, keepdims=True)
        - unit * jnp.mean(d_unit * unit, -1, keepdims=True)
    )


def split_heads(pair):
    low = lax.broadcasted_iota(jnp.int32, pair.shape, 1) < HEAD_DIM
    zero = jnp.zeros_like(pair)
    return jnp.concatenate([jnp.where(low, pair, zero), jnp.where(low, zero, pair)], 0)


def join_heads(both):
    half = both.shape[0] // 2
    low = lax.broadcasted_iota(jnp.int32, (half, both.shape[1]), 1) < HEAD_DIM
    return jnp.where(low, both[:half], both[half:])


def attend_kernel(
    clips, tab_ref, x_ref, halo_ref, gain_ref, bias_ref, w_ref, wb_ref,
    qkv_ref, normed_ref, own_ref, edge_ref, att_ref,
):
    row_count, _, width = x_ref.shape
    rows = clips.rows
    pick = chosen(tab_ref, clips, False)
    for r in range(row_count):
        window = jnp.concatenate([x_ref[r], halo_ref[r]], 0)
        unit, _ = norm_parts(dot(pick, window))
        normed_ref[r] = (unit * gain_ref[...] + bias_ref[...]).astype(jnp.bfloat16)
    for part in range(3):
        cols = slice(part * width, (part + 1) * width)
        for r in range(row_count):
            made = dot(normed_ref[r], w_ref[:, cols]) + wb_ref[:, cols]
            if part == 0:
                made = made * HEAD_DIM ** (-0.5)
            qkv_ref[r, :, cols] = made.astype(jnp.bfloat16)
    for r in range(row_count):
        masks = block_masks(tab_ref, clips, r, 1)
        for base, count, mask in ((0, clips.a_rows, masks[0]), (clips.a_rows, clips.b_rows, masks[1])):
            here = slice(base, base + count)
            if mask.shape[0] > 1:
                mask = jnp.concatenate([mask, mask], 0)
            for p in range(width // 128):
                query, key, value = (
                    qkv_ref[r, here, k * width + p * 128 : k * width + (p + 1) * 128] for k in range(3)
                )
                scores = dot_t(split_heads(query), key) + mask
                peak = jnp.max(scores, -1, keepdims=True)
                weights = jnp.exp(scores - peak)
                total = jnp.sum(weights, -1, keepdims=True)
                mixed = dot(weights.astype(jnp.bfloat16), value) / total
                att_ref[here, p * 128 : (p + 1) * 128] = join_heads(mixed).astype(jnp.bfloat16)
        back = dot(chosen(tab_ref, clips, True), att_ref[...]).astype(jnp.bfloat16)
        own_ref[r] = back[: clips.slots]
        edge_ref[r] = back[clips.slots :]


def whole(*shape):
    return pl.BlockSpec(shape, lambda *_: (0,) * len(shape))


def attend(clips, tab, tokens, halo, gain, bias, weight, weight_bias):
    row_count, slots, width = tokens.shape
    shapes = [
        ((row_count, clips.rows, 3 * width), jnp.bfloat16),
        ((row_count, clips.rows, width), jnp.bfloat16),
        ((row_count, slots, width), jnp.bfloat16),
        ((row_count, clips.halo, width), jnp.bfloat16),
    ]
    args = (tokens, halo, gain, bias, weight, weight_bias)
    return pl.pallas_call(
        functools.partial(attend_kernel, clips),
        grid_spec=pltpu.PrefetchScalarGridSpec(
            num_scalar_prefetch=1,
            grid=(1,),
            in_specs=[whole(*a.shape) for a in args],
            out_specs=[whole(*shape) for shape, _ in shapes],
            scratch_shapes=[pltpu.VMEM((clips.rows, width), jnp.bfloat16)],
        ),
        out_shape=[jax.ShapeDtypeStruct(*s) for s in shapes],
        compiler_params=pltpu.CompilerParams(vmem_limit_bytes=VMEM_LIMIT),
        name="attend",
    )(tab, *args)


def over(values, count, top):
    factor = -(-(1 << 18) // count)
    assert all((k * factor) >> 18 == k // count for k in range(top))
    return (values * factor) >> 18


def turn(tab_ref, width, parts):
    core = tab_ref[CORE_AT]
    rows, half = width // parts, width // 2
    at = lax.broadcasted_iota(jnp.int32, (width, 1), 0)
    mine = at >= half
    at = jnp.where(mine, at - half, at)
    source = at + (over(at, rows, half) + jnp.where(mine, core, 1 - core)) * rows
    column = lax.broadcasted_iota(jnp.int32, (width, width), 1)
    return jnp.where(column == source, 1.0, 0.0).astype(jnp.bfloat16)


def put_halves(grad, send_ref, keep_ref, cols):
    parts, rows, _ = send_ref.shape
    made = grad.astype(send_ref.dtype)
    for k in range(parts):
        send_ref[k, :, cols] = made[k * rows : (k + 1) * rows]
        keep_ref[k, :, cols] = made[(parts + k) * rows : (parts + k + 1) * rows]


def gelu_parts(hidden):
    cdf = 0.5 + 0.5 * lax.erf(hidden * 0.7071067811865476)
    return hidden * cdf, cdf + hidden * (0.3989422804014327 * jnp.exp(-0.5 * hidden * hidden))


def mlp_kernel(
    clips, parts, tab_ref, x_ref, att_ref, edge_ref, c_ref, w_out_ref, out_bias_ref, gain_ref, bias_ref,
    w_up_ref, up_bias_ref, w_down_ref, down_bias_ref,
    out_ref, d_att_ref, d_middle_ref, send_ref, keep_ref, out_send_ref, out_keep_ref, vec_ref, up_vec_ref,
    att_s, middle_s, unit_s, rate_s, normed_s, normed_t, cot_t, att_t, result_s, d_normed_s,
):
    step, steps = pl.program_id(0), pl.num_programs(0)
    row_count, slots, width = x_ref.shape
    chunk = w_up_ref.shape[1]

    @pl.when(step == 0)
    def _():
        for r in range(row_count):
            here = slice(r * slots, (r + 1) * slots)
            first = att_ref[r, : clips.halo] + edge_ref[r]
            att_s[here] = jnp.concatenate([first, att_ref[r, clips.halo :]], 0)
            middle = x_ref[r].astype(jnp.float32) + dot(att_s[here], w_out_ref[...]) + out_bias_ref[...]
            middle_s[here] = middle
            unit, rate = norm_parts(middle)
            unit_s[here] = unit
            rate_s[here] = rate
            normed_s[here] = (unit * gain_ref[...] + bias_ref[...]).astype(jnp.bfloat16)
        order = turn(tab_ref, width, parts)
        normed_t[...] = dot_t(order, normed_s[...]).astype(jnp.bfloat16)
        cot_t[...] = dot_t(order, c_ref[...].reshape(row_count * slots, width)).astype(jnp.bfloat16)
        att_t[...] = dot_t(order, att_s[...]).astype(jnp.bfloat16)
        result_s[...] = jnp.zeros_like(result_s)
        d_normed_s[...] = jnp.zeros_like(d_normed_s)

    hidden_back = []
    active_all = []
    for r in range(row_count):
        here = slice(r * slots, (r + 1) * slots)
        hidden = dot(normed_s[here], w_up_ref[...]) + up_bias_ref[...]
        active, slope = gelu_parts(hidden)
        active_b = active.astype(jnp.bfloat16)
        result_s[here] += dot(active_b, w_down_ref[...])
        d_hidden = (dot_t(c_ref[r], w_down_ref[...]) * slope).astype(jnp.bfloat16)
        d_normed_s[here] += dot_t(d_hidden, w_up_ref[...])
        hidden_back.append(d_hidden)
        active_all.append(active_b)
    d_hidden = jnp.concatenate(hidden_back, 0)
    active_b = jnp.concatenate(active_all, 0)
    up_vec_ref[...] = jnp.sum(d_hidden.astype(jnp.float32), 0, keepdims=True)
    put_halves(dot(normed_t[...], d_hidden), send_ref, keep_ref, slice(0, chunk))
    put_halves(dot(cot_t[...], active_b), send_ref, keep_ref, slice(chunk, 2 * chunk))

    @pl.when(step == steps - 1)
    def _():
        sums = []
        branches = []
        for r in range(row_count):
            here = slice(r * slots, (r + 1) * slots)
            out_ref[r] = (middle_s[here] + result_s[here] + down_bias_ref[...]).astype(jnp.bfloat16)
            d_normed, unit = d_normed_s[here], unit_s[here]
            cot = c_ref[r].astype(jnp.float32)
            d_middle = cot + norm_back(d_normed * gain_ref[...], unit, rate_s[here])
            d_middle_ref[r] = d_middle
            branch = d_middle.astype(jnp.bfloat16)
            branches.append(branch)
            d_att_ref[r] = dot_t(branch, w_out_ref[...]).astype(jnp.bfloat16)
            parts_here = (branch.astype(jnp.float32), d_normed * unit, d_normed, cot)
            sums.append([jnp.sum(p, 0, keepdims=True) for p in parts_here])
        for k in range(4):
            vec_ref[k : k + 1] = sum(s[k] for s in sums[1:]) + sums[0][k]
        put_halves(dot(att_t[...], jnp.concatenate(branches, 0)), out_send_ref, out_keep_ref, slice(0, width))


def mlp(clips, parts, seq_count, tab, tokens, att, edge, cot, w_out, out_bias, gain, bias, w_up, up_bias, w_down, down_bias):
    row_count, slots, width = tokens.shape
    count = row_count * slots
    chunk = w_up.shape[1] // seq_count
    rows = width // parts
    half = parts // 2
    bf16, f32 = jnp.bfloat16, jnp.float32
    args = (tokens, att, edge, cot, w_out, out_bias, gain, bias, w_up, up_bias, w_down, down_bias)
    in_specs = [whole(*a.shape) for a in args]
    in_specs[8] = pl.BlockSpec((width, chunk), lambda f, tab: (0, f))
    in_specs[9] = pl.BlockSpec((1, chunk), lambda f, tab: (0, f))
    in_specs[10] = pl.BlockSpec((chunk, width), lambda f, tab: (f, 0))
    shapes = [
        ((row_count, slots, width), bf16),
        ((row_count, slots, width), bf16),
        ((row_count, slots, width), f32),
        ((half, rows, 2 * seq_count * chunk), bf16),
        ((half, rows, 2 * seq_count * chunk), bf16),
        ((half, rows, width), bf16),
        ((half, rows, width), bf16),
        ((4, width), f32),
        ((1, seq_count * chunk), f32),
    ]
    out_specs = [whole(*shape) for shape, _ in shapes]
    out_specs[3] = out_specs[4] = pl.BlockSpec((half, rows, 2 * chunk), lambda f, tab: (0, 0, f))
    out_specs[8] = pl.BlockSpec((1, chunk), lambda f, tab: (0, f))
    return pl.pallas_call(
        functools.partial(mlp_kernel, clips, parts),
        grid_spec=pltpu.PrefetchScalarGridSpec(
            num_scalar_prefetch=1,
            grid=(seq_count,),
            in_specs=in_specs,
            out_specs=out_specs,
            scratch_shapes=[
                pltpu.VMEM((count, width), bf16),
                pltpu.VMEM((count, width), f32),
                pltpu.VMEM((count, width), f32),
                pltpu.VMEM((count, 1), f32),
                pltpu.VMEM((count, width), bf16),
                pltpu.VMEM((width, count), bf16),
                pltpu.VMEM((width, count), bf16),
                pltpu.VMEM((width, count), bf16),
                pltpu.VMEM((count, width), f32),
                pltpu.VMEM((count, width), f32),
            ],
        ),
        out_shape=[jax.ShapeDtypeStruct(*s) for s in shapes],
        compiler_params=pltpu.CompilerParams(vmem_limit_bytes=VMEM_LIMIT),
        name="mlp",
    )(tab, *args)


def attend_back_kernel(
    clips, parts, seq_count, tab_ref, qkv_ref, normed_ref, d_att_ref, d_edge_ref, out_send_ref, out_keep_ref,
    d_qkv_ref, send_ref, keep_ref, vec_ref,
    d_mixed_s, normed_t,
):
    row_count, rows, width = normed_ref.shape
    scale = HEAD_DIM ** (-0.5)
    pick = chosen(tab_ref, clips, False)
    for r in range(row_count):
        window = jnp.concatenate([d_att_ref[r], d_edge_ref[r]], 0)
        d_mixed_s[...] = dot(pick, window).astype(jnp.bfloat16)
        masks = block_masks(tab_ref, clips, r, 0)
        for base, count, mask in ((0, clips.a_rows, masks[0]), (clips.a_rows, clips.b_rows, masks[1])):
            here = slice(base, base + count)
            if mask.shape[1] > 1:
                mask = jnp.concatenate([mask, mask], 1)
            for p in range(width // 128):
                cols = [slice(k * width + p * 128, k * width + (p + 1) * 128) for k in range(3)]
                query, key, value = (qkv_ref[r, here, c] for c in cols)
                queries = split_heads(query)
                d_mixed = split_heads(d_mixed_s[here, cols[0]])
                scores = dot_t(key, queries) + mask
                peak = jnp.max(scores, 0, keepdims=True)
                weights = jnp.exp(scores - peak)
                prob = weights * (1.0 / jnp.sum(weights, 0, keepdims=True))
                d_value = dot(prob.astype(jnp.bfloat16), d_mixed)
                d_prob = dot_t(value, d_mixed)
                centre = jnp.sum(d_prob * prob, 0, keepdims=True)
                d_scores = (prob * (d_prob - centre)).astype(jnp.bfloat16)
                d_key = dot(d_scores, queries)
                d_query = join_heads(t_dot(d_scores, key)) * scale
                for c, made in zip(cols, (d_query, d_key, d_value)):
                    d_qkv_ref[r, here, c] = made.astype(jnp.bfloat16)
    total = jnp.zeros((1, 3 * width), jnp.float32)
    for r in range(row_count):
        total = total + jnp.sum(d_qkv_ref[r].astype(jnp.float32), 0, keepdims=True)
    vec_ref[...] = total
    flat = normed_ref[...].reshape(row_count * rows, width)
    normed_t[...] = dot_t(turn(tab_ref, width, parts), flat).astype(jnp.bfloat16)
    cut, out_cut = 3 * width // seq_count, width // seq_count
    for s in range(seq_count):
        d_part = d_qkv_ref[:, :, s * cut : (s + 1) * cut].reshape(row_count * rows, cut)
        made = dot(normed_t[...], d_part).astype(jnp.bfloat16)
        half = send_ref.shape[0]
        height = send_ref.shape[1]
        for ref, other, first in ((send_ref, out_send_ref, 0), (keep_ref, out_keep_ref, half)):
            for k in range(half):
                piece = made[(first + k) * height : (first + k + 1) * height]
                rest = other[k, :, s * out_cut : (s + 1) * out_cut]
                ref[k, :, s * UNIT : (s + 1) * UNIT] = jnp.concatenate([piece, rest], 1)


def attend_back(clips, parts, seq_count, tab, qkv, normed, d_att, d_edge, out_send, out_keep):
    row_count, rows, width = normed.shape
    half = parts // 2
    shapes = [
        ((row_count, rows, 3 * width), jnp.bfloat16),
        ((half, width // parts, seq_count * UNIT), jnp.bfloat16),
        ((half, width // parts, seq_count * UNIT), jnp.bfloat16),
        ((1, 3 * width), jnp.float32),
    ]
    args = (qkv, normed, d_att, d_edge, out_send, out_keep)
    return pl.pallas_call(
        functools.partial(attend_back_kernel, clips, parts, seq_count),
        grid_spec=pltpu.PrefetchScalarGridSpec(
            num_scalar_prefetch=1,
            grid=(1,),
            in_specs=[whole(*a.shape) for a in args],
            out_specs=[whole(*shape) for shape, _ in shapes],
            scratch_shapes=[
                pltpu.VMEM((rows, width), jnp.bfloat16),
                pltpu.VMEM((width, row_count * rows), jnp.bfloat16),
            ],
        ),
        out_shape=[jax.ShapeDtypeStruct(*s) for s in shapes],
        compiler_params=pltpu.CompilerParams(vmem_limit_bytes=VMEM_LIMIT),
        name="attend_back",
    )(tab, *args)


def first_back_kernel(
    clips, tab_ref, d_qkv_ref, w_ref, x_ref, halo_ref, gain_ref, own_ref, edge_ref, vec_ref
):
    row_count, rows, _ = d_qkv_ref.shape
    pick = chosen(tab_ref, clips, False)
    sums = []
    for r in range(row_count):
        unit, rate = norm_parts(dot(pick, jnp.concatenate([x_ref[r], halo_ref[r]], 0)))
        d_normed = dot_t(d_qkv_ref[r], w_ref[...])
        sums.append([jnp.sum(p, 0, keepdims=True) for p in (d_normed * unit, d_normed)])
        d_in = norm_back(d_normed * gain_ref[...], unit, rate).astype(jnp.bfloat16)
        back = dot(chosen(tab_ref, clips, True), d_in).astype(jnp.bfloat16)
        own_ref[r] = back[: clips.slots]
        edge_ref[r] = back[clips.slots :]
    for k in range(2):
        vec_ref[k : k + 1] = sum(s[k] for s in sums[1:]) + sums[0][k]


def first_back(clips, tab, d_qkv, weight, tokens, halo, gain):
    row_count, slots, width = tokens.shape
    args = (d_qkv, weight, tokens, halo, gain)
    shapes = [
        ((row_count, slots, width), jnp.bfloat16),
        ((row_count, clips.halo, width), jnp.bfloat16),
        ((2, width), jnp.float32),
    ]
    return pl.pallas_call(
        functools.partial(first_back_kernel, clips),
        grid_spec=pltpu.PrefetchScalarGridSpec(
            num_scalar_prefetch=1,
            grid=(1,),
            in_specs=[whole(*a.shape) for a in args],
            out_specs=[whole(*shape) for shape, _ in shapes],
        ),
        out_shape=[jax.ShapeDtypeStruct(*s) for s in shapes],
        compiler_params=pltpu.CompilerParams(vmem_limit_bytes=VMEM_LIMIT),
        name="first_back",
    )(tab, *args)


def moved(block, step):
    count = lax.axis_size("seq")
    return lax.ppermute(block, "seq", [(i, i + step) for i in range(count) if 0 <= i + step < count])


def on_device(
    tokens,
    segments,
    ln1_gain,
    ln1_bias,
    w_qkv,
    q_bias,
    v_bias,
    w_out,
    out_bias,
    ln2_gain,
    ln2_bias,
    w_up,
    up_bias,
    w_down,
    down_bias,
    cotangent,
):
    row_count, slot_count, width = tokens.shape
    seq_count, rows_count = lax.axis_size("seq"), lax.axis_size("rows")
    clips = Clips(slot_count, seq_count)
    route = Route(seq_count, rows_count)
    seq_at, row_at = lax.axis_index("seq"), lax.axis_index("rows")
    tab = jnp.asarray(route.table)[seq_at * rows_count + row_at]
    place = jnp.asarray(np.array(clips.shards, np.int32))[seq_at]
    six = (segments[:, clips.tail_at] >= 0) & (place[4] > 0)
    geo = jnp.concatenate([place[:4], jnp.reshape(row_at % 2, (1,)), jnp.where(six, CLIP, 0)])

    halo = moved(tokens[:, : clips.halo], -1)
    wide_bias = jnp.concatenate([q_bias, jnp.zeros_like(q_bias), v_bias])[None]
    qkv, normed, att, att_edge = attend(
        clips, geo, tokens, halo, ln1_gain[None], ln1_bias[None], w_qkv, wide_bias
    )
    att_in = moved(att_edge, 1)
    out, d_att, d_middle, mlp_send, mlp_keep, out_send, out_keep, vec_a, vec_up = mlp(
        clips, rows_count, seq_count, geo, tokens, att, att_in, cotangent, w_out, out_bias[None],
        ln2_gain[None], ln2_bias[None], w_up, up_bias[None], w_down, down_bias[None],
    )
    d_edge = moved(d_att[:, : clips.halo], -1)
    d_qkv, qkv_send, qkv_keep, vec_b = attend_back(
        clips, rows_count, seq_count, geo, qkv, normed, d_att, d_edge, out_send, out_keep
    )
    d_in, d_in_edge, vec_c = first_back(clips, geo, d_qkv, w_qkv, tokens, halo, ln1_gain[None])
    d_in_far = moved(d_in_edge, 1)
    d_total = d_middle + d_in.astype(jnp.float32)
    d_total = d_total.at[:, : clips.halo].add(d_in_far.astype(jnp.float32))

    vectors = jnp.concatenate([vec_a, vec_c, vec_b.reshape(3, width), vec_up.reshape(-1, width)], 0)
    vectors = sum_everywhere(route, vectors)
    sums_mlp = scatter_sum(route, tab, mlp_send, mlp_keep)
    sums_qkv = scatter_sum(route, tab, qkv_send, qkv_keep)
    cut = 3 * width // seq_count
    return (
        out,
        d_total.astype(jnp.bfloat16),
        vectors[4],
        vectors[5],
        sums_qkv[:, :cut],
        vectors[6],
        vectors[8],
        sums_qkv[:, cut:],
        vectors[0],
        vectors[1],
        vectors[2],
        sums_mlp[:, :UNIT],
        vectors[9:].reshape(-1),
        sums_mlp[:, UNIT:].T,
        vectors[3],
    )


def solution(mesh):
    placed = (
        P("rows", "seq", None),
        P("rows", "seq"),
        P(),
        P(),
        P(),
        P(),
        P(),
        P(),
        P(),
        P(),
        P(),
        P(),
        P(),
        P(),
        P(),
        P("rows", "seq", None),
    )
    return jax.shard_map(
        on_device,
        mesh=mesh,
        in_specs=placed,
        out_specs=(
            P("rows", "seq", None),
            P("rows", "seq", None),
            P(),
            P(),
            P("rows", "seq"),
            P(),
            P(),
            P("rows", "seq"),
            P(),
            P(),
            P(),
            P("rows", "seq"),
            P(),
            P("seq", "rows"),
            P(),
        ),
        check_vma=False,
    )
```

```python
import functools

import jax
import jax.numpy as jnp
import numpy as np
from jax import lax
from jax.experimental import pallas as pl
from jax.experimental.pallas import tpu as pltpu
from jax.sharding import PartitionSpec as P

HEAD_DIM = 64
CLIP = 157
UNIT = 768


def bit_orders(count, offset):
    bits = max(count.bit_length() - 1, 0)
    free = list(range(offset, bits))
    return free, free[::-1]


class Route:
    def __init__(self, seq_count, rows_count, shards):
        self.seq_count, self.rows_count = seq_count, rows_count
        plain, turned = bit_orders(rows_count, 1)
        self.row_bits = [[0] + plain, [0] + turned]
        self.col_bits = list(bit_orders(seq_count, 0))
        self.row_stages = len(plain)
        self.col_stages = len(self.col_bits[0])
        self.places = {}
        self.table = np.array(
            [self.one_device(s, r, first) for s, first in enumerate(shards) for r in range(rows_count)],
            np.int32,
        )

    def halves(self, r):
        bit = self.row_bits[r & 1][1]
        ours = [b for b in range(self.rows_count) if not (b ^ r) & 1]
        return [b for b in ours if (b ^ r) >> bit & 1], [b for b in ours if not (b ^ r) >> bit & 1]

    def one_device(self, s, r, shard):
        core, places = r & 1, self.places
        row = [*shard, core]
        spots = sum(self.halves(r ^ 1), []) + sorted(sum(self.halves(r), []))
        places["block"] = len(row)
        row += spots
        own = sorted(sum(self.halves(r), []))
        sent, kept = self.halves(r)
        places["row", 0] = [len(row), len(row) + len(sent)]
        row += [own.index(b) for b in sent] + list(range(len(sent)))
        lists = [own, kept, kept]
        for t, bit in enumerate(self.row_bits[core][2:], 1):
            send = [b for b in kept if (b ^ r) >> bit & 1]
            kept = [b for b in kept if not (b ^ r) >> bit & 1]
            places["row", t] = []
            for origin in lists:
                places["row", t].append(len(row))
                row += [origin.index(b) for b in send]
            lists.append(kept)
        places["own"] = []
        for origin in lists[:-1]:
            places["own"].append(len(row))
            row.append(origin.index(r))
        kept, lists = list(range(self.seq_count)), [list(range(self.seq_count))]
        for t, bit in enumerate(self.col_bits[core]):
            send = [b for b in kept if (b ^ s) >> bit & 1]
            kept = [b for b in kept if not (b ^ s) >> bit & 1]
            places["col", t] = []
            for origin in lists:
                places["col", t].append(len(row))
                row += [origin.index(b) for b in send]
            lists.append(kept)
        places["end"] = []
        for origin in lists:
            places["end"].append(len(row))
            row.append(origin.index(s))
        return row

    def pairs(self, kind, t):
        out = []
        for s in range(self.seq_count):
            for r in range(self.rows_count):
                if kind == "row":
                    to = s * self.rows_count + (r ^ (1 << self.row_bits[r & 1][t]))
                else:
                    to = (s ^ (1 << self.col_bits[r & 1][t])) * self.rows_count + r
                out.append((s * self.rows_count + r, to))
        return out


def add_up(pieces):
    total = pieces[0].astype(jnp.float32)
    for piece in pieces[1:]:
        total = total + piece.astype(jnp.float32)
    return total


def in_vmem():
    return pl.BlockSpec(memory_space=pltpu.VMEM)


def in_smem():
    return pl.BlockSpec(memory_space=pltpu.SMEM)


def vmem_call(kernel, name, flags, args, shapes, scratch, flops, mega, far=()):
    return pl.pallas_call(
        kernel,
        in_specs=[in_smem()] * len(flags) + [in_vmem()] * len(args),
        out_specs=[in_vmem()] * len(shapes) + [pl.BlockSpec(memory_space=pltpu.HBM)] * len(far),
        out_shape=[jax.ShapeDtypeStruct(*s) for s in shapes] + [pltpu.HBM(*s) for s in far],
        scratch_shapes=scratch,
        compiler_params=pltpu.CompilerParams(vmem_limit_bytes=mega << 20),
        cost_estimate=pl.CostEstimate(flops=flops, bytes_accessed=1 << 20, transcendentals=0),
        name=name,
    )(*flags, *args)


def row_kernel(route, t, last, sources, tab_ref, *refs):
    source_refs, rider_refs, out_refs = refs[:sources], refs[sources : len(refs) - 1 - last], refs[len(refs) - 1 - last :]
    if rider_refs:
        rider_refs, out_refs = refs[sources : sources + 2], refs[sources + 2 :]
        out_refs[-1][...] = rider_refs[0][...] + rider_refs[1][...]
    for j in range(out_refs[0].shape[0]):
        pieces = [ref[tab_ref[base + j]] for base, ref in zip(route.places["row", t], source_refs)]
        out_refs[0][j] = add_up(pieces).astype(jnp.bfloat16)
    if last:
        out_refs[1][...] = add_up([ref[tab_ref[base]] for base, ref in zip(route.places["own"], source_refs)])


def stage_call(kernel, name, tab, sources, riders, shapes):
    shapes = shapes + [(rider.shape, rider.dtype) for rider in riders[:1]]
    return vmem_call(kernel, name, (tab,), [*sources, *riders], shapes, [], 10**9, 8)


def row_sum(route, tab, t, sources, riders):
    _, rows, width = sources[0].shape
    last = t == route.row_stages - 1
    shapes = [((route.rows_count >> (t + 2), rows, width), jnp.bfloat16)]
    if last:
        shapes.append(((rows, width), jnp.float32))
    kernel = functools.partial(row_kernel, route, t, last, len(sources))
    return stage_call(kernel, "row_sum", tab, sources, riders, shapes)


def col_pieces(route, key, j, chunk, tab_ref, refs):
    pieces = []
    for u, ref in enumerate(refs):
        at = tab_ref[route.places[key][max(u - 1, 0)] + j] * chunk
        pieces.append(ref[:, pl.ds(pl.multiple_of(at, 128), chunk)])
    return add_up(pieces)


def col_kernel(route, t, chunk, count, sources, tab_ref, *refs):
    source_refs, out_refs = refs[:sources], refs[sources:]
    if len(out_refs) > 1:
        first, second, *out_refs = out_refs
        out_refs[-1][...] = first[...] + second[...]
    for j in range(count):
        made = col_pieces(route, ("col", t), j, chunk, tab_ref, source_refs)
        out_refs[0][:, j * chunk : (j + 1) * chunk] = made.astype(jnp.bfloat16)


def col_sum(route, tab, t, sources, riders):
    rows, width = sources[0].shape
    chunk = width // route.seq_count
    count = route.seq_count >> (t + 1)
    kernel = functools.partial(col_kernel, route, t, chunk, count, len(sources))
    return stage_call(kernel, "col_sum", tab, sources, riders, [((rows, count * chunk), jnp.bfloat16)])


def end_kernel(route, chunk, cut, sources, tab_ref, *refs):
    source_refs, out_refs = refs[:sources], refs[sources:]
    if len(out_refs) > 2:
        first, second, *out_refs = out_refs
        out_refs[-1][...] = first[...] + second[...]
    total = col_pieces(route, "end", 0, chunk, tab_ref, source_refs)
    out_refs[0][...] = total[:, :cut]
    out_refs[1][...] = total[:, cut:]


def end_sum(route, tab, sources, riders, cut):
    rows, width = sources[0].shape
    chunk = width // route.seq_count
    shapes = [((rows, cut), jnp.float32), ((rows, chunk - cut), jnp.float32)]
    kernel = functools.partial(end_kernel, route, chunk, cut, len(sources))
    return stage_call(kernel, "end_sum", tab, sources, riders, shapes)


def after(values, *others):
    values = tuple(values)
    return list(lax.optimization_barrier((*values, *others))[: len(values)])


class Scatter:
    def __init__(self, route, tab, now, later, keep):
        self.route, self.tab = route, tab
        self.first = [keep, self.swap(now, "row", 0)]
        self.rest, self.rows, self.riders = later, [keep], []

    def swap(self, send, kind, t):
        return lax.ppermute(send, ("seq", "rows"), self.route.pairs(kind, t))

    def swap_rest(self, *others):
        (rest,) = after([self.rest], *others)
        self.rows = self.rows + [self.swap(rest, "row", 0)]

    def take_on(self, rider):
        self.riders = [rider, self.swap(rider, "row", 0)]

    def sent(self, made, kind, t):
        if self.riders:
            *made, rider = made
            self.riders = [rider, self.swap(rider, kind, t)]
        return [made[0], self.swap(made[0], kind, t), *made[1:]]

    def row_step(self, t, *others):
        sources = after(self.first if t == 0 else self.rows, *others)
        made = row_sum(self.route, self.tab, t, sources, self.riders)
        send, got, *base = self.sent(made, "row", t + 1)
        self.rows = self.rows + [got]
        if base:
            self.cols = [base[0], got[0]]
        return send

    def col_step(self, t, *others):
        made = col_sum(self.route, self.tab, t, after(self.cols, *others), self.riders)
        send, got = self.sent(made, "col", t)
        self.cols = self.cols + [got]
        return send

    def end(self, cut, *others):
        return end_sum(self.route, self.tab, after(self.cols, *others), self.riders, cut)


def dot(left, right):
    return lax.dot_general(left, right, (((1,), (0,)), ((), ())), preferred_element_type=jnp.float32)


def dot_t(left, right):
    return lax.dot_general(left, right, (((1,), (1,)), ((), ())), preferred_element_type=jnp.float32)


def t_dot(left, right):
    return lax.dot_general(left, right, (((0,), (0,)), ((), ())), preferred_element_type=jnp.float32)


def up_to(value, step):
    return -(-value // step) * step


class Clips:
    def __init__(self, slot_count, seq_count):
        self.slots = slot_count
        length = slot_count * seq_count
        sure = length // CLIP - 1
        spans = [(k * CLIP, CLIP, 0) for k in range(sure)] + [(sure * CLIP, length - sure * CLIP, 1)]
        held = [[] for _ in range(seq_count)]
        self.before, self.behind = [], []
        low = high = 0
        for at, count, tail in spans:
            shares = [
                min(at + count, (s + 1) * slot_count) - max(at, s * slot_count) for s in range(seq_count)
            ]
            owner = max(range(seq_count), key=lambda s: shares[s])
            held[owner].append((at - owner * slot_count, count, tail))
            for s, share in enumerate(shares):
                if share > 0 and s != owner:
                    assert abs(s - owner) == 1 and not tail
                    (self.before if s < owner else self.behind).append((s, owner))
                    low, high = max(low, share * (s < owner)), max(high, share * (s > owner))
        self.low, self.high = up_to(low, 16), up_to(high, 16)
        self.window = self.low + slot_count + self.high
        self.a_rows = up_to(CLIP, 16)
        self.b_rows = up_to(max(CLIP, length - sure * CLIP), 16)
        self.rows = self.a_rows + self.b_rows
        self.tail_at = sure * CLIP % slot_count
        self.shards = []
        for spots in held:
            first = [spot for spot in spots if not spot[2]]
            last = [spot for spot in spots if spot[2]]
            assert len(first) + len(last) < 3
            blocks = (first[:1] or [(0, 0, 0)]) + (first[1:] + last or [(0, 0, 0)])
            self.shards.append([v for at, count, _ in blocks for v in (at + self.low, count)] + [len(last)])

    def brought(self, lows, highs):
        return lax.ppermute(lows, "seq", self.before), lax.ppermute(highs, "seq", self.behind)

    def returned(self, lows, highs):
        return (
            lax.ppermute(lows, "seq", [(owner, s) for s, owner in self.before]),
            lax.ppermute(highs, "seq", [(owner, s) for s, owner in self.behind]),
        )


TAIL_AT = 4


def chosen(tab_ref, clips, turned):
    a_at, a_len, b_at, b_len = (tab_ref[k] for k in range(4))
    if turned:
        shape, row_dim = (clips.window, clips.rows), 1
    else:
        shape, row_dim = (clips.rows, clips.window), 0
    row = lax.broadcasted_iota(jnp.int32, shape, row_dim)
    slot = lax.broadcasted_iota(jnp.int32, shape, 1 - row_dim)
    in_a = (row < a_len) & (slot == row + a_at)
    second = row - clips.a_rows
    in_b = (second >= 0) & (second < b_len) & (slot == second + b_at)
    return jnp.where(in_a | in_b, 1.0, 0.0).astype(jnp.bfloat16)


def block_masks(tab_ref, seg_ref, clips, row, key_dim):
    shape_a = (1, clips.a_rows) if key_dim == 1 else (clips.a_rows, 1)
    key_a = lax.broadcasted_iota(jnp.int32, shape_a, key_dim)
    mask_a = jnp.where(key_a < CLIP, 0.0, -1e30)
    shape_b = (clips.b_rows, clips.b_rows)
    key_b = lax.broadcasted_iota(jnp.int32, shape_b, key_dim)
    query_b = lax.broadcasted_iota(jnp.int32, shape_b, 1 - key_dim)
    six = (tab_ref[TAIL_AT] > 0) & (seg_ref[row, clips.tail_at] >= 0)
    split, b_len = jnp.where(six, CLIP, 0), jnp.maximum(tab_ref[3], 1)
    fits = (key_b < b_len) & ((key_b < split) == (query_b < split))
    mask_b = jnp.where(fits, 0.0, -1e30)
    return mask_a, mask_b


def window_of(low_ref, own_ref, high_ref, r):
    return jnp.concatenate([low_ref[r], own_ref[r], high_ref[r]], 0)


def put_window(clips, values, low_ref, own_ref, high_ref, r):
    low_ref[r] = values[: clips.low]
    own_ref[r] = values[clips.low : clips.low + clips.slots]
    high_ref[r] = values[clips.low + clips.slots :]


def norm_parts(values):
    center = values - jnp.mean(values, -1, keepdims=True)
    spread = jnp.mean(center * center, -1, keepdims=True)
    rate = lax.rsqrt(spread + 1e-06)
    return center * rate, rate


def norm_back(d_unit, unit, rate):
    return rate * (
        d_unit
        - jnp.mean(d_unit, -1, keepdims=True)
        - unit * jnp.mean(d_unit * unit, -1, keepdims=True)
    )


def split_heads(pair):
    low = lax.broadcasted_iota(jnp.int32, pair.shape, 1) < HEAD_DIM
    zero = jnp.zeros_like(pair)
    return jnp.concatenate([jnp.where(low, pair, zero), jnp.where(low, zero, pair)], 0)


def join_heads(both):
    half = both.shape[0] // 2
    low = lax.broadcasted_iota(jnp.int32, (half, both.shape[1]), 1) < HEAD_DIM
    return jnp.where(low, both[:half], both[half:])


def window_shapes(clips, row_count, width):
    return [((row_count, n, width), jnp.bfloat16) for n in (clips.low, clips.slots, clips.high)]


def cot_kernel(cot_ref, w_down_ref, d_active_ref, total_ref):
    cot = cot_ref[...].reshape(-1, cot_ref.shape[-1])
    total_ref[...] = jnp.sum(cot.astype(jnp.float32), 0, keepdims=True)
    steps, _, chunk = d_active_ref.shape
    for f in range(steps):
        d_active_ref[f] = dot_t(cot, w_down_ref[f * chunk : (f + 1) * chunk]).astype(jnp.bfloat16)


def cot_back(steps, cot, w_down):
    count, width = cot.shape[0] * cot.shape[1], cot.shape[2]
    shapes = [((steps, count, w_down.shape[0] // steps), jnp.bfloat16), ((1, width), jnp.float32)]
    return vmem_call(cot_kernel, "cot_back", (), (cot, w_down), shapes, [], 3 * 10**9, 12)


def attend_kernel(
    clips, tab_ref, seg_ref, low_ref, x_ref, high_ref, par_ref, w_ref,
    own_low_ref, own_ref, own_high_ref, qkv_out_ref, normed_out_ref, qkv_ref, normed_ref, att_ref, sems,
):
    row_count, _, width = x_ref.shape
    pick, turned = chosen(tab_ref, clips, False), chosen(tab_ref, clips, True)
    for r in range(row_count):
        unit, _ = norm_parts(dot(pick, window_of(low_ref, x_ref, high_ref, r)))
        normed_ref[r] = (unit * par_ref[0:1] + par_ref[1:2]).astype(jnp.bfloat16)
    normed_copy = pltpu.make_async_copy(normed_ref, normed_out_ref, sems.at[row_count])
    normed_copy.start()

    def one_row(r, carry):
        for part in range(3):
            cols = slice(part * width, (part + 1) * width)
            made = dot(normed_ref[r], w_ref[:, cols])
            if part != 1:
                made = made + par_ref[2 + part // 2 : 3 + part // 2]
            if part == 0:
                made = made * HEAD_DIM ** (-0.5)
            qkv_ref[r, :, cols] = made.astype(jnp.bfloat16)
        pltpu.make_async_copy(qkv_ref.at[r], qkv_out_ref.at[r], sems.at[r]).start()
        masks = block_masks(tab_ref, seg_ref, clips, r, 1)
        for base, count, mask in ((0, clips.a_rows, masks[0]), (clips.a_rows, clips.b_rows, masks[1])):
            here = slice(base, base + count)
            if mask.shape[0] > 1:
                mask = jnp.concatenate([mask, mask], 0)
            for p in range(width // 128):
                query, key, value = (
                    qkv_ref[r, here, k * width + p * 128 : k * width + (p + 1) * 128] for k in range(3)
                )
                scores = dot_t(split_heads(query), key) + mask
                peak = jnp.max(scores, -1, keepdims=True)
                weights = jnp.exp(scores - peak)
                total = jnp.sum(weights, -1, keepdims=True)
                mixed = dot(weights.astype(jnp.bfloat16), value) / total
                att_ref[here, p * 128 : (p + 1) * 128] = join_heads(mixed).astype(jnp.bfloat16)
        back = dot(turned, att_ref[...]).astype(jnp.bfloat16)
        put_window(clips, back, own_low_ref, own_ref, own_high_ref, r)
        return carry

    lax.fori_loop(0, row_count, one_row, 0)
    normed_copy.wait()
    for r in range(row_count):
        pltpu.make_async_copy(qkv_ref.at[r], qkv_out_ref.at[r], sems.at[r]).wait()


def attend(clips, tab, seg, *args):
    row_count, _, width = args[1].shape
    shapes = window_shapes(clips, row_count, width)
    far = [
        ((row_count, clips.rows, 3 * width), jnp.bfloat16),
        ((row_count, clips.rows, width), jnp.bfloat16),
    ]
    scratch = [pltpu.VMEM(*s) for s in far] + [
        pltpu.VMEM((clips.rows, width), jnp.bfloat16),
        pltpu.SemaphoreType.DMA((row_count + 1,)),
    ]
    kernel = functools.partial(attend_kernel, clips)
    return vmem_call(kernel, "attend", (tab, seg), args, shapes, scratch, 8 * 10**9, 20, far)


def gelu_parts(hidden):
    cdf = 0.5 + 0.5 * lax.erf(hidden * 0.7071067811865476)
    return hidden * cdf, cdf + hidden * (0.3989422804014327 * jnp.exp(-0.5 * hidden * hidden))


def grad_shapes(route, width, cols):
    rows, half = width // route.rows_count, route.rows_count // 2
    return [((n, rows, cols), jnp.bfloat16) for n in (half // 2, half - half // 2, half)]


def hand_out(tab_ref, route, held_ref, refs, cols):
    spots = [(ref, k) for ref in refs for k in range(ref.shape[0])]
    for at, (ref, k) in enumerate(spots):
        ref[k, :, cols] = held_ref[tab_ref[route.places["block"] + at]]


def mlp_kernel(
    clips, route, tab_ref, x_ref, att_ref, first_ref, last_ref, cot_ref, w_out_ref, par_ref,
    w_up_ref, w_down_ref, d_active_ref,
    out_ref, middle_ref, att_sum_ref, d_hidden_ref, up_vec_ref, now_ref, later_ref, keep_ref,
    normed_s, result_s, held_s,
):
    row_count, slots, width = x_ref.shape
    steps, count, chunk = d_active_ref.shape
    rows = width // route.rows_count
    for r in range(row_count):
        att_sum_ref[r] = att_ref[r]
        att_sum_ref[r, : clips.high] += first_ref[r]
        att_sum_ref[r, slots - clips.low :] += last_ref[r]
    made = dot(att_sum_ref[...].reshape(count, width), w_out_ref[...])
    middle = x_ref[...].reshape(count, width).astype(jnp.float32) + made + par_ref[4:5]
    middle_ref[...] = middle
    unit, _ = norm_parts(middle)
    normed_s[...] = (unit * par_ref[5:6] + par_ref[6:7]).astype(jnp.bfloat16)
    cot = cot_ref[...].reshape(count, width)
    for f in range(steps):
        part = slice(f * chunk, (f + 1) * chunk)
        hidden = dot(normed_s[...], w_up_ref[:, part]) + par_ref[8 + f : 9 + f]
        active, slope = gelu_parts(hidden)
        active_b = active.astype(jnp.bfloat16)
        d_hidden = (d_active_ref[f].astype(jnp.float32) * slope).astype(jnp.bfloat16)
        d_hidden_ref[f] = d_hidden
        up_vec_ref[f : f + 1] = jnp.sum(d_hidden.astype(jnp.float32), 0, keepdims=True)
        grown = dot(active_b, w_down_ref[part])
        if f == 0:
            result_s[...] = grown
        elif f < steps - 1:
            result_s[...] += grown
        else:
            total = middle_ref[...] + par_ref[7:8] + result_s[...] + grown
            out_ref[...] = total.reshape(out_ref.shape).astype(jnp.bfloat16)
        for at, grad in ((0, t_dot(normed_s[...], d_hidden)), (chunk, t_dot(cot, active_b))):
            grad = grad.astype(jnp.bfloat16)
            for b in range(route.rows_count):
                held_s[b, :, at : at + chunk] = grad[b * rows : (b + 1) * rows]
        cols = slice(2 * f * chunk, 2 * (f + 1) * chunk)
        hand_out(tab_ref, route, held_s, (now_ref, later_ref, keep_ref), cols)


def mlp(clips, route, tab, *args):
    row_count, slots, width = args[0].shape
    steps, count, chunk = args[-1].shape
    bf16, f32 = jnp.bfloat16, jnp.float32
    shapes = [
        ((row_count, slots, width), bf16),
        ((count, width), f32),
        ((row_count, slots, width), bf16),
        ((steps, count, chunk), bf16),
        ((steps, chunk), f32),
        *grad_shapes(route, width, 2 * steps * chunk),
    ]
    scratch = [
        pltpu.VMEM((count, width), bf16),
        pltpu.VMEM((count, width), f32),
        pltpu.VMEM((route.rows_count, width // route.rows_count, 2 * chunk), bf16),
    ]
    kernel = functools.partial(mlp_kernel, clips, route)
    return vmem_call(kernel, "mlp", (tab,), args, shapes, scratch, 20 * 10**9, 28)


def mlp_back_kernel(
    clips, route, tab_ref, d_hidden_ref, w_up_ref, middle_ref, par_ref, cot_ref, w_out_ref, att_ref,
    d_low_ref, d_att_ref, d_high_ref, d_middle_ref, out_grad_ref, vec_ref,
):
    row_count, slots, width = cot_ref.shape
    steps, count, chunk = d_hidden_ref.shape
    d_normed = dot_t(d_hidden_ref[0], w_up_ref[:, :chunk])
    for f in range(1, steps):
        d_normed += dot_t(d_hidden_ref[f], w_up_ref[:, f * chunk : (f + 1) * chunk])
    unit, rate = norm_parts(middle_ref[...])
    vec_ref[1:2] = jnp.sum(d_normed * unit, 0, keepdims=True)
    vec_ref[2:3] = jnp.sum(d_normed, 0, keepdims=True)
    cot = cot_ref[...].reshape(count, width).astype(jnp.float32)
    total = cot + norm_back(d_normed * par_ref[5:6], unit, rate)
    d_middle_ref[...] = total.reshape(d_middle_ref.shape)
    branch = total.astype(jnp.bfloat16)
    vec_ref[0:1] = jnp.sum(branch.astype(jnp.float32), 0, keepdims=True)
    made = dot_t(branch, w_out_ref[...]).astype(jnp.bfloat16).reshape(row_count, slots, width)
    d_att_ref[...] = made
    d_low_ref[...] = made[:, slots - clips.low :]
    d_high_ref[...] = made[:, : clips.high]
    grad = t_dot(att_ref[...].reshape(count, width), branch).astype(jnp.bfloat16)
    rows = width // route.rows_count
    for b in range(route.rows_count):
        out_grad_ref[b] = grad[b * rows : (b + 1) * rows]


def mlp_back(clips, route, tab, *args):
    row_count, _, width = args[4].shape
    shapes = window_shapes(clips, row_count, width) + [
        (args[4].shape, jnp.float32),
        ((route.rows_count, width // route.rows_count, width), jnp.bfloat16),
        ((3, width), jnp.float32),
    ]
    kernel = functools.partial(mlp_back_kernel, clips, route)
    return vmem_call(kernel, "mlp_back", (tab,), args, shapes, [], 5 * 10**9, 16)


def attend_back_kernel(
    clips, route, tab_ref, seg_ref, qkv_ref, d_low_ref, d_att_ref, d_high_ref, normed_ref, out_grad_ref,
    d_qkv_ref, vec_ref, now_ref, later_ref, keep_ref, d_mixed_s, held_s,
):
    row_count, rows, width = normed_ref.shape
    scale = HEAD_DIM ** (-0.5)
    pick = chosen(tab_ref, clips, False)

    def one_row(r, total):
        d_mixed_s[...] = dot(pick, window_of(d_low_ref, d_att_ref, d_high_ref, r)).astype(jnp.bfloat16)
        masks = block_masks(tab_ref, seg_ref, clips, r, 0)
        for base, count, mask in ((0, clips.a_rows, masks[0]), (clips.a_rows, clips.b_rows, masks[1])):
            here = slice(base, base + count)
            if mask.shape[1] > 1:
                mask = jnp.concatenate([mask, mask], 1)
            for p in range(width // 128):
                cols = [slice(k * width + p * 128, k * width + (p + 1) * 128) for k in range(3)]
                query, key, value = (qkv_ref[r, here, c] for c in cols)
                queries = split_heads(query)
                d_mixed = split_heads(d_mixed_s[here, cols[0]])
                scores = dot_t(key, queries) + mask
                peak = jnp.max(scores, 0, keepdims=True)
                weights = jnp.exp(scores - peak)
                prob = weights * (1.0 / jnp.sum(weights, 0, keepdims=True))
                d_value = dot(prob.astype(jnp.bfloat16), d_mixed)
                d_prob = dot_t(value, d_mixed)
                centre = jnp.sum(d_prob * prob, 0, keepdims=True)
                d_scores = (prob * (d_prob - centre)).astype(jnp.bfloat16)
                d_key = dot(d_scores, queries)
                d_query = join_heads(t_dot(d_scores, key)) * scale
                for c, made in zip(cols, (d_query, d_key, d_value)):
                    d_qkv_ref[r, here, c] = made.astype(jnp.bfloat16)
        return total + jnp.sum(d_qkv_ref[r].astype(jnp.float32), 0, keepdims=True)

    total = lax.fori_loop(0, row_count, one_row, jnp.zeros((1, 3 * width), jnp.float32))
    for k in range(3):
        vec_ref[k : k + 1] = total[:, k * width : (k + 1) * width]
    flat = normed_ref[...].reshape(row_count * rows, width)
    cut, out_cut = 3 * width // route.seq_count, width // route.seq_count
    height = width // route.rows_count
    for s in range(route.seq_count):
        d_part = d_qkv_ref[:, :, s * cut : (s + 1) * cut].reshape(row_count * rows, cut)
        made = t_dot(flat, d_part).astype(jnp.bfloat16)
        for b in range(route.rows_count):
            rest = out_grad_ref[b, :, s * out_cut : (s + 1) * out_cut]
            held_s[b] = jnp.concatenate([made[b * height : (b + 1) * height], rest], 1)
        hand_out(tab_ref, route, held_s, (now_ref, later_ref, keep_ref), slice(s * UNIT, (s + 1) * UNIT))


def attend_back(clips, route, tab, seg, *args):
    row_count, rows, width = args[4].shape
    shapes = [
        ((row_count, rows, 3 * width), jnp.bfloat16),
        ((3, width), jnp.float32),
        *grad_shapes(route, width, route.seq_count * UNIT),
    ]
    scratch = [
        pltpu.VMEM((rows, width), jnp.bfloat16),
        pltpu.VMEM((route.rows_count, width // route.rows_count, UNIT), jnp.bfloat16),
    ]
    kernel = functools.partial(attend_back_kernel, clips, route)
    return vmem_call(kernel, "attend_back", (tab, seg), args, shapes, scratch, 20 * 10**9, 14)


def first_back_kernel(
    clips, tab_ref, low_ref, x_ref, high_ref, par_ref, d_qkv_ref, w_ref, *refs
):
    vec_refs, (own_low_ref, own_ref, own_high_ref, vec_ref) = refs[:-4], refs[-4:]
    pick, turned = chosen(tab_ref, clips, False), chosen(tab_ref, clips, True)
    sums = []
    for r in range(x_ref.shape[0]):
        unit, rate = norm_parts(dot(pick, window_of(low_ref, x_ref, high_ref, r)))
        d_normed = dot_t(d_qkv_ref[r], w_ref[...])
        sums.append([jnp.sum(p, 0, keepdims=True) for p in (d_normed * unit, d_normed)])
        d_in = norm_back(d_normed * par_ref[0:1], unit, rate).astype(jnp.bfloat16)
        back = dot(turned, d_in).astype(jnp.bfloat16)
        put_window(clips, back, own_low_ref, own_ref, own_high_ref, r)
    for k in range(2):
        vec_ref[k : k + 1] = sum(s[k] for s in sums[1:]) + sums[0][k]
    at = 2
    for ref in vec_refs:
        vec_ref[at : at + ref.shape[0]] = ref[...]
        at += ref.shape[0]


def first_back(clips, tab, *args):
    row_count, _, width = args[1].shape
    count = 2 + sum(a.shape[0] for a in args[6:])
    shapes = window_shapes(clips, row_count, width) + [((count, width), jnp.float32)]
    kernel = functools.partial(first_back_kernel, clips)
    return vmem_call(kernel, "first_back", (tab,), args, shapes, [], 8 * 10**9, 14)


def finish_kernel(clips, d_middle_ref, own_ref, first_ref, last_ref, out_ref):
    for r in range(own_ref.shape[0]):
        total = d_middle_ref[r] + own_ref[r].astype(jnp.float32)
        tail = clips.slots - clips.low
        first = total[: clips.high] + first_ref[r].astype(jnp.float32)
        last = total[tail:] + last_ref[r].astype(jnp.float32)
        out_ref[r] = jnp.concatenate([first, total[clips.high : tail], last], 0).astype(jnp.bfloat16)


def finish(clips, *args):
    shapes = [(args[1].shape, jnp.bfloat16)]
    return vmem_call(functools.partial(finish_kernel, clips), "finish", (), args, shapes, [], 10**9, 8)[0]


def on_device(
    tokens,
    segments,
    ln1_gain,
    ln1_bias,
    w_qkv,
    q_bias,
    v_bias,
    w_out,
    out_bias,
    ln2_gain,
    ln2_bias,
    w_up,
    up_bias,
    w_down,
    down_bias,
    cotangent,
):
    row_count, slot_count, width = tokens.shape
    seq_count, rows_count = lax.axis_size("seq"), lax.axis_size("rows")
    clips = Clips(slot_count, seq_count)
    route = Route(seq_count, rows_count, clips.shards)
    low, high = clips.brought(tokens[:, slot_count - clips.low :], tokens[:, : clips.high])
    tab = jnp.asarray(route.table)[lax.axis_index("seq") * rows_count + lax.axis_index("rows")]
    total, at = 8 * width + up_bias.shape[0], 0
    params = jnp.zeros((total,), jnp.float32)
    for vector in (ln1_gain, ln1_bias, q_bias, v_bias, out_bias, ln2_gain, ln2_bias, down_bias, up_bias):
        params = params + lax.pad(vector, 0.0, [(at, total - at - vector.shape[0], 0)])
        at += vector.shape[0]
    params = params.reshape(-1, width)
    cot = cotangent
    d_active, vec_cot = cot_back(seq_count, cot, w_down)
    low, high = after((low, high), d_active)
    att_low, att, att_high, qkv, normed = attend(clips, tab, segments, low, tokens, high, params, w_qkv)
    att_last, att_first = clips.returned(att_low, att_high)
    out, middle, att, d_hidden, vec_up, *mlp_grad = mlp(
        clips, route, tab, tokens, att, att_first, att_last, cot, w_out, params, w_up, w_down, d_active
    )
    sum_a = Scatter(route, tab, *mlp_grad)
    sent = sum_a.row_step(0)
    (d_hidden,) = after([d_hidden], sent)
    d_low, d_att, d_high, d_middle, out_grad, vec_mid = mlp_back(
        clips, route, tab, d_hidden, w_up, middle, params, cot, w_out, att
    )
    d_low, d_high = clips.brought(d_low, d_high)
    sum_a.swap_rest(d_att)
    d_qkv, vec_qkv, *qkv_grad = attend_back(
        clips, route, tab, segments, qkv, d_low, d_att, d_high, normed, out_grad
    )
    sum_b = Scatter(route, tab, *qkv_grad)
    sent = sum_a.row_step(1, d_qkv)
    (d_qkv,) = after([d_qkv], sent)
    d_in_low, d_in, d_in_high, vectors = first_back(
        clips, tab, low, tokens, high, params, d_qkv, w_qkv, vec_mid, vec_cot, vec_qkv, vec_up
    )
    sum_b.take_on(vectors)
    sum_b.swap_rest(d_in)
    d_in_last, d_in_first = clips.returned(d_in_low, d_in_high)
    sent = sum_b.row_step(0, d_in)
    (d_middle,) = after([d_middle], sent)
    grad_tokens = finish(clips, d_middle, d_in, d_in_first, d_in_last)
    for t in range(2, route.row_stages):
        sum_a.row_step(t)
    for t in range(1, route.row_stages):
        sum_b.row_step(t, grad_tokens)
    for t in range(route.col_stages):
        sum_a.col_step(t)
        sum_b.col_step(t)
    sum_up, sum_down = sum_a.end(UNIT)
    sum_qkv, sum_out, vectors = sum_b.end(3 * width // seq_count)
    return (
        out,
        grad_tokens,
        vectors[0],
        vectors[1],
        sum_qkv,
        vectors[6],
        vectors[8],
        sum_out,
        vectors[2],
        vectors[3],
        vectors[4],
        sum_up,
        vectors[9:].reshape(-1),
        sum_down.T,
        vectors[5],
    )


def solution(mesh):
    placed = (
        P("rows", "seq", None),
        P("rows", "seq"),
        P(),
        P(),
        P(),
        P(),
        P(),
        P(),
        P(),
        P(),
        P(),
        P(),
        P(),
        P(),
        P(),
        P("rows", "seq", None),
    )
    return jax.shard_map(
        on_device,
        mesh=mesh,
        in_specs=placed,
        out_specs=(
            P("rows", "seq", None),
            P("rows", "seq", None),
            P(),
            P(),
            P("rows", "seq"),
            P(),
            P(),
            P("rows", "seq"),
            P(),
            P(),
            P(),
            P("rows", "seq"),
            P(),
            P("seq", "rows"),
            P(),
        ),
        check_vma=False,
    )
```

```python
import functools

import jax
import jax.numpy as jnp
import numpy as np
from jax import lax
from jax.experimental import pallas as pl
from jax.experimental.pallas import tpu as pltpu
from jax.sharding import PartitionSpec as P

HEAD_DIM = 64
CLIP = 157
UNIT = 768


def bit_orders(count, offset):
    bits = max(count.bit_length() - 1, 0)
    free = list(range(offset, bits))
    return free, free[::-1]


class Route:
    def __init__(self, seq_count, rows_count, shards):
        self.seq_count, self.rows_count = seq_count, rows_count
        plain, turned = bit_orders(rows_count, 1)
        self.row_bits = [[0] + plain, [0] + turned]
        self.col_bits = list(bit_orders(seq_count, 0))
        self.row_stages = len(plain)
        self.col_stages = len(self.col_bits[0])
        self.places = {}
        self.table = np.array(
            [self.one_device(s, r, first) for s, first in enumerate(shards) for r in range(rows_count)],
            np.int32,
        )

    def halves(self, r):
        bit = self.row_bits[r & 1][1]
        ours = [b for b in range(self.rows_count) if not (b ^ r) & 1]
        return [b for b in ours if (b ^ r) >> bit & 1], [b for b in ours if not (b ^ r) >> bit & 1]

    def one_device(self, s, r, shard):
        core, places = r & 1, self.places
        row = [*shard, core]
        spots = sum(self.halves(r ^ 1), []) + sorted(sum(self.halves(r), []))
        places["block"] = len(row)
        row += spots
        own = sorted(sum(self.halves(r), []))
        sent, kept = self.halves(r)
        places["row", 0] = [len(row), len(row) + len(sent)]
        row += [own.index(b) for b in sent] + list(range(len(sent)))
        lists = [own, kept, kept]
        for t, bit in enumerate(self.row_bits[core][2:], 1):
            send = [b for b in kept if (b ^ r) >> bit & 1]
            kept = [b for b in kept if not (b ^ r) >> bit & 1]
            places["row", t] = []
            for origin in lists:
                places["row", t].append(len(row))
                row += [origin.index(b) for b in send]
            lists.append(kept)
        places["own"] = []
        for origin in lists[:-1]:
            places["own"].append(len(row))
            row.append(origin.index(r))
        kept, lists = list(range(self.seq_count)), [list(range(self.seq_count))]
        for t, bit in enumerate(self.col_bits[core]):
            send = [b for b in kept if (b ^ s) >> bit & 1]
            kept = [b for b in kept if not (b ^ s) >> bit & 1]
            places["col", t] = []
            for origin in lists:
                places["col", t].append(len(row))
                row += [origin.index(b) for b in send]
            lists.append(kept)
        places["end"] = []
        for origin in lists:
            places["end"].append(len(row))
            row.append(origin.index(s))
        return row

    def pairs(self, kind, t):
        out = []
        for s in range(self.seq_count):
            for r in range(self.rows_count):
                if kind == "row":
                    to = s * self.rows_count + (r ^ (1 << self.row_bits[r & 1][t]))
                else:
                    to = (s ^ (1 << self.col_bits[r & 1][t])) * self.rows_count + r
                out.append((s * self.rows_count + r, to))
        return out


def add_up(pieces):
    total = pieces[0].astype(jnp.float32)
    for piece in pieces[1:]:
        total = total + piece.astype(jnp.float32)
    return total


def in_vmem():
    return pl.BlockSpec(memory_space=pltpu.VMEM)


def in_smem():
    return pl.BlockSpec(memory_space=pltpu.SMEM)


def vmem_call(kernel, name, flags, args, shapes, scratch, flops, mega, far=(), marks=()):
    head, skip = len(flags) + len(args), len(marks)

    def without_marks(*refs):
        kernel(*refs[:head], *refs[head + skip :])

    return pl.pallas_call(
        without_marks,
        in_specs=[in_smem()] * len(flags) + [in_vmem()] * (len(args) + skip),
        out_specs=[in_vmem()] * len(shapes) + [pl.BlockSpec(memory_space=pltpu.HBM)] * len(far),
        out_shape=[jax.ShapeDtypeStruct(*s) for s in shapes] + [pltpu.HBM(*s) for s in far],
        scratch_shapes=scratch,
        compiler_params=pltpu.CompilerParams(vmem_limit_bytes=mega << 20),
        cost_estimate=pl.CostEstimate(flops=flops, bytes_accessed=1 << 10, transcendentals=0),
        name=name,
    )(*flags, *args, *marks)


MARK = ((8, 128), jnp.float32)


def in_strips(rows, step):
    if rows % 16:
        step(slice(None))
        return

    def one(i, carry):
        step(pl.ds(pl.multiple_of(i * 16, 16), 16))
        return carry

    lax.fori_loop(0, rows // 16, one, 0)


def ride(out_refs, rider_refs):
    if rider_refs:
        out_refs[-1][...] = rider_refs[0][...] + rider_refs[1][...]
    else:
        out_refs[-1][...] = jnp.zeros_like(out_refs[-1])


def by_shards(values, widths, count):
    if len(widths) < 2:
        return values
    pieces = []
    for s in range(count):
        at = 0
        for wide in widths:
            part = wide // count
            pieces.append(values[:, at + s * part : at + (s + 1) * part])
            at += wide
    return jnp.concatenate(pieces, 1)


def row_kernel(route, t, widths, sources, riders, tab_ref, *refs):
    source_refs, rider_refs, out_refs = refs[:sources], refs[sources : sources + riders], refs[sources + riders :]
    ride(out_refs, rider_refs)

    def step(strip):
        for j in range(out_refs[0].shape[0]):
            pieces = [ref[tab_ref[base + j], strip] for base, ref in zip(route.places["row", t], source_refs)]
            total = add_up(pieces)
            if len(out_refs) > 2:
                total = by_shards(total, widths, route.seq_count)
            out_refs[0][j, strip] = total.astype(jnp.bfloat16)
        if len(out_refs) > 2:
            bases = zip(route.places["own"], source_refs)
            total = add_up([ref[tab_ref[base], strip] for base, ref in bases])
            out_refs[1][strip] = by_shards(total, widths, route.seq_count)

    in_strips(out_refs[0].shape[1], step)


def col_pieces(route, key, j, chunk, tab_ref, refs, strip):
    pieces = []
    for u, ref in enumerate(refs):
        at = tab_ref[route.places[key][max(u - 1, 0)] + j] * chunk
        pieces.append(ref[strip, pl.ds(pl.multiple_of(at, 128), chunk)])
    return add_up(pieces)


def col_kernel(route, t, chunk, count, sources, riders, tab_ref, *refs):
    source_refs, rider_refs, out_refs = refs[:sources], refs[sources : sources + riders], refs[sources + riders :]
    ride(out_refs, rider_refs)

    def step(strip):
        for j in range(count):
            made = col_pieces(route, ("col", t), j, chunk, tab_ref, source_refs, strip)
            out_refs[0][strip, j * chunk : (j + 1) * chunk] = made.astype(jnp.bfloat16)

    in_strips(out_refs[0].shape[0], step)


def end_kernel(route, chunk, cut, sources, riders, tab_ref, *refs):
    source_refs, rider_refs, out_refs = refs[:sources], refs[sources : sources + riders], refs[sources + riders :]
    ride(out_refs, rider_refs)

    def step(strip):
        total = col_pieces(route, "end", 0, chunk, tab_ref, source_refs, strip)
        out_refs[0][strip] = total[:, :cut]
        out_refs[1][strip] = total[:, cut:]

    in_strips(out_refs[0].shape[0], step)


def passed(route, mark):
    return lax.ppermute(mark, ("seq", "rows"), route.pairs("row", 0))


class Scatter:
    def __init__(self, route, tab, widths, now, later, keep):
        self.route, self.tab, self.widths, self.riders = route, tab, widths, []
        self.first = [keep, self.swap(now, "row", 0)]
        self.rows = [keep, self.swap(later, "row", 0)]
        self.cols = []

    def swap(self, send, kind, t):
        return lax.ppermute(send, ("seq", "rows"), self.route.pairs(kind, t))

    def take_on(self, rider):
        self.riders = [rider, self.swap(rider, "row", 0)]

    def call(self, kernel, name, sources, shapes, marks, carried=()):
        last = (self.riders[0].shape, self.riders[0].dtype) if self.riders else MARK
        kernel = functools.partial(kernel, len(sources), len(self.riders))
        args, count = [*sources, *self.riders], len(carried)

        def carry(*refs):
            head = 1 + len(args)
            for k in range(count):
                refs[head + count + k][...] = refs[head + k][...]
            kernel(*refs[:head], *refs[head + 2 * count :])

        shapes = [*((c.shape, c.dtype) for c in carried), *shapes, last]
        made = vmem_call(carry, name, (self.tab,), [*args, *carried], shapes, [], 10**9, 8, marks=marks)
        return made[:count], made[count:]

    def sent(self, made, kind, t):
        *made, mark = made
        if self.riders:
            self.riders = [mark, self.swap(mark, kind, t)]
        return [self.swap(made[0], kind, t), *made[1:]], mark

    def row_step(self, t, *marks):
        sources = self.first if t == 0 else self.rows
        _, rows, width = sources[0].shape
        shapes = [((self.route.rows_count >> (t + 2), rows, width), jnp.bfloat16)]
        if t == self.route.row_stages - 1:
            shapes.append(((rows, width), jnp.float32))
        kernel = functools.partial(row_kernel, self.route, t, self.widths)
        _, made = self.call(kernel, "row_sum", sources, shapes, marks)
        (got, *base), mark = self.sent(made, "row", t + 1)
        self.rows = self.rows + [got]
        if base:
            self.cols = [base[0], got[0]]
        return mark

    def col_step(self, t, *marks, carried=()):
        rows, width = self.cols[0].shape
        chunk, count = width // self.route.seq_count, self.route.seq_count >> (t + 1)
        kernel = functools.partial(col_kernel, self.route, t, chunk, count)
        shapes = [((rows, count * chunk), jnp.bfloat16)]
        carried, made = self.call(kernel, "col_sum", self.cols, shapes, marks, carried)
        (got,), mark = self.sent(made, "col", t)
        self.cols = self.cols + [got]
        return [mark, *carried] if carried else mark

    def end(self, cut, *marks):
        rows, width = self.cols[0].shape
        chunk = width // self.route.seq_count
        shapes = [((rows, cut), jnp.float32), ((rows, chunk - cut), jnp.float32)]
        kernel = functools.partial(end_kernel, self.route, chunk, cut)
        return self.call(kernel, "end_sum", self.cols, shapes, marks)[1]


def dot(left, right):
    return lax.dot_general(left, right, (((1,), (0,)), ((), ())), preferred_element_type=jnp.float32)


def dot_t(left, right):
    return lax.dot_general(left, right, (((1,), (1,)), ((), ())), preferred_element_type=jnp.float32)


def t_dot(left, right):
    return lax.dot_general(left, right, (((0,), (0,)), ((), ())), preferred_element_type=jnp.float32)


def up_to(value, step):
    return -(-value // step) * step


class Clips:
    def __init__(self, slot_count, seq_count):
        self.slots = slot_count
        length = slot_count * seq_count
        sure = length // CLIP - 1
        spans = [(k * CLIP, CLIP, 0) for k in range(sure)] + [(sure * CLIP, length - sure * CLIP, 1)]
        held = [[] for _ in range(seq_count)]
        self.before, self.behind = [], []
        low = high = 0
        for at, count, tail in spans:
            shares = [
                min(at + count, (s + 1) * slot_count) - max(at, s * slot_count) for s in range(seq_count)
            ]
            owner = max(range(seq_count), key=lambda s: shares[s])
            held[owner].append((at - owner * slot_count, count, tail))
            for s, share in enumerate(shares):
                if share > 0 and s != owner:
                    assert abs(s - owner) == 1 and not tail
                    (self.before if s < owner else self.behind).append((s, owner))
                    low, high = max(low, share * (s < owner)), max(high, share * (s > owner))
        self.low, self.high = up_to(low, 16), up_to(high, 16)
        self.window = self.low + slot_count + self.high
        self.a_rows = up_to(CLIP, 16)
        self.b_rows = up_to(max(CLIP, length - sure * CLIP), 16)
        self.rows = self.a_rows + self.b_rows
        self.tail_at = sure * CLIP % slot_count
        self.shards = []
        for spots in held:
            first = [spot for spot in spots if not spot[2]]
            last = [spot for spot in spots if spot[2]]
            assert len(first) + len(last) < 3
            blocks = (first[:1] or [(0, 0, 0)]) + (first[1:] + last or [(0, 0, 0)])
            self.shards.append([v for at, count, _ in blocks for v in (at + self.low, count)] + [len(last)])

    def brought(self, lows, highs):
        return lax.ppermute(lows, "seq", self.before), lax.ppermute(highs, "seq", self.behind)

    def returned(self, lows, highs):
        return (
            lax.ppermute(lows, "seq", [(owner, s) for s, owner in self.before]),
            lax.ppermute(highs, "seq", [(owner, s) for s, owner in self.behind]),
        )


TAIL_AT = 4


def chosen(tab_ref, clips, turned):
    a_at, a_len, b_at, b_len = (tab_ref[k] for k in range(4))
    if turned:
        shape, row_dim = (clips.window, clips.rows), 1
    else:
        shape, row_dim = (clips.rows, clips.window), 0
    row = lax.broadcasted_iota(jnp.int32, shape, row_dim)
    slot = lax.broadcasted_iota(jnp.int32, shape, 1 - row_dim)
    in_a = (row < a_len) & (slot == row + a_at)
    second = row - clips.a_rows
    in_b = (second >= 0) & (second < b_len) & (slot == second + b_at)
    return jnp.where(in_a | in_b, 1.0, 0.0).astype(jnp.bfloat16)


def block_masks(tab_ref, seg_ref, clips, row, key_dim):
    shape_a = (1, clips.a_rows) if key_dim == 1 else (clips.a_rows, 1)
    key_a = lax.broadcasted_iota(jnp.int32, shape_a, key_dim)
    mask_a = jnp.where(key_a < CLIP, 0.0, -1e30)
    shape_b = (clips.b_rows, clips.b_rows)
    key_b = lax.broadcasted_iota(jnp.int32, shape_b, key_dim)
    query_b = lax.broadcasted_iota(jnp.int32, shape_b, 1 - key_dim)
    six = (tab_ref[TAIL_AT] > 0) & (seg_ref[row, clips.tail_at] >= 0)
    split, b_len = jnp.where(six, CLIP, 0), jnp.maximum(tab_ref[3], 1)
    fits = (key_b < b_len) & ((key_b < split) == (query_b < split))
    mask_b = jnp.where(fits, 0.0, -1e30)
    return mask_a, mask_b


def window_of(low_ref, own_ref, high_ref, r):
    return jnp.concatenate([low_ref[r], own_ref[r], high_ref[r]], 0)


def put_window(clips, values, low_ref, own_ref, high_ref, r):
    low_ref[r] = values[: clips.low]
    own_ref[r] = values[clips.low : clips.low + clips.slots]
    high_ref[r] = values[clips.low + clips.slots :]


def norm_parts(values):
    center = values - jnp.mean(values, -1, keepdims=True)
    spread = jnp.mean(center * center, -1, keepdims=True)
    rate = lax.rsqrt(spread + 1e-06)
    return center * rate, rate


def norm_back(d_unit, unit, rate):
    return rate * (
        d_unit
        - jnp.mean(d_unit, -1, keepdims=True)
        - unit * jnp.mean(d_unit * unit, -1, keepdims=True)
    )


def split_heads(pair):
    low = lax.broadcasted_iota(jnp.int32, pair.shape, 1) < HEAD_DIM
    zero = jnp.zeros_like(pair)
    return jnp.concatenate([jnp.where(low, pair, zero), jnp.where(low, zero, pair)], 0)


def join_heads(both):
    half = both.shape[0] // 2
    low = lax.broadcasted_iota(jnp.int32, (half, both.shape[1]), 1) < HEAD_DIM
    return jnp.where(low, both[:half], both[half:])


def window_shapes(clips, row_count, width):
    return [((row_count, n, width), jnp.bfloat16) for n in (clips.low, clips.slots, clips.high)]


def cot_kernel(cot_ref, w_down_ref, total_ref, d_active_ref, made_ref, sems):
    cot = cot_ref[...].reshape(-1, cot_ref.shape[-1])
    total_ref[...] = jnp.sum(cot.astype(jnp.float32), 0, keepdims=True)
    steps, _, chunk = made_ref.shape

    def one(f, carry):
        rows = pl.ds(pl.multiple_of(f * chunk, chunk), chunk)
        made_ref[f] = dot_t(cot, w_down_ref[rows]).astype(jnp.bfloat16)
        pltpu.make_async_copy(made_ref.at[f], d_active_ref.at[f], sems.at[f]).start()
        return carry

    lax.fori_loop(0, steps, one, 0)
    for f in range(steps):
        pltpu.make_async_copy(made_ref.at[f], d_active_ref.at[f], sems.at[f]).wait()


def cot_back(steps, mark, cot, w_down):
    count, width = cot.shape[0] * cot.shape[1], cot.shape[2]
    made = ((steps, count, w_down.shape[0] // steps), jnp.bfloat16)
    scratch = [pltpu.VMEM(*made), pltpu.SemaphoreType.DMA((steps,))]
    shapes = [((1, width), jnp.float32)]
    return vmem_call(cot_kernel, "cot_back", (), (cot, w_down), shapes, scratch, 3 * 10**9, 14, [made], (mark,))


def attend_kernel(
    clips, tab_ref, seg_ref, low_ref, x_ref, high_ref, par_ref, w_ref,
    own_low_ref, own_ref, own_high_ref, mark_ref, qkv_out_ref, normed_out_ref, qkv_ref, normed_ref, att_ref, sems,
):
    mark_ref[...] = jnp.zeros_like(mark_ref)
    row_count, _, width = x_ref.shape
    pick, turned = chosen(tab_ref, clips, False), chosen(tab_ref, clips, True)
    for r in range(row_count):
        unit, _ = norm_parts(dot(pick, window_of(low_ref, x_ref, high_ref, r)))
        normed_ref[r] = (unit * par_ref[0:1] + par_ref[1:2]).astype(jnp.bfloat16)
    copies = [pltpu.make_async_copy(normed_ref, normed_out_ref, sems.at[row_count])]
    copies[0].start()
    for r in range(row_count):
        for part in range(3):
            cols = slice(part * width, (part + 1) * width)
            made = dot(normed_ref[r], w_ref[:, cols])
            if part != 1:
                made = made + par_ref[2 + part // 2 : 3 + part // 2]
            if part == 0:
                made = made * HEAD_DIM ** (-0.5)
            qkv_ref[r, :, cols] = made.astype(jnp.bfloat16)
        copies.append(pltpu.make_async_copy(qkv_ref.at[r], qkv_out_ref.at[r], sems.at[r]))
        copies[-1].start()
        masks = block_masks(tab_ref, seg_ref, clips, r, 1)
        for base, count, mask in ((0, clips.a_rows, masks[0]), (clips.a_rows, clips.b_rows, masks[1])):
            here = slice(base, base + count)
            if mask.shape[0] > 1:
                mask = jnp.concatenate([mask, mask], 0)

            def scores_of(p):
                query, key = (qkv_ref[r, here, k * width + p * 128 : k * width + (p + 1) * 128] for k in range(2))
                return dot_t(split_heads(query), key)

            pairs = width // 128
            coming = scores_of(0)
            for p in range(pairs):
                scores, coming = coming + mask, scores_of(p + 1) if p + 1 < pairs else None
                peak = jnp.max(scores, -1, keepdims=True)
                weights = jnp.exp(scores - peak)
                total = jnp.sum(weights, -1, keepdims=True)
                value = qkv_ref[r, here, 2 * width + p * 128 : 2 * width + (p + 1) * 128]
                mixed = dot(weights.astype(jnp.bfloat16), value) / total
                att_ref[here, p * 128 : (p + 1) * 128] = join_heads(mixed).astype(jnp.bfloat16)
        back = dot(turned, att_ref[...]).astype(jnp.bfloat16)
        put_window(clips, back, own_low_ref, own_ref, own_high_ref, r)
    for copy in copies:
        copy.wait()


def attend(clips, tab, seg, *args):
    row_count, _, width = args[1].shape
    shapes = window_shapes(clips, row_count, width) + [MARK]
    far = [
        ((row_count, clips.rows, 3 * width), jnp.bfloat16),
        ((row_count, clips.rows, width), jnp.bfloat16),
    ]
    scratch = [pltpu.VMEM(*s) for s in far] + [
        pltpu.VMEM((clips.rows, width), jnp.bfloat16),
        pltpu.SemaphoreType.DMA((row_count + 1,)),
    ]
    kernel = functools.partial(attend_kernel, clips)
    return vmem_call(kernel, "attend", (tab, seg), args, shapes, scratch, 8 * 10**9, 20, far)


def gelu_parts(hidden):
    cdf = 0.5 + 0.5 * lax.erf(hidden * 0.7071067811865476)
    return hidden * cdf, cdf + hidden * (0.3989422804014327 * jnp.exp(-0.5 * hidden * hidden))


def grad_shapes(route, width, cols):
    rows, half = width // route.rows_count, route.rows_count // 2
    return [((n, rows, cols), jnp.bfloat16) for n in (half // 2, half - half // 2, half)]


def hand_out(tab_ref, route, held_ref, refs, cols):
    spots = [(ref, k) for ref in refs for k in range(ref.shape[0])]
    for at, (ref, k) in enumerate(spots):
        ref[k, :, cols] = held_ref[tab_ref[route.places["block"] + at]]


def mlp_kernel(
    clips, route, tab_ref, x_ref, att_ref, first_ref, last_ref, cot_ref, w_out_ref, par_ref,
    w_up_ref, w_down_ref, d_active_ref,
    out_ref, middle_ref, att_sum_ref, d_hidden_ref, up_vec_ref, now_ref, later_ref, keep_ref,
    normed_s, result_s, held_s,
):
    row_count, slots, width = x_ref.shape
    steps, count, chunk = d_active_ref.shape
    rows = width // route.rows_count
    for r in range(row_count):
        att_sum_ref[r] = att_ref[r]
        att_sum_ref[r, : clips.high] += first_ref[r]
        att_sum_ref[r, slots - clips.low :] += last_ref[r]
    made = dot(att_sum_ref[...].reshape(count, width), w_out_ref[...])
    middle = x_ref[...].reshape(count, width).astype(jnp.float32) + made + par_ref[4:5]
    middle_ref[...] = middle
    unit, _ = norm_parts(middle)
    normed_s[...] = (unit * par_ref[5:6] + par_ref[6:7]).astype(jnp.bfloat16)
    cot = cot_ref[...].reshape(count, width)
    result_s[...] = middle + par_ref[7:8]

    def one(f, carry):
        part = pl.ds(pl.multiple_of(f * chunk, 128), chunk)
        hidden = dot(normed_s[...], w_up_ref[:, part]) + par_ref[pl.ds(8 + f, 1)]
        active, slope = gelu_parts(hidden)
        active_b = active.astype(jnp.bfloat16)
        d_hidden = (d_active_ref[f].astype(jnp.float32) * slope).astype(jnp.bfloat16)
        d_hidden_ref[f] = d_hidden
        up_vec_ref[pl.ds(f, 1)] = jnp.sum(d_hidden.astype(jnp.float32), 0, keepdims=True)
        result_s[...] += dot(active_b, w_down_ref[part])
        for at, grad in ((0, t_dot(normed_s[...], d_hidden)), (chunk, t_dot(cot, active_b))):
            grad = grad.astype(jnp.bfloat16)
            for b in range(route.rows_count):
                held_s[b, :, at : at + chunk] = grad[b * rows : (b + 1) * rows]
        cols = pl.ds(pl.multiple_of(2 * f * chunk, 128), 2 * chunk)
        hand_out(tab_ref, route, held_s, (now_ref, later_ref, keep_ref), cols)
        return carry

    lax.fori_loop(0, steps, one, 0, unroll=2)
    out_ref[...] = result_s[...].reshape(out_ref.shape).astype(jnp.bfloat16)


def mlp(clips, route, tab, *args):
    row_count, slots, width = args[0].shape
    steps, count, chunk = args[-1].shape
    bf16, f32 = jnp.bfloat16, jnp.float32
    shapes = [
        ((row_count, slots, width), bf16),
        ((count, width), f32),
        ((row_count, slots, width), bf16),
        ((steps, count, chunk), bf16),
        ((steps, chunk), f32),
        *grad_shapes(route, width, 2 * steps * chunk),
    ]
    scratch = [
        pltpu.VMEM((count, width), bf16),
        pltpu.VMEM((count, width), f32),
        pltpu.VMEM((route.rows_count, width // route.rows_count, 2 * chunk), bf16),
    ]
    kernel = functools.partial(mlp_kernel, clips, route)
    return vmem_call(kernel, "mlp", (tab,), args, shapes, scratch, 20 * 10**9, 24)


def mlp_back_kernel(
    clips, route, tab_ref, d_hidden_ref, w_up_ref, middle_ref, par_ref, cot_ref, w_out_ref, att_ref,
    d_low_ref, d_att_ref, d_high_ref, d_middle_ref, out_grad_ref, vec_ref,
):
    row_count, slots, width = cot_ref.shape
    steps, count, chunk = d_hidden_ref.shape
    d_normed = dot_t(d_hidden_ref[0], w_up_ref[:, :chunk])
    for f in range(1, steps):
        d_normed += dot_t(d_hidden_ref[f], w_up_ref[:, f * chunk : (f + 1) * chunk])
    unit, rate = norm_parts(middle_ref[...])
    vec_ref[1:2] = jnp.sum(d_normed * unit, 0, keepdims=True)
    vec_ref[2:3] = jnp.sum(d_normed, 0, keepdims=True)
    cot = cot_ref[...].reshape(count, width).astype(jnp.float32)
    total = cot + norm_back(d_normed * par_ref[5:6], unit, rate)
    d_middle_ref[...] = total.reshape(d_middle_ref.shape)
    branch = total.astype(jnp.bfloat16)
    vec_ref[0:1] = jnp.sum(branch.astype(jnp.float32), 0, keepdims=True)
    made = dot_t(branch, w_out_ref[...]).astype(jnp.bfloat16).reshape(row_count, slots, width)
    d_att_ref[...] = made
    d_low_ref[...] = made[:, slots - clips.low :]
    d_high_ref[...] = made[:, : clips.high]
    grad = t_dot(att_ref[...].reshape(count, width), branch).astype(jnp.bfloat16)
    rows = width // route.rows_count
    for b in range(route.rows_count):
        out_grad_ref[b] = grad[b * rows : (b + 1) * rows]


def mlp_back(clips, route, tab, *args):
    row_count, _, width = args[4].shape
    shapes = window_shapes(clips, row_count, width) + [
        (args[4].shape, jnp.float32),
        ((route.rows_count, width // route.rows_count, width), jnp.bfloat16),
        ((3, width), jnp.float32),
    ]
    kernel = functools.partial(mlp_back_kernel, clips, route)
    return vmem_call(kernel, "mlp_back", (tab,), args, shapes, [], 5 * 10**9, 16)


def attend_back_kernel(
    clips, route, tab_ref, seg_ref, qkv_ref, d_low_ref, d_att_ref, d_high_ref, normed_ref, out_grad_ref,
    d_qkv_ref, vec_ref, now_ref, later_ref, keep_ref, d_mixed_s, held_s,
):
    row_count, rows, width = normed_ref.shape
    scale = HEAD_DIM ** (-0.5)
    pick = chosen(tab_ref, clips, False)

    def one_row(r, total):
        d_mixed_s[...] = dot(pick, window_of(d_low_ref, d_att_ref, d_high_ref, r)).astype(jnp.bfloat16)
        masks = block_masks(tab_ref, seg_ref, clips, r, 0)
        for base, count, mask in ((0, clips.a_rows, masks[0]), (clips.a_rows, clips.b_rows, masks[1])):
            here = slice(base, base + count)
            if mask.shape[1] > 1:
                mask = jnp.concatenate([mask, mask], 1)

            def products(p):
                cols = [slice(k * width + p * 128, k * width + (p + 1) * 128) for k in range(3)]
                query, key, value = (qkv_ref[r, here, c] for c in cols)
                queries = split_heads(query)
                d_mixed = split_heads(d_mixed_s[here, cols[0]])
                return cols, key, queries, d_mixed, dot_t(key, queries), dot_t(value, d_mixed)

            pairs = width // 128
            coming = products(0)
            for p in range(pairs):
                (cols, key, queries, d_mixed, scores, d_prob), coming = (
                    coming,
                    products(p + 1) if p + 1 < pairs else None,
                )
                scores = scores + mask
                peak = jnp.max(scores, 0, keepdims=True)
                weights = jnp.exp(scores - peak)
                prob = weights * (1.0 / jnp.sum(weights, 0, keepdims=True))
                d_value = dot(prob.astype(jnp.bfloat16), d_mixed)
                centre = jnp.sum(d_prob * prob, 0, keepdims=True)
                d_scores = (prob * (d_prob - centre)).astype(jnp.bfloat16)
                d_key = dot(d_scores, queries)
                d_query = join_heads(t_dot(d_scores, key)) * scale
                for c, made in zip(cols, (d_query, d_key, d_value)):
                    d_qkv_ref[r, here, c] = made.astype(jnp.bfloat16)
        return total + jnp.sum(d_qkv_ref[r].astype(jnp.float32), 0, keepdims=True)

    total = lax.fori_loop(0, row_count, one_row, jnp.zeros((1, 3 * width), jnp.float32))
    for k in range(3):
        vec_ref[k : k + 1] = total[:, k * width : (k + 1) * width]
    flat = normed_ref[...].reshape(row_count * rows, width)
    height = width // route.rows_count
    for k in range(4):
        cols = slice(k * width, (k + 1) * width)
        if k < 3:
            made = t_dot(flat, d_qkv_ref[:, :, cols].reshape(row_count * rows, width)).astype(jnp.bfloat16)
            for b in range(route.rows_count):
                held_s[b] = made[b * height : (b + 1) * height]
        hand_out(tab_ref, route, held_s if k < 3 else out_grad_ref, (now_ref, later_ref, keep_ref), cols)


def attend_back(clips, route, tab, seg, mark, *args):
    row_count, rows, width = args[4].shape
    shapes = [
        ((row_count, rows, 3 * width), jnp.bfloat16),
        ((3, width), jnp.float32),
        *grad_shapes(route, width, 4 * width),
    ]
    scratch = [
        pltpu.VMEM((rows, width), jnp.bfloat16),
        pltpu.VMEM((route.rows_count, width // route.rows_count, width), jnp.bfloat16),
    ]
    kernel = functools.partial(attend_back_kernel, clips, route)
    return vmem_call(kernel, "attend_back", (tab, seg), args, shapes, scratch, 10**6, 18, marks=(mark,))


def first_back_kernel(clips, tab_ref, low_ref, x_ref, high_ref, par_ref, w_ref, *refs):
    row_count = x_ref.shape[0]
    d_qkv_ref, *vec_refs = refs[:-4]
    own_low_ref, own_ref, own_high_ref, vec_ref = refs[-4:]
    pick, turned = chosen(tab_ref, clips, False), chosen(tab_ref, clips, True)
    sums = []
    for r in range(row_count):
        unit, rate = norm_parts(dot(pick, window_of(low_ref, x_ref, high_ref, r)))
        d_normed = dot_t(d_qkv_ref[r], w_ref[...])
        sums.append([jnp.sum(p, 0, keepdims=True) for p in (d_normed * unit, d_normed)])
        d_in = norm_back(d_normed * par_ref[0:1], unit, rate).astype(jnp.bfloat16)
        back = dot(turned, d_in).astype(jnp.bfloat16)
        put_window(clips, back, own_low_ref, own_ref, own_high_ref, r)
    for k in range(2):
        vec_ref[k : k + 1] = sum(s[k] for s in sums[1:]) + sums[0][k]
    at = 2
    for ref in vec_refs:
        vec_ref[at : at + ref.shape[0]] = ref[...]
        at += ref.shape[0]


def first_back(clips, tab, mark, *args):
    row_count, _, width = args[1].shape
    count = 2 + sum(a.shape[0] for a in args[6:])
    shapes = window_shapes(clips, row_count, width) + [((count, width), jnp.float32)]
    kernel = functools.partial(first_back_kernel, clips)
    return vmem_call(kernel, "first_back", (tab,), args, shapes, [], 10**6, 16, marks=(mark,))


def finish_kernel(clips, d_middle_ref, own_ref, first_ref, last_ref, out_ref, mark_ref):
    for r in range(own_ref.shape[0]):
        total = d_middle_ref[r] + own_ref[r].astype(jnp.float32)
        tail = clips.slots - clips.low
        first = total[: clips.high] + first_ref[r].astype(jnp.float32)
        last = total[tail:] + last_ref[r].astype(jnp.float32)
        out_ref[r] = jnp.concatenate([first, total[clips.high : tail], last], 0).astype(jnp.bfloat16)
    mark_ref[...] = jnp.zeros_like(mark_ref)


def finish(clips, mark, *args):
    shapes = [(args[1].shape, jnp.bfloat16), MARK]
    kernel = functools.partial(finish_kernel, clips)
    return vmem_call(kernel, "finish", (), args, shapes, [], 10**9, 8, marks=(mark,))


def on_device(
    tokens,
    segments,
    ln1_gain,
    ln1_bias,
    w_qkv,
    q_bias,
    v_bias,
    w_out,
    out_bias,
    ln2_gain,
    ln2_bias,
    w_up,
    up_bias,
    w_down,
    down_bias,
    cotangent,
):
    row_count, slot_count, width = tokens.shape
    seq_count, rows_count = lax.axis_size("seq"), lax.axis_size("rows")
    clips = Clips(slot_count, seq_count)
    route = Route(seq_count, rows_count, clips.shards)
    low, high = clips.brought(tokens[:, slot_count - clips.low :], tokens[:, : clips.high])
    tab = jnp.asarray(route.table)[lax.axis_index("seq") * rows_count + lax.axis_index("rows")]
    total, at = 8 * width + up_bias.shape[0], 0
    params = jnp.zeros((total,), jnp.float32)
    for vector in (ln1_gain, ln1_bias, q_bias, v_bias, out_bias, ln2_gain, ln2_bias, down_bias, up_bias):
        params = params + lax.pad(vector, 0.0, [(at, total - at - vector.shape[0], 0)])
        at += vector.shape[0]
    params = params.reshape(-1, width)
    cot = cotangent
    att_low, att, att_high, mark, qkv, normed = attend(
        clips, tab, segments, low, tokens, high, params, w_qkv
    )
    att_last, att_first = clips.returned(att_low, att_high)
    vec_cot, d_active = cot_back(seq_count, mark, cot, w_down)
    out, middle, att, d_hidden, vec_up, *mlp_grad = mlp(
        clips, route, tab, tokens, att, att_first, att_last, cot, w_out, params, w_up, w_down, d_active
    )
    sum_a = Scatter(route, tab, (2 * w_up.shape[1],), *mlp_grad)
    d_low, d_att, d_high, d_middle, out_grad, vec_mid = mlp_back(
        clips, route, tab, d_hidden, w_up, middle, params, cot, w_out, att
    )
    mark = sum_a.row_step(0, vec_mid)
    d_low, d_high = clips.brought(d_low, d_high)
    d_qkv, vec_qkv, *qkv_grad = attend_back(
        clips, route, tab, segments, passed(route, mark), qkv, d_low, d_att, d_high, normed, out_grad
    )
    sum_b = Scatter(route, tab, (3 * width, width), *qkv_grad)
    mark = vec_qkv
    for t in range(1, route.row_stages):
        mark = sum_a.row_step(t, mark)
    d_in_low, d_in, d_in_high, vectors = first_back(
        clips, tab, passed(route, mark), low, tokens, high, params, w_qkv, d_qkv, vec_mid, vec_cot, vec_qkv, vec_up
    )
    sum_a.take_on(vectors)
    mark = sum_a.col_step(0)
    mark = sum_b.row_step(0, mark)
    for t in range(1, route.row_stages):
        mark = sum_b.row_step(t, mark)
    for t in range(1, route.col_stages):
        mark, d_in_low, d_in_high = sum_a.col_step(t, mark, carried=(d_in_low, d_in_high))
    d_in_last, d_in_first = clips.returned(d_in_low, d_in_high)
    mark = sum_b.col_step(0, mark)
    grad_tokens, _ = finish(clips, mark, d_middle, d_in, d_in_first, d_in_last)
    sum_up, sum_down, vectors = sum_a.end(UNIT, mark)
    for t in range(route.row_stages):
        vectors = vectors + sum_a.swap(vectors, "row", t + 1)
    for t in range(1, route.col_stages):
        mark = sum_b.col_step(t, mark)
    sum_qkv, sum_out, _ = sum_b.end(3 * width // seq_count)
    return (
        out,
        grad_tokens,
        vectors[0],
        vectors[1],
        sum_qkv,
        vectors[6],
        vectors[8],
        sum_out,
        vectors[2],
        vectors[3],
        vectors[4],
        sum_up,
        vectors[9:].reshape(-1),
        sum_down.T,
        vectors[5],
    )


def solution(mesh):
    placed = (
        P("rows", "seq", None),
        P("rows", "seq"),
        P(),
        P(),
        P(),
        P(),
        P(),
        P(),
        P(),
        P(),
        P(),
        P(),
        P(),
        P(),
        P(),
        P("rows", "seq", None),
    )
    return jax.shard_map(
        on_device,
        mesh=mesh,
        in_specs=placed,
        out_specs=(
            P("rows", "seq", None),
            P("rows", "seq", None),
            P(),
            P(),
            P("rows", "seq"),
            P(),
            P(),
            P("rows", "seq"),
            P(),
            P(),
            P(),
            P("rows", "seq"),
            P(),
            P("seq", "rows"),
            P(),
        ),
        check_vma=False,
    )
```

```python
import functools

import jax
import jax.numpy as jnp
import numpy as np
from jax import lax
from jax.experimental import pallas as pl
from jax.experimental.pallas import tpu as pltpu
from jax.sharding import PartitionSpec as P

HEAD_DIM = 64
CLIP = 157
UNIT = 768


def bit_orders(count, offset):
    bits = max(count.bit_length() - 1, 0)
    free = list(range(offset, bits))
    return free, free[::-1]


class Route:
    def __init__(self, seq_count, rows_count, shards):
        self.seq_count, self.rows_count = seq_count, rows_count
        plain, turned = bit_orders(rows_count, 1)
        self.row_bits = [[0] + plain, [0] + turned]
        self.col_bits = list(bit_orders(seq_count, 0))
        self.row_stages = len(plain)
        self.col_stages = len(self.col_bits[0])
        self.places = {}
        self.table = np.array(
            [self.one_device(s, r, first) for s, first in enumerate(shards) for r in range(rows_count)],
            np.int32,
        )

    def halves(self, r):
        bit = self.row_bits[r & 1][1]
        ours = [b for b in range(self.rows_count) if not (b ^ r) & 1]
        return [b for b in ours if (b ^ r) >> bit & 1], [b for b in ours if not (b ^ r) >> bit & 1]

    def one_device(self, s, r, shard):
        core, places = r & 1, self.places
        row = [*shard, core]
        spots = sum(self.halves(r ^ 1), []) + sorted(sum(self.halves(r), []))
        places["block"] = len(row)
        row += spots
        own = sorted(sum(self.halves(r), []))
        sent, kept = self.halves(r)
        places["row", 0] = [len(row), len(row) + len(sent)]
        row += [own.index(b) for b in sent] + list(range(len(sent)))
        lists = [own, kept, kept]
        for t, bit in enumerate(self.row_bits[core][2:], 1):
            send = [b for b in kept if (b ^ r) >> bit & 1]
            kept = [b for b in kept if not (b ^ r) >> bit & 1]
            places["row", t] = []
            for origin in lists:
                places["row", t].append(len(row))
                row += [origin.index(b) for b in send]
            lists.append(kept)
        places["own"] = []
        for origin in lists[:-1]:
            places["own"].append(len(row))
            row.append(origin.index(r))
        kept, lists = list(range(self.seq_count)), [list(range(self.seq_count))]
        for t, bit in enumerate(self.col_bits[core]):
            send = [b for b in kept if (b ^ s) >> bit & 1]
            kept = [b for b in kept if not (b ^ s) >> bit & 1]
            places["col", t] = []
            for origin in lists:
                places["col", t].append(len(row))
                row += [origin.index(b) for b in send]
            lists.append(kept)
        places["end"] = []
        for origin in lists:
            places["end"].append(len(row))
            row.append(origin.index(s))
        return row

    def pairs(self, kind, t):
        out = []
        for s in range(self.seq_count):
            for r in range(self.rows_count):
                if kind == "row":
                    to = s * self.rows_count + (r ^ (1 << self.row_bits[r & 1][t]))
                else:
                    to = (s ^ (1 << self.col_bits[r & 1][t])) * self.rows_count + r
                out.append((s * self.rows_count + r, to))
        return out


def add_up(pieces):
    total = pieces[0].astype(jnp.float32)
    for piece in pieces[1:]:
        total = total + piece.astype(jnp.float32)
    return total


def in_vmem():
    return pl.BlockSpec(memory_space=pltpu.VMEM)


def in_smem():
    return pl.BlockSpec(memory_space=pltpu.SMEM)


def vmem_call(kernel, name, flags, args, shapes, scratch, flops, mega, far=(), marks=()):
    head, skip = len(flags) + len(args), len(marks)

    def without_marks(*refs):
        kernel(*refs[:head], *refs[head + skip :])

    return pl.pallas_call(
        without_marks,
        in_specs=[in_smem()] * len(flags) + [in_vmem()] * (len(args) + skip),
        out_specs=[in_vmem()] * len(shapes) + [pl.BlockSpec(memory_space=pltpu.HBM)] * len(far),
        out_shape=[jax.ShapeDtypeStruct(*s) for s in shapes] + [pltpu.HBM(*s) for s in far],
        scratch_shapes=scratch,
        compiler_params=pltpu.CompilerParams(vmem_limit_bytes=mega << 20),
        cost_estimate=pl.CostEstimate(flops=flops, bytes_accessed=1 << 10, transcendentals=0),
        name=name,
    )(*flags, *args, *marks)


MARK = ((8, 128), jnp.float32)


def in_strips(rows, step):
    if rows % 16:
        step(slice(0, rows))
        return

    def one(i, carry):
        step(pl.ds(pl.multiple_of(i * 16, 16), 16))
        return carry

    lax.fori_loop(0, rows // 16, one, 0)


RIDER_ROWS = 16


def read_rider(refs, rows, width):
    held, came = refs
    if came.dtype == jnp.float32:
        return held[...] + came[...]
    high, low = (came[rows:, k * width : (k + 1) * width].astype(jnp.float32) for k in range(2))
    return held[...] + (high + low)


def put_rider(rider, out_ref, rows):
    high = rider.astype(jnp.bfloat16)
    low = (rider - high.astype(jnp.float32)).astype(jnp.bfloat16)
    for k, half in enumerate((high, low)):
        out_ref[rows:, k * rider.shape[1] : (k + 1) * rider.shape[1]] = half


def by_shards(values, widths, count):
    if len(widths) < 2:
        return values
    pieces = []
    for s in range(count):
        at = 0
        for wide in widths:
            part = wide // count
            pieces.append(values[:, at + s * part : at + (s + 1) * part])
            at += wide
    return jnp.concatenate(pieces, 1)


def row_kernel(route, t, widths, sources, riders, tab_ref, *refs):
    source_refs, out_refs = refs[:sources], refs[sources + riders :]
    out_refs[-1][...] = jnp.zeros_like(out_refs[-1])

    def step(strip):
        for j in range(out_refs[0].shape[0]):
            pieces = [ref[tab_ref[base + j], strip] for base, ref in zip(route.places["row", t], source_refs)]
            total = add_up(pieces)
            if len(out_refs) > 2:
                total = by_shards(total, widths, route.seq_count)
            out_refs[0][j, strip] = total.astype(jnp.bfloat16)
        if len(out_refs) > 2:
            bases = zip(route.places["own"], source_refs)
            total = add_up([ref[tab_ref[base], strip] for base, ref in bases])
            out_refs[1][strip] = by_shards(total, widths, route.seq_count)

    in_strips(out_refs[0].shape[1], step)


def col_pieces(route, key, j, chunk, tab_ref, refs, strip):
    pieces = []
    for u, ref in enumerate(refs):
        at = tab_ref[route.places[key][max(u - 1, 0)] + j] * chunk
        pieces.append(ref[strip, pl.ds(pl.multiple_of(at, 128), chunk)])
    return add_up(pieces)


def col_kernel(route, t, chunk, count, sources, riders, tab_ref, *refs):
    source_refs, rider_refs, out_refs = refs[:sources], refs[sources : sources + riders], refs[sources + riders :]
    rows = source_refs[0].shape[0]
    if riders:
        rider = read_rider(rider_refs, rows, out_refs[-1].shape[1])
        out_refs[-1][...] = rider
        out_refs[0][rows:] = jnp.zeros_like(out_refs[0][rows:])
        put_rider(rider, out_refs[0], rows)
    else:
        out_refs[-1][...] = jnp.zeros_like(out_refs[-1])

    def step(strip):
        for j in range(count):
            made = col_pieces(route, ("col", t), j, chunk, tab_ref, source_refs, strip)
            out_refs[0][strip, j * chunk : (j + 1) * chunk] = made.astype(jnp.bfloat16)

    in_strips(rows, step)


def end_kernel(route, chunk, cut, sources, riders, tab_ref, *refs):
    source_refs, rider_refs, out_refs = refs[:sources], refs[sources : sources + riders], refs[sources + riders :]
    if riders:
        out_refs[-1][...] = read_rider(rider_refs, source_refs[0].shape[0], out_refs[-1].shape[1])
    else:
        out_refs[-1][...] = jnp.zeros_like(out_refs[-1])

    def step(strip):
        total = col_pieces(route, "end", 0, chunk, tab_ref, source_refs, strip)
        out_refs[0][strip] = total[:, :cut]
        out_refs[1][strip] = total[:, cut:]

    in_strips(source_refs[0].shape[0], step)


def hop_kernel(held_ref, came_ref, total_ref):
    total_ref[...] = held_ref[...] + came_ref[...]


def hop_sum(held, came, mark):
    return vmem_call(hop_kernel, "hop_sum", (), (held, came), [(held.shape, held.dtype)], [], 10**6, 4, marks=(mark,))[0]


def passed(route, mark):
    return lax.ppermute(mark, ("seq", "rows"), route.pairs("row", 0))


class Scatter:
    def __init__(self, route, tab, widths, now, later, keep):
        self.route, self.tab, self.widths, self.riders = route, tab, widths, []
        self.first = [keep, self.swap(now, "row", 0)]
        self.rows = [keep, self.swap(later, "row", 0)]
        self.cols = []

    def swap(self, send, kind, t):
        return lax.ppermute(send, ("seq", "rows"), self.route.pairs(kind, t))

    def take_on(self, rider):
        self.riders = [rider, self.swap(rider, "row", 0)]

    def call(self, kernel, name, sources, shapes, marks, riders=()):
        last = (riders[0].shape, riders[0].dtype) if riders else MARK
        kernel = functools.partial(kernel, len(sources), len(riders))
        return vmem_call(kernel, name, (self.tab,), [*sources, *riders], [*shapes, last], [], 10**9, 8, marks=marks)

    def row_step(self, t, *marks):
        sources = self.first if t == 0 else self.rows
        _, rows, width = sources[0].shape
        shapes = [((self.route.rows_count >> (t + 2), rows, width), jnp.bfloat16)]
        if t == self.route.row_stages - 1:
            shapes.append(((rows, width), jnp.float32))
        kernel = functools.partial(row_kernel, self.route, t, self.widths)
        send, *base, mark = self.call(kernel, "row_sum", sources, shapes, marks)
        got = self.swap(send, "row", t + 1)
        self.rows = self.rows + [got]
        if base:
            self.cols = [base[0], got[0]]
        return mark

    def col_step(self, t, *marks):
        rows, width = self.cols[0].shape
        chunk, count = width // self.route.seq_count, self.route.seq_count >> (t + 1)
        kernel = functools.partial(col_kernel, self.route, t, chunk, count)
        more = RIDER_ROWS if self.riders else 0
        shapes = [((rows + more, count * chunk), jnp.bfloat16)]
        send, mark = self.call(kernel, "col_sum", self.cols, shapes, marks, self.riders)
        got = self.swap(send, "col", t)
        self.cols = self.cols + [got]
        if self.riders:
            self.riders = [mark, got]
        return mark

    def end(self, cut, *marks):
        rows, width = self.cols[0].shape
        chunk = width // self.route.seq_count
        shapes = [((rows, cut), jnp.float32), ((rows, chunk - cut), jnp.float32)]
        kernel = functools.partial(end_kernel, self.route, chunk, cut)
        return self.call(kernel, "end_sum", self.cols, shapes, marks, self.riders)


def dot(left, right):
    return lax.dot_general(left, right, (((1,), (0,)), ((), ())), preferred_element_type=jnp.float32)


def dot_t(left, right):
    return lax.dot_general(left, right, (((1,), (1,)), ((), ())), preferred_element_type=jnp.float32)


def t_dot(left, right):
    return lax.dot_general(left, right, (((0,), (0,)), ((), ())), preferred_element_type=jnp.float32)


def up_to(value, step):
    return -(-value // step) * step


class Clips:
    def __init__(self, slot_count, seq_count):
        self.slots = slot_count
        length = slot_count * seq_count
        sure = length // CLIP - 1
        spans = [(k * CLIP, CLIP, 0) for k in range(sure)] + [(sure * CLIP, length - sure * CLIP, 1)]
        held = [[] for _ in range(seq_count)]
        self.before, self.behind = [], []
        low = high = 0
        for at, count, tail in spans:
            shares = [
                min(at + count, (s + 1) * slot_count) - max(at, s * slot_count) for s in range(seq_count)
            ]
            owner = max(range(seq_count), key=lambda s: shares[s])
            held[owner].append((at - owner * slot_count, count, tail))
            for s, share in enumerate(shares):
                if share > 0 and s != owner:
                    assert abs(s - owner) == 1 and not tail
                    (self.before if s < owner else self.behind).append((s, owner))
                    low, high = max(low, share * (s < owner)), max(high, share * (s > owner))
        self.low, self.high = up_to(low, 16), up_to(high, 16)
        self.window = self.low + slot_count + self.high
        self.a_rows = up_to(CLIP, 16)
        self.b_rows = up_to(max(CLIP, length - sure * CLIP), 16)
        self.rows = self.a_rows + self.b_rows
        self.tail_at = sure * CLIP % slot_count
        self.shards = []
        for spots in held:
            first = [spot for spot in spots if not spot[2]]
            last = [spot for spot in spots if spot[2]]
            assert len(first) + len(last) < 3
            blocks = (first[:1] or [(0, 0, 0)]) + (first[1:] + last or [(0, 0, 0)])
            self.shards.append([v for at, count, _ in blocks for v in (at + self.low, count)] + [len(last)])

    def brought(self, lows, highs):
        highs = lax.ppermute(highs, "seq", self.behind)
        return lax.ppermute(lows, "seq", self.before), highs

    def returned(self, lows, highs):
        return (
            lax.ppermute(lows, "seq", [(owner, s) for s, owner in self.before]),
            lax.ppermute(highs, "seq", [(owner, s) for s, owner in self.behind]),
        )


TAIL_AT = 4


def chosen(tab_ref, clips, turned):
    a_at, a_len, b_at, b_len = (tab_ref[k] for k in range(4))
    if turned:
        shape, row_dim = (clips.window, clips.rows), 1
    else:
        shape, row_dim = (clips.rows, clips.window), 0
    row = lax.broadcasted_iota(jnp.int32, shape, row_dim)
    slot = lax.broadcasted_iota(jnp.int32, shape, 1 - row_dim)
    in_a = (row < a_len) & (slot == row + a_at)
    second = row - clips.a_rows
    in_b = (second >= 0) & (second < b_len) & (slot == second + b_at)
    return jnp.where(in_a | in_b, 1.0, 0.0).astype(jnp.bfloat16)


def block_masks(tab_ref, seg_ref, clips, row, key_dim):
    shape_a = (1, clips.a_rows) if key_dim == 1 else (clips.a_rows, 1)
    key_a = lax.broadcasted_iota(jnp.int32, shape_a, key_dim)
    mask_a = jnp.where(key_a < CLIP, 0.0, -1e30)
    shape_b = (clips.b_rows, clips.b_rows)
    key_b = lax.broadcasted_iota(jnp.int32, shape_b, key_dim)
    query_b = lax.broadcasted_iota(jnp.int32, shape_b, 1 - key_dim)
    six = (tab_ref[TAIL_AT] > 0) & (seg_ref[row, clips.tail_at] >= 0)
    split, b_len = jnp.where(six, CLIP, 0), jnp.maximum(tab_ref[3], 1)
    fits = (key_b < b_len) & ((key_b < split) == (query_b < split))
    mask_b = jnp.where(fits, 0.0, -1e30)
    return mask_a, mask_b


def window_of(low_ref, own_ref, high_ref, r):
    return jnp.concatenate([low_ref[r], own_ref[r], high_ref[r]], 0)


def put_window(clips, values, low_ref, own_ref, high_ref, r):
    low_ref[r] = values[: clips.low]
    own_ref[r] = values[clips.low : clips.low + clips.slots]
    high_ref[r] = values[clips.low + clips.slots :]


def norm_parts(values):
    center = values - jnp.mean(values, -1, keepdims=True)
    spread = jnp.mean(center * center, -1, keepdims=True)
    rate = lax.rsqrt(spread + 1e-06)
    return center * rate, rate


def norm_back(d_unit, unit, rate):
    return rate * (
        d_unit
        - jnp.mean(d_unit, -1, keepdims=True)
        - unit * jnp.mean(d_unit * unit, -1, keepdims=True)
    )


def split_heads(pair):
    low = lax.broadcasted_iota(jnp.int32, pair.shape, 1) < HEAD_DIM
    zero = jnp.zeros_like(pair)
    return jnp.concatenate([jnp.where(low, pair, zero), jnp.where(low, zero, pair)], 0)


def join_heads(both):
    half = both.shape[0] // 2
    low = lax.broadcasted_iota(jnp.int32, (half, both.shape[1]), 1) < HEAD_DIM
    return jnp.where(low, both[:half], both[half:])


def window_shapes(clips, row_count, width):
    return [((row_count, n, width), jnp.bfloat16) for n in (clips.low, clips.slots, clips.high)]


def hold_kernel(*refs):
    refs[-1][...] = jnp.zeros_like(refs[-1])


def hold(*args):
    return vmem_call(hold_kernel, "hold", (), args, [MARK], [], 10**6, 4)[0]


def cot_kernel(cot_ref, w_down_ref, total_ref, d_active_ref):
    cot = cot_ref[...].reshape(-1, cot_ref.shape[-1])
    total_ref[...] = jnp.sum(cot.astype(jnp.float32), 0, keepdims=True)
    steps, _, chunk = d_active_ref.shape

    def one(f, carry):
        rows = pl.ds(pl.multiple_of(f * chunk, chunk), chunk)
        d_active_ref[f] = dot_t(cot, w_down_ref[rows]).astype(jnp.bfloat16)
        return carry

    lax.fori_loop(0, steps, one, 0)


def cot_back(steps, mark, cot, w_down):
    count, width = cot.shape[0] * cot.shape[1], cot.shape[2]
    shapes = [((1, width), jnp.float32), ((steps, count, w_down.shape[0] // steps), jnp.bfloat16)]
    return vmem_call(cot_kernel, "cot_back", (), (cot, w_down), shapes, [], 3 * 10**9, 14, marks=(mark,))


def attend_kernel(
    clips, tab_ref, seg_ref, low_ref, x_ref, high_ref, par_ref, w_ref,
    own_low_ref, own_ref, own_high_ref, mark_ref, qkv_out_ref, normed_out_ref, qkv_ref, normed_ref, att_ref, sems,
):
    mark_ref[...] = jnp.zeros_like(mark_ref)
    row_count, _, width = x_ref.shape
    pick, turned = chosen(tab_ref, clips, False), chosen(tab_ref, clips, True)
    for r in range(row_count):
        unit, _ = norm_parts(dot(pick, window_of(low_ref, x_ref, high_ref, r)))
        normed_ref[r] = (unit * par_ref[0:1] + par_ref[1:2]).astype(jnp.bfloat16)
    copies = [pltpu.make_async_copy(normed_ref, normed_out_ref, sems.at[row_count])]
    copies[0].start()
    for r in range(row_count):
        for part in range(3):
            cols = slice(part * width, (part + 1) * width)
            made = dot(normed_ref[r], w_ref[:, cols])
            if part != 1:
                made = made + par_ref[2 + part // 2 : 3 + part // 2]
            if part == 0:
                made = made * HEAD_DIM ** (-0.5)
            qkv_ref[r, :, cols] = made.astype(jnp.bfloat16)
        copies.append(pltpu.make_async_copy(qkv_ref.at[r], qkv_out_ref.at[r], sems.at[r]))
        copies[-1].start()
        masks = block_masks(tab_ref, seg_ref, clips, r, 1)
        for base, count, mask in ((0, clips.a_rows, masks[0]), (clips.a_rows, clips.b_rows, masks[1])):
            here = slice(base, base + count)
            if mask.shape[0] > 1:
                mask = jnp.concatenate([mask, mask], 0)

            def scores_of(p):
                query, key = (qkv_ref[r, here, k * width + p * 128 : k * width + (p + 1) * 128] for k in range(2))
                return dot_t(split_heads(query), key)

            pairs = width // 128
            coming = scores_of(0)
            for p in range(pairs):
                scores, coming = coming + mask, scores_of(p + 1) if p + 1 < pairs else None
                peak = jnp.max(scores, -1, keepdims=True)
                weights = jnp.exp(scores - peak)
                total = jnp.sum(weights, -1, keepdims=True)
                value = qkv_ref[r, here, 2 * width + p * 128 : 2 * width + (p + 1) * 128]
                mixed = dot(weights.astype(jnp.bfloat16), value) / total
                att_ref[here, p * 128 : (p + 1) * 128] = join_heads(mixed).astype(jnp.bfloat16)
        back = dot(turned, att_ref[...]).astype(jnp.bfloat16)
        put_window(clips, back, own_low_ref, own_ref, own_high_ref, r)
    for copy in copies:
        copy.wait()


def attend(clips, tab, seg, mark, *args):
    row_count, _, width = args[1].shape
    shapes = window_shapes(clips, row_count, width) + [MARK]
    far = [
        ((row_count, clips.rows, 3 * width), jnp.bfloat16),
        ((row_count, clips.rows, width), jnp.bfloat16),
    ]
    scratch = [pltpu.VMEM(*s) for s in far] + [
        pltpu.VMEM((clips.rows, width), jnp.bfloat16),
        pltpu.SemaphoreType.DMA((row_count + 1,)),
    ]
    kernel = functools.partial(attend_kernel, clips)
    return vmem_call(kernel, "attend", (tab, seg), args, shapes, scratch, 8 * 10**9, 20, far, (mark,))


def gelu_parts(hidden):
    cdf = 0.5 + 0.5 * lax.erf(hidden * 0.7071067811865476)
    return hidden * cdf, cdf + hidden * (0.3989422804014327 * jnp.exp(-0.5 * hidden * hidden))


def grad_shapes(route, width, cols):
    rows, half = width // route.rows_count, route.rows_count // 2
    return [((n, rows, cols), jnp.bfloat16) for n in (half // 2, half - half // 2, half)]


def hand_out(tab_ref, route, held_ref, refs, cols):
    spots = [(ref, k) for ref in refs for k in range(ref.shape[0])]
    for at, (ref, k) in enumerate(spots):
        ref[k, :, cols] = held_ref[tab_ref[route.places["block"] + at]]


def mlp_kernel(
    clips, route, tab_ref, x_ref, att_ref, first_ref, last_ref, cot_ref, w_out_ref, par_ref,
    w_up_ref, w_down_ref, d_active_ref,
    out_ref, middle_ref, att_sum_ref, d_hidden_ref, up_vec_ref, now_ref, later_ref, keep_ref,
    normed_s, result_s, held_s,
):
    row_count, slots, width = x_ref.shape
    steps, count, chunk = d_active_ref.shape
    rows = width // route.rows_count
    for r in range(row_count):
        att_sum_ref[r] = att_ref[r]
        att_sum_ref[r, : clips.high] += first_ref[r]
        att_sum_ref[r, slots - clips.low :] += last_ref[r]
    made = dot(att_sum_ref[...].reshape(count, width), w_out_ref[...])
    middle = x_ref[...].reshape(count, width).astype(jnp.float32) + made + par_ref[4:5]
    middle_ref[...] = middle
    unit, _ = norm_parts(middle)
    normed_s[...] = (unit * par_ref[5:6] + par_ref[6:7]).astype(jnp.bfloat16)
    cot = cot_ref[...].reshape(count, width)
    result_s[...] = middle + par_ref[7:8]

    def one(f, carry):
        part = pl.ds(pl.multiple_of(f * chunk, 128), chunk)
        hidden = dot(normed_s[...], w_up_ref[:, part]) + par_ref[pl.ds(8 + f, 1)]
        active, slope = gelu_parts(hidden)
        active_b = active.astype(jnp.bfloat16)
        d_hidden = (d_active_ref[f].astype(jnp.float32) * slope).astype(jnp.bfloat16)
        d_hidden_ref[f] = d_hidden
        up_vec_ref[pl.ds(f, 1)] = jnp.sum(d_hidden.astype(jnp.float32), 0, keepdims=True)
        result_s[...] += dot(active_b, w_down_ref[part])
        for at, grad in ((0, t_dot(normed_s[...], d_hidden)), (chunk, t_dot(cot, active_b))):
            grad = grad.astype(jnp.bfloat16)
            for b in range(route.rows_count):
                held_s[b, :, at : at + chunk] = grad[b * rows : (b + 1) * rows]
        cols = pl.ds(pl.multiple_of(2 * f * chunk, 128), 2 * chunk)
        hand_out(tab_ref, route, held_s, (now_ref, later_ref, keep_ref), cols)
        return carry

    lax.fori_loop(0, steps, one, 0, unroll=2)
    out_ref[...] = result_s[...].reshape(out_ref.shape).astype(jnp.bfloat16)


def mlp(clips, route, tab, *args):
    row_count, slots, width = args[0].shape
    steps, count, chunk = args[-1].shape
    bf16, f32 = jnp.bfloat16, jnp.float32
    shapes = [
        ((row_count, slots, width), bf16),
        ((count, width), f32),
        ((row_count, slots, width), bf16),
        ((steps, count, chunk), bf16),
        ((steps, chunk), f32),
        *grad_shapes(route, width, 2 * steps * chunk),
    ]
    scratch = [
        pltpu.VMEM((count, width), bf16),
        pltpu.VMEM((count, width), f32),
        pltpu.VMEM((route.rows_count, width // route.rows_count, 2 * chunk), bf16),
    ]
    kernel = functools.partial(mlp_kernel, clips, route)
    return vmem_call(kernel, "mlp", (tab,), args, shapes, scratch, 20 * 10**9, 24)


def mlp_back_kernel(
    clips, route, tab_ref, d_hidden_ref, w_up_ref, middle_ref, par_ref, cot_ref, w_out_ref, att_ref,
    d_low_ref, d_att_ref, d_high_ref, d_middle_ref, out_grad_ref, vec_ref,
):
    row_count, slots, width = cot_ref.shape
    steps, count, chunk = d_hidden_ref.shape
    d_normed = dot_t(d_hidden_ref[0], w_up_ref[:, :chunk])
    for f in range(1, steps):
        d_normed += dot_t(d_hidden_ref[f], w_up_ref[:, f * chunk : (f + 1) * chunk])
    unit, rate = norm_parts(middle_ref[...])
    vec_ref[1:2] = jnp.sum(d_normed * unit, 0, keepdims=True)
    vec_ref[2:3] = jnp.sum(d_normed, 0, keepdims=True)
    cot = cot_ref[...].reshape(count, width).astype(jnp.float32)
    total = cot + norm_back(d_normed * par_ref[5:6], unit, rate)
    d_middle_ref[...] = total.reshape(d_middle_ref.shape)
    branch = total.astype(jnp.bfloat16)
    vec_ref[0:1] = jnp.sum(branch.astype(jnp.float32), 0, keepdims=True)
    made = dot_t(branch, w_out_ref[...]).astype(jnp.bfloat16).reshape(row_count, slots, width)
    d_att_ref[...] = made
    d_low_ref[...] = made[:, slots - clips.low :]
    d_high_ref[...] = made[:, : clips.high]
    grad = t_dot(att_ref[...].reshape(count, width), branch).astype(jnp.bfloat16)
    rows = width // route.rows_count
    for b in range(route.rows_count):
        out_grad_ref[b] = grad[b * rows : (b + 1) * rows]


def mlp_back(clips, route, tab, *args):
    row_count, _, width = args[4].shape
    shapes = window_shapes(clips, row_count, width) + [
        (args[4].shape, jnp.float32),
        ((route.rows_count, width // route.rows_count, width), jnp.bfloat16),
        ((3, width), jnp.float32),
    ]
    kernel = functools.partial(mlp_back_kernel, clips, route)
    return vmem_call(kernel, "mlp_back", (tab,), args, shapes, [], 5 * 10**9, 16)


def attend_back_kernel(
    clips, route, tab_ref, seg_ref, qkv_ref, d_low_ref, d_att_ref, d_high_ref, normed_ref, out_grad_ref,
    d_qkv_ref, vec_ref, now_ref, later_ref, keep_ref, d_mixed_s, held_s,
):
    row_count, rows, width = normed_ref.shape
    scale = HEAD_DIM ** (-0.5)
    pick = chosen(tab_ref, clips, False)

    def one_row(r, total):
        d_mixed_s[...] = dot(pick, window_of(d_low_ref, d_att_ref, d_high_ref, r)).astype(jnp.bfloat16)
        masks = block_masks(tab_ref, seg_ref, clips, r, 0)
        for base, count, mask in ((0, clips.a_rows, masks[0]), (clips.a_rows, clips.b_rows, masks[1])):
            here = slice(base, base + count)
            if mask.shape[1] > 1:
                mask = jnp.concatenate([mask, mask], 1)

            def products(p):
                cols = [slice(k * width + p * 128, k * width + (p + 1) * 128) for k in range(3)]
                query, key, value = (qkv_ref[r, here, c] for c in cols)
                queries = split_heads(query)
                d_mixed = split_heads(d_mixed_s[here, cols[0]])
                return cols, key, queries, d_mixed, dot_t(key, queries), dot_t(value, d_mixed)

            pairs = width // 128
            coming = products(0)
            for p in range(pairs):
                (cols, key, queries, d_mixed, scores, d_prob), coming = (
                    coming,
                    products(p + 1) if p + 1 < pairs else None,
                )
                scores = scores + mask
                peak = jnp.max(scores, 0, keepdims=True)
                weights = jnp.exp(scores - peak)
                prob = weights * (1.0 / jnp.sum(weights, 0, keepdims=True))
                d_value = dot(prob.astype(jnp.bfloat16), d_mixed)
                centre = jnp.sum(d_prob * prob, 0, keepdims=True)
                d_scores = (prob * (d_prob - centre)).astype(jnp.bfloat16)
                d_key = dot(d_scores, queries)
                d_query = join_heads(t_dot(d_scores, key)) * scale
                for c, made in zip(cols, (d_query, d_key, d_value)):
                    d_qkv_ref[r, here, c] = made.astype(jnp.bfloat16)
        return total + jnp.sum(d_qkv_ref[r].astype(jnp.float32), 0, keepdims=True)

    total = lax.fori_loop(0, row_count, one_row, jnp.zeros((1, 3 * width), jnp.float32))
    for k in range(3):
        vec_ref[k : k + 1] = total[:, k * width : (k + 1) * width]
    flat = normed_ref[...].reshape(row_count * rows, width)
    height = width // route.rows_count
    for k in range(4):
        cols = slice(k * width, (k + 1) * width)
        if k < 3:
            made = t_dot(flat, d_qkv_ref[:, :, cols].reshape(row_count * rows, width)).astype(jnp.bfloat16)
            for b in range(route.rows_count):
                held_s[b] = made[b * height : (b + 1) * height]
        hand_out(tab_ref, route, held_s if k < 3 else out_grad_ref, (now_ref, later_ref, keep_ref), cols)


def attend_back(clips, route, tab, seg, mark, *args):
    row_count, rows, width = args[4].shape
    shapes = [
        ((row_count, rows, 3 * width), jnp.bfloat16),
        ((3, width), jnp.float32),
        *grad_shapes(route, width, 4 * width),
    ]
    scratch = [
        pltpu.VMEM((rows, width), jnp.bfloat16),
        pltpu.VMEM((route.rows_count, width // route.rows_count, width), jnp.bfloat16),
    ]
    kernel = functools.partial(attend_back_kernel, clips, route)
    return vmem_call(kernel, "attend_back", (tab, seg), args, shapes, scratch, 10**6, 18, marks=(mark,))


def first_back_kernel(clips, tab_ref, low_ref, x_ref, high_ref, par_ref, w_ref, *refs):
    row_count = x_ref.shape[0]
    d_qkv_ref, *vec_refs = refs[:-4]
    own_low_ref, own_ref, own_high_ref, vec_ref = refs[-4:]
    pick, turned = chosen(tab_ref, clips, False), chosen(tab_ref, clips, True)
    sums = []
    for r in range(row_count):
        unit, rate = norm_parts(dot(pick, window_of(low_ref, x_ref, high_ref, r)))
        d_normed = dot_t(d_qkv_ref[r], w_ref[...])
        sums.append([jnp.sum(p, 0, keepdims=True) for p in (d_normed * unit, d_normed)])
        d_in = norm_back(d_normed * par_ref[0:1], unit, rate).astype(jnp.bfloat16)
        back = dot(turned, d_in).astype(jnp.bfloat16)
        put_window(clips, back, own_low_ref, own_ref, own_high_ref, r)
    for k in range(2):
        vec_ref[k : k + 1] = sum(s[k] for s in sums[1:]) + sums[0][k]
    vec_ref[8:] = jnp.zeros_like(vec_ref[8:])
    at = 2
    for ref in vec_refs:
        vec_ref[at : at + ref.shape[0]] = ref[...]
        at += ref.shape[0]


def first_back(clips, tab, mark, *args):
    row_count, _, width = args[1].shape
    assert 2 + sum(a.shape[0] for a in args[6:]) <= RIDER_ROWS
    shapes = window_shapes(clips, row_count, width) + [((RIDER_ROWS, width), jnp.float32)]
    kernel = functools.partial(first_back_kernel, clips)
    return vmem_call(kernel, "first_back", (tab,), args, shapes, [], 10**6, 16, marks=(mark,))


def finish_kernel(clips, d_middle_ref, own_ref, first_ref, last_ref, out_ref, mark_ref):
    for r in range(own_ref.shape[0]):
        total = d_middle_ref[r] + own_ref[r].astype(jnp.float32)
        tail = clips.slots - clips.low
        first = total[: clips.high] + first_ref[r].astype(jnp.float32)
        last = total[tail:] + last_ref[r].astype(jnp.float32)
        out_ref[r] = jnp.concatenate([first, total[clips.high : tail], last], 0).astype(jnp.bfloat16)
    mark_ref[...] = jnp.zeros_like(mark_ref)


def finish(clips, mark, *args):
    shapes = [(args[1].shape, jnp.bfloat16), MARK]
    kernel = functools.partial(finish_kernel, clips)
    return vmem_call(kernel, "finish", (), args, shapes, [], 10**9, 8, marks=(mark,))


def on_device(
    tokens,
    segments,
    ln1_gain,
    ln1_bias,
    w_qkv,
    q_bias,
    v_bias,
    w_out,
    out_bias,
    ln2_gain,
    ln2_bias,
    w_up,
    up_bias,
    w_down,
    down_bias,
    cotangent,
):
    row_count, slot_count, width = tokens.shape
    seq_count, rows_count = lax.axis_size("seq"), lax.axis_size("rows")
    clips = Clips(slot_count, seq_count)
    route = Route(seq_count, rows_count, clips.shards)
    low, high = clips.brought(tokens[:, slot_count - clips.low :], tokens[:, : clips.high])
    tab = jnp.asarray(route.table)[lax.axis_index("seq") * rows_count + lax.axis_index("rows")]
    total, at = 8 * width + up_bias.shape[0], 0
    params = jnp.zeros((total,), jnp.float32)
    for vector in (ln1_gain, ln1_bias, q_bias, v_bias, out_bias, ln2_gain, ln2_bias, down_bias, up_bias):
        params = params + lax.pad(vector, 0.0, [(at, total - at - vector.shape[0], 0)])
        at += vector.shape[0]
    params = params.reshape(-1, width)
    cot = cotangent
    att_low, att, att_high, mark, qkv, normed = attend(
        clips, tab, segments, hold(tokens, w_qkv, params), low, tokens, high, params, w_qkv
    )
    att_last, att_first = clips.returned(att_low, att_high)
    vec_cot, d_active = cot_back(seq_count, mark, cot, w_down)
    out, middle, att, d_hidden, vec_up, *mlp_grad = mlp(
        clips, route, tab, tokens, att, att_first, att_last, cot, w_out, params, w_up, w_down, d_active
    )
    sum_a = Scatter(route, tab, (2 * w_up.shape[1],), *mlp_grad)
    d_low, d_att, d_high, d_middle, out_grad, vec_mid = mlp_back(
        clips, route, tab, d_hidden, w_up, middle, params, cot, w_out, att
    )
    mark = sum_a.row_step(0, vec_mid)
    d_low, d_high = clips.brought(d_low, d_high)
    d_qkv, vec_qkv, *qkv_grad = attend_back(
        clips, route, tab, segments, passed(route, mark), qkv, d_low, d_att, d_high, normed, out_grad
    )
    sum_b = Scatter(route, tab, (3 * width, width), *qkv_grad)
    mark = vec_qkv
    for t in range(1, route.row_stages):
        mark = sum_a.row_step(t, mark)
    d_in_low, d_in, d_in_high, vectors = first_back(
        clips, tab, passed(route, mark), low, tokens, high, params, w_qkv, d_qkv, vec_mid, vec_cot, vec_qkv, vec_up
    )
    d_in_last, d_in_first = clips.returned(d_in_low, d_in_high)
    grad_tokens, mark = finish(clips, mark, d_middle, d_in, d_in_first, d_in_last)
    sum_a.take_on(vectors)
    mark = sum_a.col_step(0, mark)
    mark = sum_b.row_step(0, mark)
    for t in range(1, route.row_stages):
        mark = sum_b.row_step(t, mark)
    for t in range(1, route.col_stages):
        mark = sum_a.col_step(t, mark)
    mark = sum_b.col_step(0, mark)
    sum_up, sum_down, vectors = sum_a.end(UNIT, mark)
    for t in range(1, route.col_stages):
        mark = sum_b.col_step(t, mark)
    for t in range(route.row_stages):
        vectors = hop_sum(vectors, sum_a.swap(vectors, "row", t + 1), mark)
    sum_qkv, sum_out, _ = sum_b.end(3 * width // seq_count)
    return (
        out,
        grad_tokens,
        vectors[0],
        vectors[1],
        sum_qkv,
        vectors[6],
        vectors[8],
        sum_out,
        vectors[2],
        vectors[3],
        vectors[4],
        sum_up,
        vectors[9 : 9 + up_bias.shape[0] // width].reshape(-1),
        sum_down.T,
        vectors[5],
    )


def solution(mesh):
    placed = (
        P("rows", "seq", None),
        P("rows", "seq"),
        P(),
        P(),
        P(),
        P(),
        P(),
        P(),
        P(),
        P(),
        P(),
        P(),
        P(),
        P(),
        P(),
        P("rows", "seq", None),
    )
    return jax.shard_map(
        on_device,
        mesh=mesh,
        in_specs=placed,
        out_specs=(
            P("rows", "seq", None),
            P("rows", "seq", None),
            P(),
            P(),
            P("rows", "seq"),
            P(),
            P(),
            P("rows", "seq"),
            P(),
            P(),
            P(),
            P("rows", "seq"),
            P(),
            P("seq", "rows"),
            P(),
        ),
        check_vma=False,
    )
```

```python
import functools

import jax
import jax.numpy as jnp
import numpy as np
from jax import lax
from jax.experimental import pallas as pl
from jax.experimental.pallas import tpu as pltpu
from jax.sharding import PartitionSpec as P

HEAD_DIM = 64
CLIP = 157
UNIT = 768


def bit_orders(count, offset):
    bits = max(count.bit_length() - 1, 0)
    free = list(range(offset, bits))
    return free, free[::-1]


class Route:
    def __init__(self, seq_count, rows_count, shards):
        self.seq_count, self.rows_count = seq_count, rows_count
        plain, turned = bit_orders(rows_count, 1)
        self.row_bits = [[0] + plain, [0] + turned]
        self.col_bits = list(bit_orders(seq_count, 0))
        self.row_stages = len(plain)
        self.col_stages = len(self.col_bits[0])
        self.places = {}
        self.table = np.array(
            [self.one_device(s, r, first) for s, first in enumerate(shards) for r in range(rows_count)],
            np.int32,
        )

    def halves(self, r):
        bit = self.row_bits[r & 1][1]
        ours = [b for b in range(self.rows_count) if not (b ^ r) & 1]
        return [b for b in ours if (b ^ r) >> bit & 1], [b for b in ours if not (b ^ r) >> bit & 1]

    def one_device(self, s, r, shard):
        core, places = r & 1, self.places
        row = [*shard, core]
        spots = sum(self.halves(r ^ 1), []) + sorted(sum(self.halves(r), []))
        places["block"] = len(row)
        row += spots
        own = sorted(sum(self.halves(r), []))
        sent, kept = self.halves(r)
        places["row", 0] = [len(row), len(row) + len(sent)]
        row += [own.index(b) for b in sent] + list(range(len(sent)))
        lists = [own, kept, kept]
        for t, bit in enumerate(self.row_bits[core][2:], 1):
            send = [b for b in kept if (b ^ r) >> bit & 1]
            kept = [b for b in kept if not (b ^ r) >> bit & 1]
            places["row", t] = []
            for origin in lists:
                places["row", t].append(len(row))
                row += [origin.index(b) for b in send]
            lists.append(kept)
        places["own"] = []
        for origin in lists[:-1]:
            places["own"].append(len(row))
            row.append(origin.index(r))
        kept, lists = list(range(self.seq_count)), [list(range(self.seq_count))]
        for t, bit in enumerate(self.col_bits[core]):
            send = [b for b in kept if (b ^ s) >> bit & 1]
            kept = [b for b in kept if not (b ^ s) >> bit & 1]
            places["col", t] = []
            for origin in lists:
                places["col", t].append(len(row))
                row += [origin.index(b) for b in send]
            lists.append(kept)
        places["end"] = []
        for origin in lists:
            places["end"].append(len(row))
            row.append(origin.index(s))
        return row

    def pairs(self, kind, t):
        out = []
        for s in range(self.seq_count):
            for r in range(self.rows_count):
                if kind == "row":
                    to = s * self.rows_count + (r ^ (1 << self.row_bits[r & 1][t]))
                else:
                    to = (s ^ (1 << self.col_bits[r & 1][t])) * self.rows_count + r
                out.append((s * self.rows_count + r, to))
        return out


def add_up(pieces):
    total = pieces[0].astype(jnp.float32)
    for piece in pieces[1:]:
        total = total + piece.astype(jnp.float32)
    return total


def in_vmem():
    return pl.BlockSpec(memory_space=pltpu.VMEM)


def in_smem():
    return pl.BlockSpec(memory_space=pltpu.SMEM)


def vmem_call(kernel, name, flags, args, shapes, scratch, flops, mega, far=(), marks=()):
    head, skip = len(flags) + len(args), len(marks)

    def without_marks(*refs):
        kernel(*refs[:head], *refs[head + skip :])

    return pl.pallas_call(
        without_marks,
        in_specs=[in_smem()] * len(flags) + [in_vmem()] * (len(args) + skip),
        out_specs=[in_vmem()] * len(shapes) + [pl.BlockSpec(memory_space=pltpu.HBM)] * len(far),
        out_shape=[jax.ShapeDtypeStruct(*s) for s in shapes] + [pltpu.HBM(*s) for s in far],
        scratch_shapes=scratch,
        compiler_params=pltpu.CompilerParams(vmem_limit_bytes=mega << 20),
        cost_estimate=pl.CostEstimate(flops=flops, bytes_accessed=1 << 10, transcendentals=0),
        name=name,
    )(*flags, *args, *marks)


MARK = ((8, 128), jnp.float32)


def in_strips(rows, step):
    if rows % 16:
        step(slice(0, rows))
        return

    def one(i, carry):
        step(pl.ds(pl.multiple_of(i * 16, 16), 16))
        return carry

    lax.fori_loop(0, rows // 16, one, 0)


RIDER_ROWS = 16


def read_rider(refs, rows, width):
    held, came = refs
    if came.dtype == jnp.float32:
        return held[...] + came[...]
    high, low = (came[rows:, k * width : (k + 1) * width].astype(jnp.float32) for k in range(2))
    return held[...] + (high + low)


def put_rider(rider, out_ref, rows):
    high = rider.astype(jnp.bfloat16)
    low = (rider - high.astype(jnp.float32)).astype(jnp.bfloat16)
    for k, half in enumerate((high, low)):
        out_ref[rows:, k * rider.shape[1] : (k + 1) * rider.shape[1]] = half


def by_shards(values, widths, count):
    if len(widths) < 2:
        return values
    pieces = []
    for s in range(count):
        at = 0
        for wide in widths:
            part = wide // count
            pieces.append(values[:, at + s * part : at + (s + 1) * part])
            at += wide
    return jnp.concatenate(pieces, 1)


def row_kernel(route, t, widths, sources, riders, tab_ref, *refs):
    source_refs, out_refs = refs[:sources], refs[sources + riders :]
    out_refs[-1][...] = jnp.zeros_like(out_refs[-1])

    def step(strip):
        for j in range(out_refs[0].shape[0]):
            pieces = [ref[tab_ref[base + j], strip] for base, ref in zip(route.places["row", t], source_refs)]
            total = add_up(pieces)
            if t == route.row_stages - 1:
                total = by_shards(total, widths, route.seq_count)
            out_refs[0][j, strip] = total.astype(jnp.bfloat16)

    in_strips(out_refs[0].shape[1], step)


def stay_kernel(route, widths, sources, riders, tab_ref, *refs):
    source_refs, out_refs = refs[:sources], refs[sources + riders :]
    out_refs[-1][...] = jnp.zeros_like(out_refs[-1])

    def step(strip):
        total = add_up([ref[tab_ref[base], strip] for base, ref in zip(route.places["own"], source_refs)])
        out_refs[0][strip] = by_shards(total, widths, route.seq_count)

    in_strips(out_refs[0].shape[0], step)


def col_pieces(route, key, j, chunk, tab_ref, refs, strip):
    pieces = []
    for u, ref in enumerate(refs):
        at = tab_ref[route.places[key][max(u - 1, 0)] + j] * chunk
        pieces.append(ref[strip, pl.ds(pl.multiple_of(at, 128), chunk)])
    return add_up(pieces)


def col_kernel(route, t, chunk, count, sources, riders, tab_ref, *refs):
    source_refs, rider_refs, out_refs = refs[:sources], refs[sources : sources + riders], refs[sources + riders :]
    rows = source_refs[0].shape[0]
    if riders:
        rider = read_rider(rider_refs, rows, out_refs[-1].shape[1])
        out_refs[-1][...] = rider
        out_refs[0][rows:] = jnp.zeros_like(out_refs[0][rows:])
        put_rider(rider, out_refs[0], rows)
    else:
        out_refs[-1][...] = jnp.zeros_like(out_refs[-1])

    def step(strip):
        for j in range(count):
            made = col_pieces(route, ("col", t), j, chunk, tab_ref, source_refs, strip)
            out_refs[0][strip, j * chunk : (j + 1) * chunk] = made.astype(jnp.bfloat16)

    in_strips(rows, step)


def end_kernel(route, chunk, cut, sources, riders, tab_ref, *refs):
    source_refs, rider_refs, out_refs = refs[:sources], refs[sources : sources + riders], refs[sources + riders :]
    if riders:
        out_refs[-1][...] = read_rider(rider_refs, source_refs[0].shape[0], out_refs[-1].shape[1])
    else:
        out_refs[-1][...] = jnp.zeros_like(out_refs[-1])

    def step(strip):
        total = col_pieces(route, "end", 0, chunk, tab_ref, source_refs, strip)
        out_refs[0][strip] = total[:, :cut]
        out_refs[1][strip] = total[:, cut:]

    in_strips(source_refs[0].shape[0], step)


def hop_kernel(held_ref, came_ref, total_ref):
    total_ref[...] = held_ref[...] + came_ref[...]


def hop_sum(held, came, mark):
    return vmem_call(hop_kernel, "hop_sum", (), (held, came), [(held.shape, held.dtype)], [], 10**6, 4, marks=(mark,))[0]


def passed(route, mark):
    return lax.ppermute(mark, ("seq", "rows"), route.pairs("row", 0))


class Scatter:
    def __init__(self, route, tab, widths, now, later, keep):
        self.route, self.tab, self.widths, self.riders = route, tab, widths, []
        self.first = [keep, self.swap(now, "row", 0)]
        self.rows = [keep, self.swap(later, "row", 0)]
        self.cols = []

    def swap(self, send, kind, t):
        return lax.ppermute(send, ("seq", "rows"), self.route.pairs(kind, t))

    def take_on(self, rider):
        self.riders = [rider, self.swap(rider, "row", 0)]

    def call(self, kernel, name, sources, shapes, marks, riders=()):
        last = (riders[0].shape, riders[0].dtype) if riders else MARK
        kernel = functools.partial(kernel, len(sources), len(riders))
        return vmem_call(kernel, name, (self.tab,), [*sources, *riders], [*shapes, last], [], 10**9, 8, marks=marks)

    def row_step(self, t, *marks):
        sources = self.first if t == 0 else self.rows
        _, rows, width = sources[0].shape
        shapes = [((self.route.rows_count >> (t + 2), rows, width), jnp.bfloat16)]
        kernel = functools.partial(row_kernel, self.route, t, self.widths)
        send, mark = self.call(kernel, "row_sum", sources, shapes, marks)
        got = self.swap(send, "row", t + 1)
        self.rows = self.rows + [got]
        if t == self.route.row_stages - 1:
            kernel = functools.partial(stay_kernel, self.route, self.widths)
            base, _ = self.call(kernel, "stay_sum", sources, [((rows, width), jnp.float32)], (mark,))
            self.cols = [base, got[0]]
        return mark

    def col_step(self, t, *marks):
        rows, width = self.cols[0].shape
        chunk, count = width // self.route.seq_count, self.route.seq_count >> (t + 1)
        kernel = functools.partial(col_kernel, self.route, t, chunk, count)
        more = RIDER_ROWS if self.riders else 0
        shapes = [((rows + more, count * chunk), jnp.bfloat16)]
        send, mark = self.call(kernel, "col_sum", self.cols, shapes, marks, self.riders)
        got = self.swap(send, "col", t)
        self.cols = self.cols + [got]
        if self.riders:
            self.riders = [mark, got]
        return mark

    def end(self, cut, *marks):
        rows, width = self.cols[0].shape
        chunk = width // self.route.seq_count
        shapes = [((rows, cut), jnp.float32), ((rows, chunk - cut), jnp.float32)]
        kernel = functools.partial(end_kernel, self.route, chunk, cut)
        return self.call(kernel, "end_sum", self.cols, shapes, marks, self.riders)


def dot(left, right):
    return lax.dot_general(left, right, (((1,), (0,)), ((), ())), preferred_element_type=jnp.float32)


def dot_t(left, right):
    return lax.dot_general(left, right, (((1,), (1,)), ((), ())), preferred_element_type=jnp.float32)


def t_dot(left, right):
    return lax.dot_general(left, right, (((0,), (0,)), ((), ())), preferred_element_type=jnp.float32)


def up_to(value, step):
    return -(-value // step) * step


class Clips:
    def __init__(self, slot_count, seq_count):
        self.slots = slot_count
        length = slot_count * seq_count
        sure = length // CLIP - 1
        spans = [(k * CLIP, CLIP, 0) for k in range(sure)] + [(sure * CLIP, length - sure * CLIP, 1)]
        held = [[] for _ in range(seq_count)]
        self.before, self.behind = [], []
        low = high = 0
        for at, count, tail in spans:
            shares = [
                min(at + count, (s + 1) * slot_count) - max(at, s * slot_count) for s in range(seq_count)
            ]
            owner = max(range(seq_count), key=lambda s: shares[s])
            held[owner].append((at - owner * slot_count, count, tail))
            for s, share in enumerate(shares):
                if share > 0 and s != owner:
                    assert abs(s - owner) == 1 and not tail
                    (self.before if s < owner else self.behind).append((s, owner))
                    low, high = max(low, share * (s < owner)), max(high, share * (s > owner))
        self.low, self.high = up_to(low, 16), up_to(high, 16)
        self.window = self.low + slot_count + self.high
        self.a_rows = up_to(CLIP, 16)
        self.b_rows = up_to(max(CLIP, length - sure * CLIP), 16)
        self.rows = self.a_rows + self.b_rows
        self.tail_at = sure * CLIP % slot_count
        self.shards = []
        for spots in held:
            first = [spot for spot in spots if not spot[2]]
            last = [spot for spot in spots if spot[2]]
            assert len(first) + len(last) < 3
            blocks = (first[:1] or [(0, 0, 0)]) + (first[1:] + last or [(0, 0, 0)])
            self.shards.append([v for at, count, _ in blocks for v in (at + self.low, count)] + [len(last)])

    def brought(self, lows, highs):
        highs = lax.ppermute(highs, "seq", self.behind)
        return lax.ppermute(lows, "seq", self.before), highs

    def returned(self, lows, highs):
        return (
            lax.ppermute(lows, "seq", [(owner, s) for s, owner in self.before]),
            lax.ppermute(highs, "seq", [(owner, s) for s, owner in self.behind]),
        )


TAIL_AT = 4


def chosen(tab_ref, clips, turned):
    a_at, a_len, b_at, b_len = (tab_ref[k] for k in range(4))
    if turned:
        shape, row_dim = (clips.window, clips.rows), 1
    else:
        shape, row_dim = (clips.rows, clips.window), 0
    row = lax.broadcasted_iota(jnp.int32, shape, row_dim)
    slot = lax.broadcasted_iota(jnp.int32, shape, 1 - row_dim)
    in_a = (row < a_len) & (slot == row + a_at)
    second = row - clips.a_rows
    in_b = (second >= 0) & (second < b_len) & (slot == second + b_at)
    return jnp.where(in_a | in_b, 1.0, 0.0).astype(jnp.bfloat16)


def block_masks(tab_ref, seg_ref, clips, row, key_dim):
    shape_a = (1, clips.a_rows) if key_dim == 1 else (clips.a_rows, 1)
    key_a = lax.broadcasted_iota(jnp.int32, shape_a, key_dim)
    mask_a = jnp.where(key_a < CLIP, 0.0, -1e30)
    shape_b = (clips.b_rows, clips.b_rows)
    key_b = lax.broadcasted_iota(jnp.int32, shape_b, key_dim)
    query_b = lax.broadcasted_iota(jnp.int32, shape_b, 1 - key_dim)
    six = (tab_ref[TAIL_AT] > 0) & (seg_ref[row, clips.tail_at] >= 0)
    split, b_len = jnp.where(six, CLIP, 0), jnp.maximum(tab_ref[3], 1)
    fits = (key_b < b_len) & ((key_b < split) == (query_b < split))
    mask_b = jnp.where(fits, 0.0, -1e30)
    return mask_a, mask_b


def window_of(low_ref, own_ref, high_ref, r):
    return jnp.concatenate([low_ref[r], own_ref[r], high_ref[r]], 0)


def put_window(clips, values, low_ref, own_ref, high_ref, r):
    low_ref[r] = values[: clips.low]
    own_ref[r] = values[clips.low : clips.low + clips.slots]
    high_ref[r] = values[clips.low + clips.slots :]


def norm_parts(values):
    center = values - jnp.mean(values, -1, keepdims=True)
    spread = jnp.mean(center * center, -1, keepdims=True)
    rate = lax.rsqrt(spread + 1e-06)
    return center * rate, rate


def norm_back(d_unit, unit, rate):
    return rate * (
        d_unit
        - jnp.mean(d_unit, -1, keepdims=True)
        - unit * jnp.mean(d_unit * unit, -1, keepdims=True)
    )


def split_heads(pair):
    low = lax.broadcasted_iota(jnp.int32, pair.shape, 1) < HEAD_DIM
    zero = jnp.zeros_like(pair)
    return jnp.concatenate([jnp.where(low, pair, zero), jnp.where(low, zero, pair)], 0)


def join_heads(both):
    half = both.shape[0] // 2
    low = lax.broadcasted_iota(jnp.int32, (half, both.shape[1]), 1) < HEAD_DIM
    return jnp.where(low, both[:half], both[half:])


def window_shapes(clips, row_count, width):
    return [((row_count, n, width), jnp.bfloat16) for n in (clips.low, clips.slots, clips.high)]


def hold_kernel(*refs):
    refs[-1][...] = jnp.zeros_like(refs[-1])


def hold(*args):
    return vmem_call(hold_kernel, "hold", (), args, [MARK], [], 10**6, 4)[0]


def edges_kernel(x_ref, low_ref, high_ref):
    low_ref[...] = x_ref[:, x_ref.shape[1] - low_ref.shape[1] :]
    high_ref[...] = x_ref[:, : high_ref.shape[1]]


def edges(clips, tokens):
    row_count, _, width = tokens.shape
    shapes = [((row_count, n, width), tokens.dtype) for n in (clips.low, clips.high)]
    return vmem_call(edges_kernel, "edges", (), (tokens,), shapes, [], 10**6, 4)


def cot_kernel(cot_ref, w_down_ref, total_ref, d_active_ref):
    cot = cot_ref[...].reshape(-1, cot_ref.shape[-1])
    total_ref[...] = jnp.sum(cot.astype(jnp.float32), 0, keepdims=True)
    steps, _, chunk = d_active_ref.shape

    def one(f, carry):
        rows = pl.ds(pl.multiple_of(f * chunk, chunk), chunk)
        d_active_ref[f] = dot_t(cot, w_down_ref[rows]).astype(jnp.bfloat16)
        return carry

    lax.fori_loop(0, steps, one, 0)


def cot_back(steps, mark, cot, w_down):
    count, width = cot.shape[0] * cot.shape[1], cot.shape[2]
    shapes = [((1, width), jnp.float32), ((steps, count, w_down.shape[0] // steps), jnp.bfloat16)]
    return vmem_call(cot_kernel, "cot_back", (), (cot, w_down), shapes, [], 3 * 10**9, 14, marks=(mark,))


def attend_kernel(
    clips, tab_ref, seg_ref, low_ref, x_ref, high_ref, par_ref, w_ref,
    own_low_ref, own_ref, own_high_ref, mark_ref, qkv_out_ref, normed_out_ref, qkv_ref, normed_ref, att_ref, sems,
):
    mark_ref[...] = jnp.zeros_like(mark_ref)
    row_count, _, width = x_ref.shape
    pick, turned = chosen(tab_ref, clips, False), chosen(tab_ref, clips, True)
    for r in range(row_count):
        unit, _ = norm_parts(dot(pick, window_of(low_ref, x_ref, high_ref, r)))
        normed_ref[r] = (unit * par_ref[0:1] + par_ref[1:2]).astype(jnp.bfloat16)
    copies = [pltpu.make_async_copy(normed_ref, normed_out_ref, sems.at[row_count])]
    copies[0].start()
    for r in range(row_count):
        for part in range(3):
            cols = slice(part * width, (part + 1) * width)
            made = dot(normed_ref[r], w_ref[:, cols])
            if part != 1:
                made = made + par_ref[2 + part // 2 : 3 + part // 2]
            if part == 0:
                made = made * HEAD_DIM ** (-0.5)
            qkv_ref[r, :, cols] = made.astype(jnp.bfloat16)
        copies.append(pltpu.make_async_copy(qkv_ref.at[r], qkv_out_ref.at[r], sems.at[r]))
        copies[-1].start()
        masks = block_masks(tab_ref, seg_ref, clips, r, 1)
        for base, count, mask in ((0, clips.a_rows, masks[0]), (clips.a_rows, clips.b_rows, masks[1])):
            here = slice(base, base + count)
            if mask.shape[0] > 1:
                mask = jnp.concatenate([mask, mask], 0)

            def scores_of(p):
                query, key = (qkv_ref[r, here, k * width + p * 128 : k * width + (p + 1) * 128] for k in range(2))
                return dot_t(split_heads(query), key)

            pairs = width // 128
            coming = scores_of(0)
            for p in range(pairs):
                scores, coming = coming + mask, scores_of(p + 1) if p + 1 < pairs else None
                peak = jnp.max(scores, -1, keepdims=True)
                weights = jnp.exp(scores - peak)
                total = jnp.sum(weights, -1, keepdims=True)
                value = qkv_ref[r, here, 2 * width + p * 128 : 2 * width + (p + 1) * 128]
                mixed = dot(weights.astype(jnp.bfloat16), value) / total
                att_ref[here, p * 128 : (p + 1) * 128] = join_heads(mixed).astype(jnp.bfloat16)
        back = dot(turned, att_ref[...]).astype(jnp.bfloat16)
        put_window(clips, back, own_low_ref, own_ref, own_high_ref, r)
    for copy in copies:
        copy.wait()


def attend(clips, tab, seg, mark, *args):
    row_count, _, width = args[1].shape
    shapes = window_shapes(clips, row_count, width) + [MARK]
    far = [
        ((row_count, clips.rows, 3 * width), jnp.bfloat16),
        ((row_count, clips.rows, width), jnp.bfloat16),
    ]
    scratch = [pltpu.VMEM(*s) for s in far] + [
        pltpu.VMEM((clips.rows, width), jnp.bfloat16),
        pltpu.SemaphoreType.DMA((row_count + 1,)),
    ]
    kernel = functools.partial(attend_kernel, clips)
    return vmem_call(kernel, "attend", (tab, seg), args, shapes, scratch, 8 * 10**9, 20, far, (mark,))


def gelu_parts(hidden):
    cdf = 0.5 + 0.5 * lax.erf(hidden * 0.7071067811865476)
    return hidden * cdf, cdf + hidden * (0.3989422804014327 * jnp.exp(-0.5 * hidden * hidden))


def grad_shapes(route, width, cols):
    rows, half = width // route.rows_count, route.rows_count // 2
    return [((n, rows, cols), jnp.bfloat16) for n in (half // 2, half - half // 2, half)]


def hand_out(tab_ref, route, held_ref, refs, cols):
    spots = [(ref, k) for ref in refs for k in range(ref.shape[0])]
    for at, (ref, k) in enumerate(spots):
        ref[k, :, cols] = held_ref[tab_ref[route.places["block"] + at]]


def mlp_kernel(
    clips, route, tab_ref, x_ref, att_ref, first_ref, last_ref, cot_ref, w_out_ref, par_ref,
    w_up_ref, w_down_ref, d_active_ref,
    out_ref, middle_ref, att_sum_ref, d_hidden_ref, up_vec_ref, now_ref, later_ref, keep_ref,
    normed_s, result_s, held_s,
):
    row_count, slots, width = x_ref.shape
    steps, count, chunk = d_active_ref.shape
    rows = width // route.rows_count
    for r in range(row_count):
        att_sum_ref[r] = att_ref[r]
        att_sum_ref[r, : clips.high] += first_ref[r]
        att_sum_ref[r, slots - clips.low :] += last_ref[r]
    made = dot(att_sum_ref[...].reshape(count, width), w_out_ref[...])
    middle = x_ref[...].reshape(count, width).astype(jnp.float32) + made + par_ref[4:5]
    middle_ref[...] = middle
    unit, _ = norm_parts(middle)
    normed_s[...] = (unit * par_ref[5:6] + par_ref[6:7]).astype(jnp.bfloat16)
    cot = cot_ref[...].reshape(count, width)
    result_s[...] = middle + par_ref[7:8]

    def one(f, carry):
        part = pl.ds(pl.multiple_of(f * chunk, 128), chunk)
        hidden = dot(normed_s[...], w_up_ref[:, part]) + par_ref[pl.ds(8 + f, 1)]
        active, slope = gelu_parts(hidden)
        active_b = active.astype(jnp.bfloat16)
        d_hidden = (d_active_ref[f].astype(jnp.float32) * slope).astype(jnp.bfloat16)
        d_hidden_ref[f] = d_hidden
        up_vec_ref[pl.ds(f, 1)] = jnp.sum(d_hidden.astype(jnp.float32), 0, keepdims=True)
        result_s[...] += dot(active_b, w_down_ref[part])
        for at, grad in ((0, t_dot(normed_s[...], d_hidden)), (chunk, t_dot(cot, active_b))):
            grad = grad.astype(jnp.bfloat16)
            for b in range(route.rows_count):
                held_s[b, :, at : at + chunk] = grad[b * rows : (b + 1) * rows]
        cols = pl.ds(pl.multiple_of(2 * f * chunk, 128), 2 * chunk)
        hand_out(tab_ref, route, held_s, (now_ref, later_ref, keep_ref), cols)
        return carry

    lax.fori_loop(0, steps, one, 0, unroll=4)
    out_ref[...] = result_s[...].reshape(out_ref.shape).astype(jnp.bfloat16)


def mlp(clips, route, tab, *args):
    row_count, slots, width = args[0].shape
    steps, count, chunk = args[-1].shape
    bf16, f32 = jnp.bfloat16, jnp.float32
    shapes = [
        ((row_count, slots, width), bf16),
        ((count, width), f32),
        ((row_count, slots, width), bf16),
        ((steps, count, chunk), bf16),
        ((steps, chunk), f32),
        *grad_shapes(route, width, 2 * steps * chunk),
    ]
    scratch = [
        pltpu.VMEM((count, width), bf16),
        pltpu.VMEM((count, width), f32),
        pltpu.VMEM((route.rows_count, width // route.rows_count, 2 * chunk), bf16),
    ]
    kernel = functools.partial(mlp_kernel, clips, route)
    return vmem_call(kernel, "mlp", (tab,), args, shapes, scratch, 20 * 10**9, 24)


def mlp_back_kernel(
    clips, route, tab_ref, d_hidden_ref, w_up_ref, middle_ref, par_ref, cot_ref, w_out_ref, att_ref,
    d_low_ref, d_att_ref, d_high_ref, d_middle_ref, out_grad_ref, vec_ref,
):
    row_count, slots, width = cot_ref.shape
    steps, count, chunk = d_hidden_ref.shape
    d_normed = dot_t(d_hidden_ref[0], w_up_ref[:, :chunk])
    for f in range(1, steps):
        d_normed += dot_t(d_hidden_ref[f], w_up_ref[:, f * chunk : (f + 1) * chunk])
    unit, rate = norm_parts(middle_ref[...])
    vec_ref[1:2] = jnp.sum(d_normed * unit, 0, keepdims=True)
    vec_ref[2:3] = jnp.sum(d_normed, 0, keepdims=True)
    cot = cot_ref[...].reshape(count, width).astype(jnp.float32)
    total = cot + norm_back(d_normed * par_ref[5:6], unit, rate)
    d_middle_ref[...] = total.reshape(d_middle_ref.shape)
    branch = total.astype(jnp.bfloat16)
    vec_ref[0:1] = jnp.sum(branch.astype(jnp.float32), 0, keepdims=True)
    made = dot_t(branch, w_out_ref[...]).astype(jnp.bfloat16).reshape(row_count, slots, width)
    d_att_ref[...] = made
    d_low_ref[...] = made[:, slots - clips.low :]
    d_high_ref[...] = made[:, : clips.high]
    grad = t_dot(att_ref[...].reshape(count, width), branch).astype(jnp.bfloat16)
    rows = width // route.rows_count
    for b in range(route.rows_count):
        out_grad_ref[b] = grad[b * rows : (b + 1) * rows]


def mlp_back(clips, route, tab, *args):
    row_count, _, width = args[4].shape
    shapes = window_shapes(clips, row_count, width) + [
        (args[4].shape, jnp.float32),
        ((route.rows_count, width // route.rows_count, width), jnp.bfloat16),
        ((3, width), jnp.float32),
    ]
    kernel = functools.partial(mlp_back_kernel, clips, route)
    return vmem_call(kernel, "mlp_back", (tab,), args, shapes, [], 5 * 10**9, 16)


def attend_back_kernel(
    clips, route, tab_ref, seg_ref, qkv_ref, d_low_ref, d_att_ref, d_high_ref, normed_ref, out_grad_ref,
    d_qkv_ref, vec_ref, now_ref, later_ref, keep_ref, d_mixed_s, held_s,
):
    row_count, rows, width = normed_ref.shape
    scale = HEAD_DIM ** (-0.5)
    pick = chosen(tab_ref, clips, False)

    def one_row(r, total):
        d_mixed_s[...] = dot(pick, window_of(d_low_ref, d_att_ref, d_high_ref, r)).astype(jnp.bfloat16)
        masks = block_masks(tab_ref, seg_ref, clips, r, 0)
        for base, count, mask in ((0, clips.a_rows, masks[0]), (clips.a_rows, clips.b_rows, masks[1])):
            here = slice(base, base + count)
            if mask.shape[1] > 1:
                mask = jnp.concatenate([mask, mask], 1)

            def products(p):
                cols = [slice(k * width + p * 128, k * width + (p + 1) * 128) for k in range(3)]
                query, key, value = (qkv_ref[r, here, c] for c in cols)
                queries = split_heads(query)
                d_mixed = split_heads(d_mixed_s[here, cols[0]])
                return cols, key, queries, d_mixed, dot_t(key, queries), dot_t(value, d_mixed)

            pairs = width // 128
            coming = products(0)
            for p in range(pairs):
                (cols, key, queries, d_mixed, scores, d_prob), coming = (
                    coming,
                    products(p + 1) if p + 1 < pairs else None,
                )
                scores = scores + mask
                peak = jnp.max(scores, 0, keepdims=True)
                weights = jnp.exp(scores - peak)
                prob = weights * (1.0 / jnp.sum(weights, 0, keepdims=True))
                d_value = dot(prob.astype(jnp.bfloat16), d_mixed)
                centre = jnp.sum(d_prob * prob, 0, keepdims=True)
                d_scores = (prob * (d_prob - centre)).astype(jnp.bfloat16)
                d_key = dot(d_scores, queries)
                d_query = join_heads(t_dot(d_scores, key)) * scale
                for c, made in zip(cols, (d_query, d_key, d_value)):
                    d_qkv_ref[r, here, c] = made.astype(jnp.bfloat16)
        return total + jnp.sum(d_qkv_ref[r].astype(jnp.float32), 0, keepdims=True)

    total = lax.fori_loop(0, row_count, one_row, jnp.zeros((1, 3 * width), jnp.float32))
    for k in range(3):
        vec_ref[k : k + 1] = total[:, k * width : (k + 1) * width]
    flat = normed_ref[...].reshape(row_count * rows, width)
    height = width // route.rows_count
    for k in range(4):
        cols = slice(k * width, (k + 1) * width)
        if k < 3:
            made = t_dot(flat, d_qkv_ref[:, :, cols].reshape(row_count * rows, width)).astype(jnp.bfloat16)
            for b in range(route.rows_count):
                held_s[b] = made[b * height : (b + 1) * height]
        hand_out(tab_ref, route, held_s if k < 3 else out_grad_ref, (now_ref, later_ref, keep_ref), cols)


def attend_back(clips, route, tab, seg, mark, *args):
    row_count, rows, width = args[4].shape
    shapes = [
        ((row_count, rows, 3 * width), jnp.bfloat16),
        ((3, width), jnp.float32),
        *grad_shapes(route, width, 4 * width),
    ]
    scratch = [
        pltpu.VMEM((rows, width), jnp.bfloat16),
        pltpu.VMEM((route.rows_count, width // route.rows_count, width), jnp.bfloat16),
    ]
    kernel = functools.partial(attend_back_kernel, clips, route)
    return vmem_call(kernel, "attend_back", (tab, seg), args, shapes, scratch, 10**6, 18, marks=(mark,))


def first_back_kernel(clips, tab_ref, low_ref, x_ref, high_ref, par_ref, w_ref, *refs):
    row_count = x_ref.shape[0]
    d_qkv_ref, *vec_refs = refs[:-4]
    own_low_ref, own_ref, own_high_ref, vec_ref = refs[-4:]
    pick, turned = chosen(tab_ref, clips, False), chosen(tab_ref, clips, True)
    sums = []
    for r in range(row_count):
        unit, rate = norm_parts(dot(pick, window_of(low_ref, x_ref, high_ref, r)))
        d_normed = dot_t(d_qkv_ref[r], w_ref[...])
        sums.append([jnp.sum(p, 0, keepdims=True) for p in (d_normed * unit, d_normed)])
        d_in = norm_back(d_normed * par_ref[0:1], unit, rate).astype(jnp.bfloat16)
        back = dot(turned, d_in).astype(jnp.bfloat16)
        put_window(clips, back, own_low_ref, own_ref, own_high_ref, r)
    for k in range(2):
        vec_ref[k : k + 1] = sum(s[k] for s in sums[1:]) + sums[0][k]
    vec_ref[8:] = jnp.zeros_like(vec_ref[8:])
    at = 2
    for ref in vec_refs:
        vec_ref[at : at + ref.shape[0]] = ref[...]
        at += ref.shape[0]


def first_back(clips, tab, mark, *args):
    row_count, _, width = args[1].shape
    assert 2 + sum(a.shape[0] for a in args[6:]) <= RIDER_ROWS
    shapes = window_shapes(clips, row_count, width) + [((RIDER_ROWS, width), jnp.float32)]
    kernel = functools.partial(first_back_kernel, clips)
    return vmem_call(kernel, "first_back", (tab,), args, shapes, [], 10**6, 16, marks=(mark,))


def finish_kernel(clips, d_middle_ref, own_ref, first_ref, last_ref, out_ref, mark_ref):
    for r in range(own_ref.shape[0]):
        total = d_middle_ref[r] + own_ref[r].astype(jnp.float32)
        tail = clips.slots - clips.low
        first = total[: clips.high] + first_ref[r].astype(jnp.float32)
        last = total[tail:] + last_ref[r].astype(jnp.float32)
        out_ref[r] = jnp.concatenate([first, total[clips.high : tail], last], 0).astype(jnp.bfloat16)
    mark_ref[...] = jnp.zeros_like(mark_ref)


def finish(clips, mark, *args):
    shapes = [(args[1].shape, jnp.bfloat16), MARK]
    kernel = functools.partial(finish_kernel, clips)
    return vmem_call(kernel, "finish", (), args, shapes, [], 10**9, 8, marks=(mark,))


def on_device(
    tokens,
    segments,
    ln1_gain,
    ln1_bias,
    w_qkv,
    q_bias,
    v_bias,
    w_out,
    out_bias,
    ln2_gain,
    ln2_bias,
    w_up,
    up_bias,
    w_down,
    down_bias,
    cotangent,
):
    row_count, slot_count, width = tokens.shape
    seq_count, rows_count = lax.axis_size("seq"), lax.axis_size("rows")
    clips = Clips(slot_count, seq_count)
    route = Route(seq_count, rows_count, clips.shards)
    low, high = clips.brought(*edges(clips, tokens))
    tab = jnp.asarray(route.table)[lax.axis_index("seq") * rows_count + lax.axis_index("rows")]
    total, at = 8 * width + up_bias.shape[0], 0
    params = jnp.zeros((total,), jnp.float32)
    for vector in (ln1_gain, ln1_bias, q_bias, v_bias, out_bias, ln2_gain, ln2_bias, down_bias, up_bias):
        params = params + lax.pad(vector, 0.0, [(at, total - at - vector.shape[0], 0)])
        at += vector.shape[0]
    params = params.reshape(-1, width)
    cot = cotangent
    att_low, att, att_high, mark, qkv, normed = attend(
        clips, tab, segments, hold(w_qkv, params), low, tokens, high, params, w_qkv
    )
    att_last, att_first = clips.returned(att_low, att_high)
    vec_cot, d_active = cot_back(seq_count, mark, cot, w_down)
    out, middle, att, d_hidden, vec_up, *mlp_grad = mlp(
        clips, route, tab, tokens, att, att_first, att_last, cot, w_out, params, w_up, w_down, d_active
    )
    sum_a = Scatter(route, tab, (2 * w_up.shape[1],), *mlp_grad)
    d_low, d_att, d_high, d_middle, out_grad, vec_mid = mlp_back(
        clips, route, tab, d_hidden, w_up, middle, params, cot, w_out, att
    )
    mark = sum_a.row_step(0, vec_mid)
    d_low, d_high = clips.brought(d_low, d_high)
    d_qkv, vec_qkv, *qkv_grad = attend_back(
        clips, route, tab, segments, passed(route, mark), qkv, d_low, d_att, d_high, normed, out_grad
    )
    sum_b = Scatter(route, tab, (3 * width, width), *qkv_grad)
    mark = vec_qkv
    for t in range(1, route.row_stages):
        mark = sum_a.row_step(t, mark)
    d_in_low, d_in, d_in_high, vectors = first_back(
        clips, tab, passed(route, mark), low, tokens, high, params, w_qkv, d_qkv, vec_mid, vec_cot, vec_qkv, vec_up
    )
    d_in_last, d_in_first = clips.returned(d_in_low, d_in_high)
    sum_a.take_on(vectors)
    mark = sum_a.col_step(0, mark)
    mark = sum_b.row_step(0, mark)
    for t in range(1, route.row_stages):
        mark = sum_b.row_step(t, mark)
    grad_tokens, _ = finish(clips, mark, d_middle, d_in, d_in_first, d_in_last)
    for t in range(1, route.col_stages):
        mark = sum_a.col_step(t, mark)
    mark = sum_b.col_step(0, mark)
    sum_up, sum_down, vectors = sum_a.end(UNIT, mark)
    for t in range(1, route.col_stages):
        mark = sum_b.col_step(t, mark)
    for t in range(route.row_stages):
        vectors = hop_sum(vectors, sum_a.swap(vectors, "row", t + 1), mark)
    sum_qkv, sum_out, _ = sum_b.end(3 * width // seq_count)
    return (
        out,
        grad_tokens,
        vectors[0],
        vectors[1],
        sum_qkv,
        vectors[6],
        vectors[8],
        sum_out,
        vectors[2],
        vectors[3],
        vectors[4],
        sum_up,
        vectors[9 : 9 + up_bias.shape[0] // width].reshape(-1),
        sum_down.T,
        vectors[5],
    )


def solution(mesh):
    placed = (
        P("rows", "seq", None),
        P("rows", "seq"),
        P(),
        P(),
        P(),
        P(),
        P(),
        P(),
        P(),
        P(),
        P(),
        P(),
        P(),
        P(),
        P(),
        P("rows", "seq", None),
    )
    return jax.shard_map(
        on_device,
        mesh=mesh,
        in_specs=placed,
        out_specs=(
            P("rows", "seq", None),
            P("rows", "seq", None),
            P(),
            P(),
            P("rows", "seq"),
            P(),
            P(),
            P("rows", "seq"),
            P(),
            P(),
            P(),
            P("rows", "seq"),
            P(),
            P("seq", "rows"),
            P(),
        ),
        check_vma=False,
    )
```

```python
import functools

import jax
import jax.numpy as jnp
import numpy as np
from jax import lax
from jax.experimental import pallas as pl
from jax.experimental.pallas import tpu as pltpu
from jax.sharding import PartitionSpec as P

HEAD_DIM = 64
CLIP = 157
UNIT = 768


def bit_orders(count, offset):
    bits = max(count.bit_length() - 1, 0)
    free = list(range(offset, bits))
    return free, free[::-1]


class Route:
    def __init__(self, seq_count, rows_count, shards):
        self.seq_count, self.rows_count = seq_count, rows_count
        plain, turned = bit_orders(rows_count, 1)
        self.row_bits = [[0] + plain, [0] + turned]
        self.col_bits = list(bit_orders(seq_count, 0))
        self.row_stages = len(plain)
        self.col_stages = len(self.col_bits[0])
        self.places = {}
        self.table = np.array(
            [self.one_device(s, r, first) for s, first in enumerate(shards) for r in range(rows_count)],
            np.int32,
        )

    def halves(self, r):
        bit = self.row_bits[r & 1][1]
        ours = [b for b in range(self.rows_count) if not (b ^ r) & 1]
        return [b for b in ours if (b ^ r) >> bit & 1], [b for b in ours if not (b ^ r) >> bit & 1]

    def one_device(self, s, r, shard):
        core, places = r & 1, self.places
        row = [*shard, core]
        spots = sum(self.halves(r ^ 1), []) + sorted(sum(self.halves(r), []))
        places["block"] = len(row)
        row += spots
        own = sorted(sum(self.halves(r), []))
        sent, kept = self.halves(r)
        places["row", 0] = [len(row), len(row) + len(sent)]
        row += [own.index(b) for b in sent] + list(range(len(sent)))
        lists = [own, kept, kept]
        for t, bit in enumerate(self.row_bits[core][2:], 1):
            send = [b for b in kept if (b ^ r) >> bit & 1]
            kept = [b for b in kept if not (b ^ r) >> bit & 1]
            places["row", t] = []
            for origin in lists:
                places["row", t].append(len(row))
                row += [origin.index(b) for b in send]
            lists.append(kept)
        places["own"] = []
        for origin in lists[:-1]:
            places["own"].append(len(row))
            row.append(origin.index(r))
        kept, lists = list(range(self.seq_count)), [list(range(self.seq_count))]
        for t, bit in enumerate(self.col_bits[core]):
            send = [b for b in kept if (b ^ s) >> bit & 1]
            kept = [b for b in kept if not (b ^ s) >> bit & 1]
            places["col", t] = []
            for origin in lists:
                places["col", t].append(len(row))
                row += [origin.index(b) for b in send]
            lists.append(kept)
        places["end"] = []
        for origin in lists:
            places["end"].append(len(row))
            row.append(origin.index(s))
        return row

    def pairs(self, kind, t):
        out = []
        for s in range(self.seq_count):
            for r in range(self.rows_count):
                if kind == "row":
                    to = s * self.rows_count + (r ^ (1 << self.row_bits[r & 1][t]))
                else:
                    to = (s ^ (1 << self.col_bits[r & 1][t])) * self.rows_count + r
                out.append((s * self.rows_count + r, to))
        return out


def add_up(pieces):
    total = pieces[0].astype(jnp.float32)
    for piece in pieces[1:]:
        total = total + piece.astype(jnp.float32)
    return total


def in_vmem():
    return pl.BlockSpec(memory_space=pltpu.VMEM)


def in_smem():
    return pl.BlockSpec(memory_space=pltpu.SMEM)


def vmem_call(kernel, name, flags, args, shapes, scratch, flops, mega, far=(), marks=()):
    head, skip = len(flags) + len(args), len(marks)

    def without_marks(*refs):
        kernel(*refs[:head], *refs[head + skip :])

    return pl.pallas_call(
        without_marks,
        in_specs=[in_smem()] * len(flags) + [in_vmem()] * (len(args) + skip),
        out_specs=[in_vmem()] * len(shapes) + [pl.BlockSpec(memory_space=pltpu.HBM)] * len(far),
        out_shape=[jax.ShapeDtypeStruct(*s) for s in shapes] + [pltpu.HBM(*s) for s in far],
        scratch_shapes=scratch,
        compiler_params=pltpu.CompilerParams(vmem_limit_bytes=mega << 20),
        cost_estimate=pl.CostEstimate(flops=flops, bytes_accessed=1 << 10, transcendentals=0),
        name=name,
    )(*flags, *args, *marks)


MARK = ((8, 128), jnp.float32)


def in_strips(rows, step):
    if rows % 16:
        step(slice(0, rows))
        return

    def one(i, carry):
        step(pl.ds(pl.multiple_of(i * 16, 16), 16))
        return carry

    lax.fori_loop(0, rows // 16, one, 0)


RIDER_ROWS = 16


def read_rider(refs, rows, width):
    held, came = refs
    if came.dtype == jnp.float32:
        return held[...] + came[...]
    high, low = (came[rows:, k * width : (k + 1) * width].astype(jnp.float32) for k in range(2))
    return held[...] + (high + low)


def put_rider(rider, out_ref, rows):
    high = rider.astype(jnp.bfloat16)
    low = (rider - high.astype(jnp.float32)).astype(jnp.bfloat16)
    for k, half in enumerate((high, low)):
        out_ref[rows:, k * rider.shape[1] : (k + 1) * rider.shape[1]] = half


def by_shards(values, widths, count):
    if len(widths) < 2:
        return values
    pieces = []
    for s in range(count):
        at = 0
        for wide in widths:
            part = wide // count
            pieces.append(values[:, at + s * part : at + (s + 1) * part])
            at += wide
    return jnp.concatenate(pieces, 1)


def row_kernel(route, t, widths, sources, riders, tab_ref, *refs):
    source_refs, out_refs = refs[:sources], refs[sources + riders :]
    out_refs[-1][...] = jnp.zeros_like(out_refs[-1])

    def step(strip):
        for j in range(out_refs[0].shape[0]):
            pieces = [ref[tab_ref[base + j], strip] for base, ref in zip(route.places["row", t], source_refs)]
            total = add_up(pieces)
            if t == route.row_stages - 1:
                total = by_shards(total, widths, route.seq_count)
            out_refs[0][j, strip] = total.astype(jnp.bfloat16)

    in_strips(out_refs[0].shape[1], step)


def stay_kernel(route, widths, sources, riders, tab_ref, *refs):
    source_refs, out_refs = refs[:sources], refs[sources + riders :]
    out_refs[-1][...] = jnp.zeros_like(out_refs[-1])

    def step(strip):
        total = add_up([ref[tab_ref[base], strip] for base, ref in zip(route.places["own"], source_refs)])
        out_refs[0][strip] = by_shards(total, widths, route.seq_count)

    in_strips(out_refs[0].shape[0], step)


def col_pieces(route, key, j, chunk, tab_ref, refs, strip):
    pieces = []
    for u, ref in enumerate(refs):
        at = tab_ref[route.places[key][max(u - 1, 0)] + j] * chunk
        pieces.append(ref[strip, pl.ds(pl.multiple_of(at, 128), chunk)])
    return add_up(pieces)


def col_kernel(route, t, chunk, count, sources, riders, tab_ref, *refs):
    source_refs, rider_refs, out_refs = refs[:sources], refs[sources : sources + riders], refs[sources + riders :]
    rows = source_refs[0].shape[0]
    if riders:
        rider = read_rider(rider_refs, rows, out_refs[-1].shape[1])
        out_refs[-1][...] = rider
        out_refs[0][rows:] = jnp.zeros_like(out_refs[0][rows:])
        put_rider(rider, out_refs[0], rows)
    else:
        out_refs[-1][...] = jnp.zeros_like(out_refs[-1])

    def step(strip):
        for j in range(count):
            made = col_pieces(route, ("col", t), j, chunk, tab_ref, source_refs, strip)
            out_refs[0][strip, j * chunk : (j + 1) * chunk] = made.astype(jnp.bfloat16)

    in_strips(rows, step)


def end_kernel(route, chunk, cut, sources, riders, tab_ref, *refs):
    source_refs, rider_refs, out_refs = refs[:sources], refs[sources : sources + riders], refs[sources + riders :]
    if riders:
        out_refs[-1][...] = read_rider(rider_refs, source_refs[0].shape[0], out_refs[-1].shape[1])
    else:
        out_refs[-1][...] = jnp.zeros_like(out_refs[-1])

    def step(strip):
        total = col_pieces(route, "end", 0, chunk, tab_ref, source_refs, strip)
        out_refs[0][strip] = total[:, :cut]
        out_refs[1][strip] = total[:, cut:]

    in_strips(source_refs[0].shape[0], step)


def hop_kernel(held_ref, came_ref, total_ref):
    total_ref[...] = held_ref[...] + came_ref[...]


def hop_sum(held, came, mark):
    return vmem_call(hop_kernel, "hop_sum", (), (held, came), [(held.shape, held.dtype)], [], 10**6, 4, marks=(mark,))[0]


def passed(route, mark):
    return lax.ppermute(mark, ("seq", "rows"), route.pairs("row", 0))


class Scatter:
    def __init__(self, route, tab, widths, now, later, keep):
        self.route, self.tab, self.widths, self.riders = route, tab, widths, []
        self.first = [keep, self.swap(now, "row", 0)]
        self.rows = [keep, self.swap(later, "row", 0)]
        self.cols = []

    def swap(self, send, kind, t):
        return lax.ppermute(send, ("seq", "rows"), self.route.pairs(kind, t))

    def take_on(self, rider):
        self.riders = [rider, self.swap(rider, "row", 0)]

    def call(self, kernel, name, sources, shapes, marks, riders=()):
        last = (riders[0].shape, riders[0].dtype) if riders else MARK
        kernel = functools.partial(kernel, len(sources), len(riders))
        return vmem_call(kernel, name, (self.tab,), [*sources, *riders], [*shapes, last], [], 10**9, 8, marks=marks)

    def row_step(self, t, *marks):
        sources = self.first if t == 0 else self.rows
        _, rows, width = sources[0].shape
        shapes = [((self.route.rows_count >> (t + 2), rows, width), jnp.bfloat16)]
        kernel = functools.partial(row_kernel, self.route, t, self.widths)
        send, mark = self.call(kernel, "row_sum", sources, shapes, marks)
        got = self.swap(send, "row", t + 1)
        self.rows = self.rows + [got]
        if t == self.route.row_stages - 1:
            kernel = functools.partial(stay_kernel, self.route, self.widths)
            base, _ = self.call(kernel, "stay_sum", sources, [((rows, width), jnp.float32)], (mark,))
            self.cols = [base, got[0]]
        return mark

    def col_step(self, t, *marks):
        rows, width = self.cols[0].shape
        chunk, count = width // self.route.seq_count, self.route.seq_count >> (t + 1)
        kernel = functools.partial(col_kernel, self.route, t, chunk, count)
        more = RIDER_ROWS if self.riders else 0
        shapes = [((rows + more, count * chunk), jnp.bfloat16)]
        send, mark = self.call(kernel, "col_sum", self.cols, shapes, marks, self.riders)
        got = self.swap(send, "col", t)
        self.cols = self.cols + [got]
        if self.riders:
            self.riders = [mark, got]
        return mark

    def end(self, cut, *marks):
        rows, width = self.cols[0].shape
        chunk = width // self.route.seq_count
        shapes = [((rows, cut), jnp.float32), ((rows, chunk - cut), jnp.float32)]
        kernel = functools.partial(end_kernel, self.route, chunk, cut)
        return self.call(kernel, "end_sum", self.cols, shapes, marks, self.riders)


def dot(left, right):
    return lax.dot_general(left, right, (((1,), (0,)), ((), ())), preferred_element_type=jnp.float32)


def dot_t(left, right):
    return lax.dot_general(left, right, (((1,), (1,)), ((), ())), preferred_element_type=jnp.float32)


def t_dot(left, right):
    return lax.dot_general(left, right, (((0,), (0,)), ((), ())), preferred_element_type=jnp.float32)


def up_to(value, step):
    return -(-value // step) * step


class Clips:
    def __init__(self, slot_count, seq_count):
        self.slots = slot_count
        length = slot_count * seq_count
        sure = length // CLIP - 1
        spans = [(k * CLIP, CLIP, 0) for k in range(sure)] + [(sure * CLIP, length - sure * CLIP, 1)]
        held = [[] for _ in range(seq_count)]
        self.before, self.behind = [], []
        low = high = 0
        for at, count, tail in spans:
            shares = [
                min(at + count, (s + 1) * slot_count) - max(at, s * slot_count) for s in range(seq_count)
            ]
            owner = max(range(seq_count), key=lambda s: shares[s])
            held[owner].append((at - owner * slot_count, count, tail))
            for s, share in enumerate(shares):
                if share > 0 and s != owner:
                    assert abs(s - owner) == 1 and not tail
                    (self.before if s < owner else self.behind).append((s, owner))
                    low, high = max(low, share * (s < owner)), max(high, share * (s > owner))
        self.low, self.high = up_to(low, 16), up_to(high, 16)
        self.window = self.low + slot_count + self.high
        self.a_rows = up_to(CLIP, 16)
        self.b_rows = up_to(max(CLIP, length - sure * CLIP), 16)
        self.rows = self.a_rows + self.b_rows
        self.tail_at = sure * CLIP % slot_count
        self.shards = []
        for spots in held:
            first = [spot for spot in spots if not spot[2]]
            last = [spot for spot in spots if spot[2]]
            assert len(first) + len(last) < 3
            blocks = (first[:1] or [(0, 0, 0)]) + (first[1:] + last or [(0, 0, 0)])
            self.shards.append([v for at, count, _ in blocks for v in (at + self.low, count)] + [len(last)])

    def brought(self, lows, highs):
        highs = lax.ppermute(highs, "seq", self.behind)
        return lax.ppermute(lows, "seq", self.before), highs

    def returned(self, lows, highs):
        return (
            lax.ppermute(lows, "seq", [(owner, s) for s, owner in self.before]),
            lax.ppermute(highs, "seq", [(owner, s) for s, owner in self.behind]),
        )


TAIL_AT = 4


def chosen(tab_ref, clips, turned):
    a_at, a_len, b_at, b_len = (tab_ref[k] for k in range(4))
    if turned:
        shape, row_dim = (clips.window, clips.rows), 1
    else:
        shape, row_dim = (clips.rows, clips.window), 0
    row = lax.broadcasted_iota(jnp.int32, shape, row_dim)
    slot = lax.broadcasted_iota(jnp.int32, shape, 1 - row_dim)
    in_a = (row < a_len) & (slot == row + a_at)
    second = row - clips.a_rows
    in_b = (second >= 0) & (second < b_len) & (slot == second + b_at)
    return jnp.where(in_a | in_b, 1.0, 0.0).astype(jnp.bfloat16)


def block_masks(tab_ref, seg_ref, clips, row, key_dim):
    shape_a = (1, clips.a_rows) if key_dim == 1 else (clips.a_rows, 1)
    key_a = lax.broadcasted_iota(jnp.int32, shape_a, key_dim)
    mask_a = jnp.where(key_a < CLIP, 0.0, -1e30)
    shape_b = (clips.b_rows, clips.b_rows)
    key_b = lax.broadcasted_iota(jnp.int32, shape_b, key_dim)
    query_b = lax.broadcasted_iota(jnp.int32, shape_b, 1 - key_dim)
    six = (tab_ref[TAIL_AT] > 0) & (seg_ref[row, clips.tail_at] >= 0)
    split, b_len = jnp.where(six, CLIP, 0), jnp.maximum(tab_ref[3], 1)
    fits = (key_b < b_len) & ((key_b < split) == (query_b < split))
    mask_b = jnp.where(fits, 0.0, -1e30)
    return mask_a, mask_b


def window_of(low_ref, own_ref, high_ref, r):
    return jnp.concatenate([low_ref[r], own_ref[r], high_ref[r]], 0)


def put_window(clips, values, low_ref, own_ref, high_ref, r):
    low_ref[r] = values[: clips.low]
    own_ref[r] = values[clips.low : clips.low + clips.slots]
    high_ref[r] = values[clips.low + clips.slots :]


def norm_parts(values):
    center = values - jnp.mean(values, -1, keepdims=True)
    spread = jnp.mean(center * center, -1, keepdims=True)
    rate = lax.rsqrt(spread + 1e-06)
    return center * rate, rate


def norm_back(d_unit, unit, rate):
    return rate * (
        d_unit
        - jnp.mean(d_unit, -1, keepdims=True)
        - unit * jnp.mean(d_unit * unit, -1, keepdims=True)
    )


def split_heads(pair):
    low = lax.broadcasted_iota(jnp.int32, pair.shape, 1) < HEAD_DIM
    zero = jnp.zeros_like(pair)
    return jnp.concatenate([jnp.where(low, pair, zero), jnp.where(low, zero, pair)], 0)


def join_heads(both):
    half = both.shape[0] // 2
    low = lax.broadcasted_iota(jnp.int32, (half, both.shape[1]), 1) < HEAD_DIM
    return jnp.where(low, both[:half], both[half:])


def window_shapes(clips, row_count, width):
    return [((row_count, n, width), jnp.bfloat16) for n in (clips.low, clips.slots, clips.high)]


def hold_kernel(*refs):
    refs[-1][...] = jnp.zeros_like(refs[-1])


def hold(*args):
    return vmem_call(hold_kernel, "hold", (), args, [MARK], [], 10**6, 4)[0]


def edges_kernel(x_ref, low_ref, high_ref):
    low_ref[...] = x_ref[:, x_ref.shape[1] - low_ref.shape[1] :]
    high_ref[...] = x_ref[:, : high_ref.shape[1]]


def edges(clips, tokens):
    row_count, _, width = tokens.shape
    shapes = [((row_count, n, width), tokens.dtype) for n in (clips.low, clips.high)]
    return vmem_call(edges_kernel, "edges", (), (tokens,), shapes, [], 10**6, 4)


def cot_kernel(cot_ref, w_down_ref, total_ref, d_active_ref):
    cot = cot_ref[...].reshape(-1, cot_ref.shape[-1])
    total_ref[...] = jnp.sum(cot.astype(jnp.float32), 0, keepdims=True)
    steps, _, chunk = d_active_ref.shape

    def one(f, carry):
        rows = pl.ds(pl.multiple_of(f * chunk, chunk), chunk)
        d_active_ref[f] = dot_t(cot, w_down_ref[rows]).astype(jnp.bfloat16)
        return carry

    lax.fori_loop(0, steps, one, 0, unroll=4)


def cot_back(steps, mark, cot, w_down):
    count, width = cot.shape[0] * cot.shape[1], cot.shape[2]
    shapes = [((1, width), jnp.float32), ((steps, count, w_down.shape[0] // steps), jnp.bfloat16)]
    return vmem_call(cot_kernel, "cot_back", (), (cot, w_down), shapes, [], 3 * 10**9, 14, marks=(mark,))


def attend_kernel(
    clips, tab_ref, seg_ref, low_ref, x_ref, high_ref, par_ref, w_ref,
    own_low_ref, own_ref, own_high_ref, mark_ref, qkv_out_ref, normed_out_ref, qkv_ref, normed_ref, att_ref, sems,
):
    mark_ref[...] = jnp.zeros_like(mark_ref)
    row_count, _, width = x_ref.shape
    pick, turned = chosen(tab_ref, clips, False), chosen(tab_ref, clips, True)
    for r in range(row_count):
        unit, _ = norm_parts(dot(pick, window_of(low_ref, x_ref, high_ref, r)))
        normed_ref[r] = (unit * par_ref[0:1] + par_ref[1:2]).astype(jnp.bfloat16)
    copies = [pltpu.make_async_copy(normed_ref, normed_out_ref, sems.at[row_count])]
    copies[0].start()
    for r in range(row_count):
        for part in range(3):
            cols = slice(part * width, (part + 1) * width)
            made = dot(normed_ref[r], w_ref[:, cols])
            if part != 1:
                made = made + par_ref[2 + part // 2 : 3 + part // 2]
            if part == 0:
                made = made * HEAD_DIM ** (-0.5)
            qkv_ref[r, :, cols] = made.astype(jnp.bfloat16)
        copies.append(pltpu.make_async_copy(qkv_ref.at[r], qkv_out_ref.at[r], sems.at[r]))
        copies[-1].start()
        masks = block_masks(tab_ref, seg_ref, clips, r, 1)
        for base, count, mask in ((0, clips.a_rows, masks[0]), (clips.a_rows, clips.b_rows, masks[1])):
            here = slice(base, base + count)
            if mask.shape[0] > 1:
                mask = jnp.concatenate([mask, mask], 0)

            def scores_of(p):
                query, key = (qkv_ref[r, here, k * width + p * 128 : k * width + (p + 1) * 128] for k in range(2))
                return dot_t(split_heads(query), key)

            pairs = width // 128
            coming = scores_of(0)
            for p in range(pairs):
                scores, coming = coming + mask, scores_of(p + 1) if p + 1 < pairs else None
                peak = jnp.max(scores, -1, keepdims=True)
                weights = jnp.exp(scores - peak)
                total = jnp.sum(weights, -1, keepdims=True)
                value = qkv_ref[r, here, 2 * width + p * 128 : 2 * width + (p + 1) * 128]
                mixed = dot(weights.astype(jnp.bfloat16), value) / total
                att_ref[here, p * 128 : (p + 1) * 128] = join_heads(mixed).astype(jnp.bfloat16)
        back = dot(turned, att_ref[...]).astype(jnp.bfloat16)
        put_window(clips, back, own_low_ref, own_ref, own_high_ref, r)
    for copy in copies:
        copy.wait()


def attend(clips, tab, seg, mark, *args):
    row_count, _, width = args[1].shape
    shapes = window_shapes(clips, row_count, width) + [MARK]
    far = [
        ((row_count, clips.rows, 3 * width), jnp.bfloat16),
        ((row_count, clips.rows, width), jnp.bfloat16),
    ]
    scratch = [pltpu.VMEM(*s) for s in far] + [
        pltpu.VMEM((clips.rows, width), jnp.bfloat16),
        pltpu.SemaphoreType.DMA((row_count + 1,)),
    ]
    kernel = functools.partial(attend_kernel, clips)
    return vmem_call(kernel, "attend", (tab, seg), args, shapes, scratch, 8 * 10**9, 20, far, (mark,))


def gelu_parts(hidden):
    cdf = 0.5 + 0.5 * lax.erf(hidden * 0.7071067811865476)
    return hidden * cdf, cdf + hidden * (0.3989422804014327 * jnp.exp(-0.5 * hidden * hidden))


def grad_shapes(route, width, cols):
    rows, half = width // route.rows_count, route.rows_count // 2
    return [((n, rows, cols), jnp.bfloat16) for n in (half // 2, half - half // 2, half)]


def hand_out(tab_ref, route, held_ref, refs, cols):
    spots = [(ref, k) for ref in refs for k in range(ref.shape[0])]
    for at, (ref, k) in enumerate(spots):
        ref[k, :, cols] = held_ref[tab_ref[route.places["block"] + at]]


def mlp_kernel(
    clips, route, tab_ref, x_ref, att_ref, first_ref, last_ref, cot_ref, w_out_ref, par_ref,
    w_up_ref, w_down_ref, d_active_ref,
    out_ref, middle_ref, att_sum_ref, d_hidden_ref, up_vec_ref, now_ref, later_ref, keep_ref,
    normed_s, result_s, held_s,
):
    row_count, slots, width = x_ref.shape
    steps, count, chunk = d_active_ref.shape
    rows = width // route.rows_count
    for r in range(row_count):
        att_sum_ref[r] = att_ref[r]
        att_sum_ref[r, : clips.high] += first_ref[r]
        att_sum_ref[r, slots - clips.low :] += last_ref[r]
    made = dot(att_sum_ref[...].reshape(count, width), w_out_ref[...])
    middle = x_ref[...].reshape(count, width).astype(jnp.float32) + made + par_ref[4:5]
    middle_ref[...] = middle
    unit, _ = norm_parts(middle)
    normed_s[...] = (unit * par_ref[5:6] + par_ref[6:7]).astype(jnp.bfloat16)
    cot = cot_ref[...].reshape(count, width)
    result_s[...] = middle + par_ref[7:8]

    def one(f, carry):
        part = pl.ds(pl.multiple_of(f * chunk, 128), chunk)
        hidden = dot(normed_s[...], w_up_ref[:, part]) + par_ref[pl.ds(8 + f, 1)]
        active, slope = gelu_parts(hidden)
        active_b = active.astype(jnp.bfloat16)
        d_hidden = (d_active_ref[f].astype(jnp.float32) * slope).astype(jnp.bfloat16)
        d_hidden_ref[f] = d_hidden
        up_vec_ref[pl.ds(f, 1)] = jnp.sum(d_hidden.astype(jnp.float32), 0, keepdims=True)
        result_s[...] += dot(active_b, w_down_ref[part])
        for at, grad in ((0, t_dot(normed_s[...], d_hidden)), (chunk, t_dot(cot, active_b))):
            grad = grad.astype(jnp.bfloat16)
            for b in range(route.rows_count):
                held_s[b, :, at : at + chunk] = grad[b * rows : (b + 1) * rows]
        cols = pl.ds(pl.multiple_of(2 * f * chunk, 128), 2 * chunk)
        hand_out(tab_ref, route, held_s, (now_ref, later_ref, keep_ref), cols)
        return carry

    lax.fori_loop(0, steps, one, 0, unroll=2)
    out_ref[...] = result_s[...].reshape(out_ref.shape).astype(jnp.bfloat16)


def mlp(clips, route, tab, *args):
    row_count, slots, width = args[0].shape
    steps, count, chunk = args[-1].shape
    bf16, f32 = jnp.bfloat16, jnp.float32
    shapes = [
        ((row_count, slots, width), bf16),
        ((count, width), f32),
        ((row_count, slots, width), bf16),
        ((steps, count, chunk), bf16),
        ((steps, chunk), f32),
        *grad_shapes(route, width, 2 * steps * chunk),
    ]
    scratch = [
        pltpu.VMEM((count, width), bf16),
        pltpu.VMEM((count, width), f32),
        pltpu.VMEM((route.rows_count, width // route.rows_count, 2 * chunk), bf16),
    ]
    kernel = functools.partial(mlp_kernel, clips, route)
    return vmem_call(kernel, "mlp", (tab,), args, shapes, scratch, 20 * 10**9, 24)


def mlp_back_kernel(
    clips, route, tab_ref, d_hidden_ref, w_up_ref, middle_ref, par_ref, cot_ref, w_out_ref, att_ref,
    d_low_ref, d_att_ref, d_high_ref, d_middle_ref, out_grad_ref, vec_ref,
):
    row_count, slots, width = cot_ref.shape
    steps, count, chunk = d_hidden_ref.shape
    d_normed = dot_t(d_hidden_ref[0], w_up_ref[:, :chunk])
    for f in range(1, steps):
        d_normed += dot_t(d_hidden_ref[f], w_up_ref[:, f * chunk : (f + 1) * chunk])
    unit, rate = norm_parts(middle_ref[...])
    vec_ref[1:2] = jnp.sum(d_normed * unit, 0, keepdims=True)
    vec_ref[2:3] = jnp.sum(d_normed, 0, keepdims=True)
    cot = cot_ref[...].reshape(count, width).astype(jnp.float32)
    total = cot + norm_back(d_normed * par_ref[5:6], unit, rate)
    d_middle_ref[...] = total.reshape(d_middle_ref.shape)
    branch = total.astype(jnp.bfloat16)
    vec_ref[0:1] = jnp.sum(branch.astype(jnp.float32), 0, keepdims=True)
    made = dot_t(branch, w_out_ref[...]).astype(jnp.bfloat16).reshape(row_count, slots, width)
    d_att_ref[...] = made
    d_low_ref[...] = made[:, slots - clips.low :]
    d_high_ref[...] = made[:, : clips.high]
    grad = t_dot(att_ref[...].reshape(count, width), branch).astype(jnp.bfloat16)
    rows = width // route.rows_count
    for b in range(route.rows_count):
        out_grad_ref[b] = grad[b * rows : (b + 1) * rows]


def mlp_back(clips, route, tab, *args):
    row_count, _, width = args[4].shape
    shapes = window_shapes(clips, row_count, width) + [
        (args[4].shape, jnp.float32),
        ((route.rows_count, width // route.rows_count, width), jnp.bfloat16),
        ((3, width), jnp.float32),
    ]
    kernel = functools.partial(mlp_back_kernel, clips, route)
    return vmem_call(kernel, "mlp_back", (tab,), args, shapes, [], 5 * 10**9, 16)


def attend_back_kernel(
    clips, route, tab_ref, seg_ref, qkv_ref, d_low_ref, d_att_ref, d_high_ref, normed_ref, out_grad_ref,
    d_qkv_ref, vec_ref, now_ref, later_ref, keep_ref, d_mixed_s, held_s,
):
    row_count, rows, width = normed_ref.shape
    scale = HEAD_DIM ** (-0.5)
    pick = chosen(tab_ref, clips, False)

    def one_row(r, total):
        d_mixed_s[...] = dot(pick, window_of(d_low_ref, d_att_ref, d_high_ref, r)).astype(jnp.bfloat16)
        masks = block_masks(tab_ref, seg_ref, clips, r, 0)
        for base, count, mask in ((0, clips.a_rows, masks[0]), (clips.a_rows, clips.b_rows, masks[1])):
            here = slice(base, base + count)
            if mask.shape[1] > 1:
                mask = jnp.concatenate([mask, mask], 1)

            def products(p):
                cols = [slice(k * width + p * 128, k * width + (p + 1) * 128) for k in range(3)]
                query, key, value = (qkv_ref[r, here, c] for c in cols)
                queries = split_heads(query)
                d_mixed = split_heads(d_mixed_s[here, cols[0]])
                return cols, key, queries, d_mixed, dot_t(key, queries), dot_t(value, d_mixed)

            pairs = width // 128
            coming = products(0)
            for p in range(pairs):
                (cols, key, queries, d_mixed, scores, d_prob), coming = (
                    coming,
                    products(p + 1) if p + 1 < pairs else None,
                )
                scores = scores + mask
                peak = jnp.max(scores, 0, keepdims=True)
                weights = jnp.exp(scores - peak)
                prob = weights * (1.0 / jnp.sum(weights, 0, keepdims=True))
                d_value = dot(prob.astype(jnp.bfloat16), d_mixed)
                centre = jnp.sum(d_prob * prob, 0, keepdims=True)
                d_scores = (prob * (d_prob - centre)).astype(jnp.bfloat16)
                d_key = dot(d_scores, queries)
                d_query = join_heads(t_dot(d_scores, key)) * scale
                for c, made in zip(cols, (d_query, d_key, d_value)):
                    d_qkv_ref[r, here, c] = made.astype(jnp.bfloat16)
        return total + jnp.sum(d_qkv_ref[r].astype(jnp.float32), 0, keepdims=True)

    total = lax.fori_loop(0, row_count, one_row, jnp.zeros((1, 3 * width), jnp.float32))
    for k in range(3):
        vec_ref[k : k + 1] = total[:, k * width : (k + 1) * width]
    flat = normed_ref[...].reshape(row_count * rows, width)
    height = width // route.rows_count
    for k in range(4):
        cols = slice(k * width, (k + 1) * width)
        if k < 3:
            made = t_dot(flat, d_qkv_ref[:, :, cols].reshape(row_count * rows, width)).astype(jnp.bfloat16)
            for b in range(route.rows_count):
                held_s[b] = made[b * height : (b + 1) * height]
        hand_out(tab_ref, route, held_s if k < 3 else out_grad_ref, (now_ref, later_ref, keep_ref), cols)


def attend_back(clips, route, tab, seg, mark, *args):
    row_count, rows, width = args[4].shape
    shapes = [
        ((row_count, rows, 3 * width), jnp.bfloat16),
        ((3, width), jnp.float32),
        *grad_shapes(route, width, 4 * width),
    ]
    scratch = [
        pltpu.VMEM((rows, width), jnp.bfloat16),
        pltpu.VMEM((route.rows_count, width // route.rows_count, width), jnp.bfloat16),
    ]
    kernel = functools.partial(attend_back_kernel, clips, route)
    return vmem_call(kernel, "attend_back", (tab, seg), args, shapes, scratch, 10**6, 18, marks=(mark,))


def first_back_kernel(clips, tab_ref, low_ref, x_ref, high_ref, par_ref, w_ref, *refs):
    row_count = x_ref.shape[0]
    d_qkv_ref, *vec_refs = refs[:-4]
    own_low_ref, own_ref, own_high_ref, vec_ref = refs[-4:]
    pick, turned = chosen(tab_ref, clips, False), chosen(tab_ref, clips, True)
    sums = []
    for r in range(row_count):
        unit, rate = norm_parts(dot(pick, window_of(low_ref, x_ref, high_ref, r)))
        d_normed = dot_t(d_qkv_ref[r], w_ref[...])
        sums.append([jnp.sum(p, 0, keepdims=True) for p in (d_normed * unit, d_normed)])
        d_in = norm_back(d_normed * par_ref[0:1], unit, rate).astype(jnp.bfloat16)
        back = dot(turned, d_in).astype(jnp.bfloat16)
        put_window(clips, back, own_low_ref, own_ref, own_high_ref, r)
    for k in range(2):
        vec_ref[k : k + 1] = sum(s[k] for s in sums[1:]) + sums[0][k]
    vec_ref[8:] = jnp.zeros_like(vec_ref[8:])
    at = 2
    for ref in vec_refs:
        vec_ref[at : at + ref.shape[0]] = ref[...]
        at += ref.shape[0]


def first_back(clips, tab, mark, *args):
    row_count, _, width = args[1].shape
    assert 2 + sum(a.shape[0] for a in args[6:]) <= RIDER_ROWS
    shapes = window_shapes(clips, row_count, width) + [((RIDER_ROWS, width), jnp.float32)]
    kernel = functools.partial(first_back_kernel, clips)
    return vmem_call(kernel, "first_back", (tab,), args, shapes, [], 10**6, 16, marks=(mark,))


def finish_kernel(clips, d_middle_ref, own_ref, first_ref, last_ref, out_ref, mark_ref):
    for r in range(own_ref.shape[0]):
        total = d_middle_ref[r] + own_ref[r].astype(jnp.float32)
        tail = clips.slots - clips.low
        first = total[: clips.high] + first_ref[r].astype(jnp.float32)
        last = total[tail:] + last_ref[r].astype(jnp.float32)
        out_ref[r] = jnp.concatenate([first, total[clips.high : tail], last], 0).astype(jnp.bfloat16)
    mark_ref[...] = jnp.zeros_like(mark_ref)


def finish(clips, mark, *args):
    shapes = [(args[1].shape, jnp.bfloat16), MARK]
    kernel = functools.partial(finish_kernel, clips)
    return vmem_call(kernel, "finish", (), args, shapes, [], 10**9, 8, marks=(mark,))


def on_device(
    tokens,
    segments,
    ln1_gain,
    ln1_bias,
    w_qkv,
    q_bias,
    v_bias,
    w_out,
    out_bias,
    ln2_gain,
    ln2_bias,
    w_up,
    up_bias,
    w_down,
    down_bias,
    cotangent,
):
    row_count, slot_count, width = tokens.shape
    seq_count, rows_count = lax.axis_size("seq"), lax.axis_size("rows")
    clips = Clips(slot_count, seq_count)
    route = Route(seq_count, rows_count, clips.shards)
    low, high = clips.brought(*edges(clips, tokens))
    tab = jnp.asarray(route.table)[lax.axis_index("seq") * rows_count + lax.axis_index("rows")]
    total, at = 8 * width + up_bias.shape[0], 0
    params = jnp.zeros((total,), jnp.float32)
    for vector in (ln1_gain, ln1_bias, q_bias, v_bias, out_bias, ln2_gain, ln2_bias, down_bias, up_bias):
        params = params + lax.pad(vector, 0.0, [(at, total - at - vector.shape[0], 0)])
        at += vector.shape[0]
    params = params.reshape(-1, width)
    cot = cotangent
    att_low, att, att_high, mark, qkv, normed = attend(
        clips, tab, segments, hold(w_qkv, params), low, tokens, high, params, w_qkv
    )
    att_last, att_first = clips.returned(att_low, att_high)
    vec_cot, d_active = cot_back(seq_count, mark, cot, w_down)
    out, middle, att, d_hidden, vec_up, *mlp_grad = mlp(
        clips, route, tab, tokens, att, att_first, att_last, cot, w_out, params, w_up, w_down, d_active
    )
    sum_a = Scatter(route, tab, (2 * w_up.shape[1],), *mlp_grad)
    d_low, d_att, d_high, d_middle, out_grad, vec_mid = mlp_back(
        clips, route, tab, d_hidden, w_up, middle, params, cot, w_out, att
    )
    mark = sum_a.row_step(0, vec_mid)
    d_low, d_high = clips.brought(d_low, d_high)
    d_qkv, vec_qkv, *qkv_grad = attend_back(
        clips, route, tab, segments, passed(route, mark), qkv, d_low, d_att, d_high, normed, out_grad
    )
    sum_b = Scatter(route, tab, (3 * width, width), *qkv_grad)
    mark = vec_qkv
    for t in range(1, route.row_stages):
        mark = sum_a.row_step(t, mark)
    d_in_low, d_in, d_in_high, vectors = first_back(
        clips, tab, passed(route, mark), low, tokens, high, params, w_qkv, d_qkv, vec_mid, vec_cot, vec_qkv, vec_up
    )
    d_in_last, d_in_first = clips.returned(d_in_low, d_in_high)
    sum_a.take_on(vectors)
    mark = sum_a.col_step(0, mark)
    mark = sum_b.row_step(0, mark)
    for t in range(1, route.row_stages):
        mark = sum_b.row_step(t, mark)
    grad_tokens, _ = finish(clips, mark, d_middle, d_in, d_in_first, d_in_last)
    for t in range(1, route.col_stages):
        mark = sum_a.col_step(t, mark)
    mark = sum_b.col_step(0, mark)
    sum_up, sum_down, vectors = sum_a.end(UNIT, mark)
    for t in range(1, route.col_stages):
        mark = sum_b.col_step(t, mark)
    for t in range(route.row_stages):
        vectors = hop_sum(vectors, sum_a.swap(vectors, "row", t + 1), mark)
    sum_qkv, sum_out, _ = sum_b.end(3 * width // seq_count)
    return (
        out,
        grad_tokens,
        vectors[0],
        vectors[1],
        sum_qkv,
        vectors[6],
        vectors[8],
        sum_out,
        vectors[2],
        vectors[3],
        vectors[4],
        sum_up,
        vectors[9 : 9 + up_bias.shape[0] // width].reshape(-1),
        sum_down.T,
        vectors[5],
    )


def solution(mesh):
    placed = (
        P("rows", "seq", None),
        P("rows", "seq"),
        P(),
        P(),
        P(),
        P(),
        P(),
        P(),
        P(),
        P(),
        P(),
        P(),
        P(),
        P(),
        P(),
        P("rows", "seq", None),
    )
    return jax.shard_map(
        on_device,
        mesh=mesh,
        in_specs=placed,
        out_specs=(
            P("rows", "seq", None),
            P("rows", "seq", None),
            P(),
            P(),
            P("rows", "seq"),
            P(),
            P(),
            P("rows", "seq"),
            P(),
            P(),
            P(),
            P("rows", "seq"),
            P(),
            P("seq", "rows"),
            P(),
        ),
        check_vma=False,
    )
```
